256 devices in a mesh: blk: 128 (over x_lo, z, y, core), rep: 2 (over x_hi).
Axes of the slice: x: 4 (x_hi: 2, x_lo: 2; x = x_hi * 2 + x_lo), y: 4, z: 8, core: 2. Of those that a mesh axis runs over, the one named last changes fastest.
Arguments:
- embeddings: bfloat16 [65536, 400], P('blk'), may hold values from -1.8 to 1.8
- relations: bfloat16 [2560, 400], replicated, may hold values from -3 to 3
- heads: int32 [3, 131072], P(None, ('blk', 'rep')), may hold values from 0 to 511
- tails: int32 [3, 131072], P(None, ('blk', 'rep')), may hold values from 0 to 511
- rels: int32 [3, 131072], P(None, ('blk', 'rep')), may hold values from 0 to 2559
- negatives: int32 [3, 512, 256], P(None, ('blk', 'rep')), may hold values from 0 to 511
- live: int32 [3, 256], P(None, ('blk', 'rep')), may hold values from 1 to 2
Outputs:
- gradient: float32 [65536, 400], P('blk')
- mean_loss: float32 [], replicated
The draws below stay inside these ranges and needn't reach their ends.
All inputs are finite; a program needn't handle non-finite values.
Results may differ from the reference program's by a relative error of at most 0.0027.
Values may be sent and summed in bfloat16 or wider, within the bound.
No kernel may reach another device: no remote copies, remote signals or barrier semaphores. Data moves between devices by JAX's collectives and lax.ppermute only.
A program may use at most 64 MiB of HBM per device.

```python
import jax
import jax.numpy as jnp
from jax import lax

D = 400
REL = 2560
ENT_DEV = 512
GROUP = 256
NEG = 256
GROUPS = 2
STEPS = 3
ENT = 65536
ROWS = 131072
GROUP_ALL = 512
LANES = 256
N_BLK = 128
N_REP = 2


def draw_embeddings(key, part):
    key = jax.random.fold_in(key, 11)
    noise = jax.random.normal(jax.random.fold_in(key, 1), (ENT, D), jnp.float32)
    values = 0.3 * noise
    return jnp.clip(values, -1.8, 1.8).astype(jnp.bfloat16)


def draw_relations(key, part):
    key = jax.random.fold_in(key, 12)
    noise = jax.random.normal(jax.random.fold_in(key, 1), (REL, D), jnp.float32)
    values = 0.5 * noise
    return jnp.clip(values, -3.0, 3.0).astype(jnp.bfloat16)


def touch_ends(array, key, smallest, high):
    longest = array.shape.index(max(array.shape))
    spots = []
    for shift in (0, 1):
        where = [jax.random.randint(jax.random.fold_in(key, axis), (), 0, length) for axis, length in enumerate(array.shape)]
        where[longest] = (where[longest] + shift) % array.shape[longest]
        spots.append(tuple(where))
    return array.at[spots[0]].set(smallest).at[spots[1]].set(high)


def setup_inputs(seed: int = 0) -> dict:
    keys = jax.random.split(jax.random.key(seed), 8)
    embeddings = draw_embeddings(jax.random.fold_in(keys[7], 71), 0)
    relations = draw_relations(jax.random.fold_in(keys[7], 71), 0)
    heads = touch_ends(jax.random.randint(keys[2], (STEPS, ROWS), 0, ENT_DEV), jax.random.fold_in(keys[2], 1), 0, ENT_DEV - 1).astype(jnp.int32)
    tails = touch_ends(jax.random.randint(keys[3], (STEPS, ROWS), 0, ENT_DEV), jax.random.fold_in(keys[3], 1), 0, ENT_DEV - 1).astype(jnp.int32)
    rels = touch_ends(jax.random.randint(keys[4], (STEPS, ROWS), 0, REL), jax.random.fold_in(keys[4], 1), 0, REL - 1).astype(jnp.int32)
    negatives = touch_ends(jax.random.randint(keys[5], (STEPS, GROUP_ALL, NEG), 0, ENT_DEV), jax.random.fold_in(keys[5], 1), 0, ENT_DEV - 1).astype(jnp.int32)
    live = touch_ends(jax.random.randint(keys[6], (STEPS, LANES), 1, GROUPS + 1), jax.random.fold_in(keys[6], 1), 1, GROUPS).astype(jnp.int32)
    return {"embeddings": embeddings, "relations": relations, "heads": heads, "tails": tails, "rels": rels, "negatives": negatives, "live": live}


def complex_query(head_rows, rel_rows):
    hf = head_rows.astype(jnp.float32)
    rf = rel_rows.astype(jnp.float32)
    half = hf.shape[1] // 2
    real_part = hf[:, :half] * rf[:, :half] - hf[:, half:] * rf[:, half:]
    imag_part = hf[:, :half] * rf[:, half:] + hf[:, half:] * rf[:, :half]
    return jnp.concatenate([real_part, imag_part], axis=1).astype(jnp.bfloat16)

def head_grad(d_query, rel_rows):
    rf = rel_rows.astype(jnp.float32)
    half = rf.shape[1] // 2
    real_part = d_query[:, :half] * rf[:, :half] + d_query[:, half:] * rf[:, half:]
    imag_part = -d_query[:, :half] * rf[:, half:] + d_query[:, half:] * rf[:, :half]
    return jnp.concatenate([real_part, imag_part], axis=1)

def group_terms(query, tail_rows, neg_rows, weight):
    positive = lax.optimization_barrier(jnp.sum(query.astype(jnp.float32) * tail_rows.astype(jnp.float32), axis=1))
    scores = jnp.dot(query, neg_rows.T, preferred_element_type=jnp.float32)
    top = jnp.maximum(positive, lax.optimization_barrier(jnp.max(scores, axis=1)))
    pos_exp = jnp.exp(positive - top)
    neg_exp = jnp.exp(scores - top[:, None])
    total = pos_exp + lax.optimization_barrier(jnp.sum(neg_exp, axis=1))
    edge_loss = jnp.log(total) + top - positive
    first_prob = pos_exp / total
    probs_low = (neg_exp / total[:, None]).astype(jnp.bfloat16)
    scale = weight / query.shape[0]
    coeff = (first_prob - 1.0)[:, None]
    d_query = scale * (coeff * tail_rows.astype(jnp.float32) + jnp.dot(probs_low, neg_rows, preferred_element_type=jnp.float32))
    d_tail = scale * coeff * query.astype(jnp.float32)
    d_negative = scale * jnp.dot(probs_low.T, query, preferred_element_type=jnp.float32)
    return (weight * jnp.sum(edge_loss), d_query, d_tail, d_negative)

def bucket_step(head_part, tail_part, relations, heads, tails, rels, negatives, live_count):
    groups = negatives.shape[0]
    group_rows = heads.shape[0] // groups
    width = head_part.shape[1]
    head_rows = head_part[heads]
    rel_rows = relations[rels]
    tail_rows = tail_part[tails]
    query = complex_query(head_rows, rel_rows)
    neg_rows = tail_part[negatives]
    weight = (jnp.arange(groups, dtype=jnp.int32) < live_count).astype(jnp.float32)
    loss_parts, d_query, d_tail, d_negative = jax.vmap(group_terms)(query.reshape(groups, group_rows, width), tail_rows.reshape(groups, group_rows, width), neg_rows, weight)
    d_head = head_grad(d_query.reshape(-1, width), rel_rows)
    head_acc = jnp.zeros(head_part.shape, jnp.float32).at[heads].add(d_head)
    tail_acc = jnp.zeros(tail_part.shape, jnp.float32).at[tails].add(d_tail.reshape(-1, width))
    tail_acc = tail_acc.at[negatives.reshape(-1)].add(d_negative.reshape(-1, width))
    edge_count = jnp.sum(weight) * group_rows
    return (jnp.sum(loss_parts), edge_count, head_acc, tail_acc)

def reference(embeddings, relations, heads, tails, rels, negatives, live):
    rows = GROUPS * GROUP
    width = embeddings.shape[1]
    gradient = jnp.zeros(embeddings.shape, jnp.float32)
    loss_sum = jnp.zeros((), jnp.float32)
    edge_count = jnp.zeros((), jnp.float32)
    for step in range(STEPS):

        def one_lane(carry, lane):
            grads, total, counted = carry
            owner = lane // N_REP
            source = (owner - step) % N_BLK
            head_start = (owner * ENT_DEV).astype(jnp.int32)
            tail_start = (source * ENT_DEV).astype(jnp.int32)
            head_part = lax.dynamic_slice_in_dim(embeddings, head_start, ENT_DEV, 0)
            tail_part = lax.dynamic_slice_in_dim(embeddings, tail_start, ENT_DEV, 0)
            lane_heads = lax.dynamic_slice_in_dim(heads[step], (lane * rows).astype(jnp.int32), rows, 0)
            lane_tails = lax.dynamic_slice_in_dim(tails[step], (lane * rows).astype(jnp.int32), rows, 0)
            lane_rels = lax.dynamic_slice_in_dim(rels[step], (lane * rows).astype(jnp.int32), rows, 0)
            lane_negs = lax.dynamic_slice_in_dim(negatives[step], (lane * GROUPS).astype(jnp.int32), GROUPS, 0)
            part_loss, part_count, head_acc, tail_acc = bucket_step(head_part, tail_part, relations, lane_heads, lane_tails, lane_rels, lane_negs, live[step, lane])
            block = lax.dynamic_slice_in_dim(grads, head_start, ENT_DEV, 0) + head_acc
            grads = lax.dynamic_update_slice_in_dim(grads, block, head_start, 0)
            block = lax.dynamic_slice_in_dim(grads, tail_start, ENT_DEV, 0) + tail_acc
            grads = lax.dynamic_update_slice_in_dim(grads, block, tail_start, 0)
            return ((grads, total + part_loss, counted + part_count), None)
        (gradient, loss_sum, edge_count), _ = lax.scan(one_lane, (gradient, loss_sum, edge_count), jnp.arange(N_BLK * N_REP, dtype=jnp.int32))
    return (gradient, loss_sum / edge_count)
```

```python
import jax
import jax.numpy as jnp
from jax import lax
from jax.experimental import pallas as pl
from jax.experimental.pallas import tpu as pltpu
from jax.sharding import PartitionSpec as P

STEPS = 3
F32 = jnp.float32
BF16 = jnp.bfloat16
NEVER = -1e30
TN = (((0,), (0,)), ((), ()))
NN = (((1,), (0,)), ((), ()))
NT = (((1,), (1,)), ((), ()))


def dot(a, b, dims):
    return lax.dot_general(a, b, dims, preferred_element_type=F32)


def one_hot(row, size):
    hit = lax.broadcasted_iota(jnp.int32, (size, row.shape[1]), 0) == row
    return jnp.where(hit, 1.0, 0.0).astype(BF16)


def gather_relations(rel_t, row, hot_ref):
    block = 256
    low = one_hot(row & (block - 1), block)
    high = row >> 8
    for j in range(rel_t.shape[1] // block):
        here = jnp.where(high == j, 1.0, 0.0).astype(BF16)
        hot_ref[j * block:(j + 1) * block, :] = low * here
    return dot(rel_t[...], hot_ref[...], NN)


def make_query(h_ref, r_ref, q_ref):
    half = h_ref.shape[0] // 2
    step = 40
    for c in range(0, half, step):
        re, im = slice(c, c + step), slice(half + c, half + c + step)
        h_re, h_im, r_re, r_im = h_ref[re, :], h_ref[im, :], r_ref[re, :], r_ref[im, :]
        q_ref[re, :] = h_re * r_re - h_im * r_im
        q_ref[im, :] = h_re * r_im + h_im * r_re


def head_grad(d_ref, r_ref, scale, out_ref):
    half = d_ref.shape[0] // 2
    step = 40
    for c in range(0, half, step):
        re, im = slice(c, c + step), slice(half + c, half + c + step)
        d_re, d_im, r_re, r_im = d_ref[re, :] * scale, d_ref[im, :] * scale, r_ref[re, :], r_ref[im, :]
        out_ref[re, :] = d_re * r_re + d_im * r_im
        out_ref[im, :] = d_im * r_re - d_re * r_im


def log_counts(neg_row, entities):
    groups = []
    half = neg_row.shape[1] // 2
    for g in range(2):
        hot = one_hot(neg_row[:, g * half:(g + 1) * half], entities)
        count = dot(hot, jnp.ones((half, 128), BF16), NN)
        log = jnp.where(count > 0.5, jnp.log(jnp.maximum(count, 1.0)), NEVER)
        groups += [log, log]
    return groups


def softmax_terms(s_ref, logs, tail_row, q_ref):
    entities, edges = s_ref.shape
    step = 32
    iota = lax.broadcasted_iota(jnp.int32, (step, edges), 0)
    top = jnp.full((8, edges), NEVER, F32)
    pos = jnp.zeros((8, edges), F32)
    for c in range(0, entities, step):
        s = s_ref[c:c + step, :]
        hit = jnp.where(iota == tail_row - c, s, 0.0)
        log = jnp.concatenate([g[c:c + step, :] for g in logs], axis=1)
        s = s + log
        s_ref[c:c + step, :] = s
        for k in range(0, step, 8):
            pos = pos + hit[k:k + 8, :]
            top = jnp.maximum(top, s[k:k + 8, :])
    positive = jnp.sum(pos, axis=0, keepdims=True)
    top = jnp.max(top, axis=0, keepdims=True)
    total = jnp.zeros((8, edges), F32)
    for c in range(0, entities, step):
        e = jnp.exp(s_ref[c:c + step, :] - top)
        s_ref[c:c + step, :] = e
        for k in range(0, step, 8):
            total = total + e[k:k + 8, :]
    total = jnp.sum(total, axis=0, keepdims=True)
    share = 1.0 / total
    for c in range(0, entities, step):
        p = s_ref[c:c + step, :] * share
        q_ref[c:c + step, :] = jnp.where(iota == tail_row - c, p - 1.0, p).astype(BF16)
    gap = jnp.log(total) + top - positive
    low = jnp.exp(-jnp.abs(gap))
    loss = jnp.maximum(gap, 0.0) + jnp.log(1.0 + low)
    miss = jnp.where(gap >= 0.0, 1.0, low) / (1.0 + low)
    return loss, miss


def live_row(lists, row, edges):
    group = lax.broadcasted_iota(jnp.int32, (1, edges), 1) // (edges // 2)
    return jnp.where(group < lists[row:row + 1, :], 1.0, 0.0)


HEADS, TAILS, RELS, NEGS, LIVE = 0, 3, 6, 9, 12


def row_of(lists, kind, step):
    return lists[kind + step:kind + step + 1, :]


def split(x):
    high = x.astype(BF16)
    return high, (x - high.astype(F32)).astype(BF16)


def prepare_kernel(emb, rel, lists, grad, sums, q1, q2, r1, r2, hot, hf, rf, qf, sf, qq):
    edges = lists.shape[1]
    entities = emb.shape[1]
    for step, q_out, r_out in ((1, q1, r1), (2, q2, r2), (0, None, None)):
        rf[...] = gather_relations(rel, row_of(lists, RELS, step), hot)
        head_hot = one_hot(row_of(lists, HEADS, step), entities)
        hf[...] = dot(emb[...], head_hot, NN)
        make_query(hf, rf, qf)
        if step:
            r_out[...] = rf[...].astype(BF16)
            q_out[...] = qf[...].astype(BF16)
    q = qf[...].astype(BF16)
    sf[...] = dot(emb[...], q, TN)
    logs = log_counts(row_of(lists, NEGS, 0), entities)
    loss, miss = softmax_terms(sf, logs, row_of(lists, TAILS, 0), qq)
    live = live_row(lists, LIVE, edges)
    scale = miss * live * (1.0 / 256.0)
    qs = q.astype(F32) * scale
    high, low = split(qs)
    g = dot(high, qq[...], NT) + dot(low, qq[...], NT)
    hf[...] = dot(emb[...], qq[...], NN)
    head_grad(hf, rf, scale, qf)
    high, low = split(qf[...])
    grad[...] = g + dot(high, head_hot, NT) + dot(low, head_hot, NT)
    sums[0:1, :] = loss * live
    sums[1:2, :] = live


def far_relations_kernel(rel, lists1, lists2, r1, r2, hot):
    for step, lists, out in ((1, lists1, r1), (2, lists2, r2)):
        out[...] = gather_relations(rel, row_of(lists, RELS, step), hot).astype(BF16)


def rest_kernel(emb, prev1, prev2, next1, next2, q1, q2, r1, r2, far_r1, far_r2, lists, lists1, lists2, part, sums,
                grad, rows, hf, rf, qf, sf, qq, acc):
    edges = lists.shape[1]
    entities = emb.shape[1]
    acc[...] = part[...]
    loss_row = sums[0:1, :]
    live_sum = sums[1:2, :]
    for step, tail, q_in, r_in in ((1, prev1, q1, r1), (2, prev2, q2, r2)):
        sf[...] = dot(tail[...], q_in[...], TN)
        logs = log_counts(row_of(lists, NEGS, step), entities)
        loss, miss = softmax_terms(sf, logs, row_of(lists, TAILS, step), qq)
        live = live_row(lists, LIVE + step, edges)
        loss_row = loss_row + loss * live
        live_sum = live_sum + live
        hf[...] = dot(tail[...], qq[...], NN)
        rf[...] = r_in[...].astype(F32)
        head_grad(hf, rf, miss * live * (1.0 / 256.0), qf)
        high, low = split(qf[...])
        head_hot = one_hot(row_of(lists, HEADS, step), entities)
        acc[...] += dot(high, head_hot, NT) + dot(low, head_hot, NT)
    lane = lax.broadcasted_iota(jnp.int32, (1, 128), 1)
    loss_all = jnp.sum(loss_row, axis=1, keepdims=True)
    live_all = jnp.sum(live_sum, axis=1, keepdims=True)
    row = jnp.where(lane == 0, loss_all, jnp.where(lane == 1, live_all, 0.0))
    rows[...] = jnp.broadcast_to(row, rows.shape)
    for step, head, r_in, far in ((1, next1, far_r1, lists1), (2, next2, far_r2, lists2)):
        hf[...] = dot(head[...], one_hot(row_of(far, HEADS, step), entities), NN)
        rf[...] = r_in[...].astype(F32)
        make_query(hf, rf, qf)
        q = qf[...].astype(BF16)
        sf[...] = dot(emb[...], q, TN)
        logs = log_counts(row_of(far, NEGS, step), entities)
        loss, miss = softmax_terms(sf, logs, row_of(far, TAILS, step), qq)
        scale = miss * live_row(far, LIVE + step, edges) * (1.0 / 256.0)
        high, low = split(q.astype(F32) * scale)
        acc[...] += dot(high, qq[...], NT) + dot(low, qq[...], NT)
    grad[...] = acc[...].astype(BF16)


def finish_kernel(own, other, rows, grad, mean):
    grad[...] = own[...].astype(F32) + other[...].astype(F32)
    total = jnp.sum(rows[...], axis=0, keepdims=True)
    mean[...] = total[:, 0:1] / total[:, 1:2]


def kernel(body, outs, scratch, flops):
    return pl.pallas_call(
        body,
        out_shape=[jax.ShapeDtypeStruct(s, t) for s, t in outs],
        scratch_shapes=[pltpu.VMEM(s, t) for s, t in scratch],
        compiler_params=pltpu.CompilerParams(vmem_limit_bytes=48 * 2**20),
        cost_estimate=pl.CostEstimate(flops=flops, bytes_accessed=4 * 2**20, transcendentals=0),
    )


def shifted(x, by):
    peers = lax.axis_size("blk")
    return lax.ppermute(x, "blk", [(i, (i + by) % peers) for i in range(peers)])


def per_device(embeddings, relations, heads, tails, rels, negatives, live):
    edges = heads.shape[1]
    entities, width = embeddings.shape
    n_rel = relations.shape[0]
    devices = lax.axis_size("blk") * lax.axis_size("rep")
    emb = embeddings.T
    rel = relations.T
    lists = jnp.concatenate(
        [heads, tails, rels, negatives.reshape(STEPS, edges), jnp.broadcast_to(live, (STEPS, edges)),
         jnp.zeros((1, edges), jnp.int32)], axis=0)
    prev1 = shifted(emb, 1)
    next2 = shifted(emb, -2)
    next1 = shifted(emb, -1)
    prev2 = shifted(emb, 2)
    lists1 = shifted(lists, -1)
    lists2 = shifted(lists, -2)
    big = (width, edges)
    part, sums, q1, q2, r1, r2 = kernel(
        prepare_kernel,
        [((width, entities), F32), ((8, edges), F32)] + [(big, BF16)] * 4,
        [((n_rel, edges), BF16), (big, F32), (big, F32), (big, F32), ((entities, edges), F32), ((entities, edges), BF16)],
        6 * 10**9,
    )(emb, rel, lists)
    far_r1, far_r2 = kernel(far_relations_kernel, [(big, BF16)] * 2, [((n_rel, edges), BF16)], 3 * 10**9)(
        rel, lists1, lists2)
    own, rows = kernel(
        rest_kernel,
        [((width, entities), BF16), ((devices, 128), F32)],
        [(big, F32), (big, F32), (big, F32), ((entities, edges), F32), ((entities, edges), BF16), ((width, entities), F32)],
        4 * 10**9,
    )(emb, prev1, prev2, next1, next2, q1, q2, r1, r2, far_r1, far_r2, lists, lists1, lists2, part, sums)
    other = lax.ppermute(own, "rep", [(0, 1), (1, 0)])
    rows = lax.all_to_all(rows, ("blk", "rep"), 0, 0, tiled=True)
    grad, mean = kernel(finish_kernel, [((width, entities), F32), ((1, 1), F32)], [], 10**6)(own, other, rows)
    return grad.T, mean[0, 0]


def solution(mesh):
    placed = (
        P("blk", None),
        P(),
        P(None, ("blk", "rep")),
        P(None, ("blk", "rep")),
        P(None, ("blk", "rep")),
        P(None, ("blk", "rep"), None),
        P(None, ("blk", "rep")),
    )
    return jax.shard_map(
        per_device, mesh=mesh, in_specs=placed, out_specs=(P("blk", None), P()), check_vma=False
    )
```

```python
import jax
import jax.numpy as jnp
from jax import lax
from jax.experimental import pallas as pl
from jax.experimental.pallas import tpu as pltpu
from jax.sharding import PartitionSpec as P

STEPS = 3
F32 = jnp.float32
BF16 = jnp.bfloat16
NEVER = -1e30
TN = (((0,), (0,)), ((), ()))
NN = (((1,), (0,)), ((), ()))
NT = (((1,), (1,)), ((), ()))


def dot(a, b, dims):
    return lax.dot_general(a, b, dims, preferred_element_type=F32)


def one_hot(row, size):
    hit = lax.broadcasted_iota(jnp.int32, (size, row.shape[1]), 0) == row
    return jnp.where(hit, 1.0, 0.0).astype(BF16)


def gather_relations(rel_t, row, hot_ref):
    block = 256
    low = one_hot(row & (block - 1), block)
    high = row >> 8
    for j in range(rel_t.shape[1] // block):
        here = jnp.where(high == j, 1.0, 0.0).astype(BF16)
        hot_ref[j * block:(j + 1) * block, :] = low * here
    return dot(rel_t[...], hot_ref[...], NN)


def make_query(h_ref, r_ref, q_ref):
    half = h_ref.shape[0] // 2
    step = 40
    for c in range(0, half, step):
        re, im = slice(c, c + step), slice(half + c, half + c + step)
        h_re, h_im, r_re, r_im = h_ref[re, :], h_ref[im, :], r_ref[re, :], r_ref[im, :]
        q_ref[re, :] = h_re * r_re - h_im * r_im
        q_ref[im, :] = h_re * r_im + h_im * r_re


def head_grad(d_ref, r_ref, scale, out_ref):
    half = d_ref.shape[0] // 2
    step = 40
    for c in range(0, half, step):
        re, im = slice(c, c + step), slice(half + c, half + c + step)
        d_re, d_im, r_re, r_im = d_ref[re, :] * scale, d_ref[im, :] * scale, r_ref[re, :], r_ref[im, :]
        out_ref[re, :] = d_re * r_re + d_im * r_im
        out_ref[im, :] = d_im * r_re - d_re * r_im


def halves(row):
    half = row.shape[1] // 2
    return row[:, :half], row[:, half:]


def log_counts(neg_rows, entities, out_ref):
    for g, neg_row in enumerate(neg_rows):
        hot = one_hot(neg_row, entities)
        count = dot(hot, jnp.ones((neg_row.shape[1], 128), BF16), NN)
        out_ref[:, g * 128:(g + 1) * 128] = jnp.where(count > 0.5, jnp.log(jnp.maximum(count, 1.0)), NEVER)


def softmax_terms(s_ref, log_ref, tail_row, q_ref):
    entities, edges = s_ref.shape
    step = 32
    iota = lax.broadcasted_iota(jnp.int32, (step, edges), 0)
    top = jnp.full((8, edges), NEVER, F32)
    pos = jnp.zeros((8, edges), F32)
    for c in range(0, entities, step):
        s = s_ref[c:c + step, :]
        hit = jnp.where(iota == tail_row - c, s, 0.0)
        first, second = log_ref[c:c + step, :128], log_ref[c:c + step, 128:]
        log = jnp.concatenate([first, first, second, second], axis=1)
        s = s + log
        s_ref[c:c + step, :] = s
        for k in range(0, step, 8):
            pos = pos + hit[k:k + 8, :]
            top = jnp.maximum(top, s[k:k + 8, :])
    positive = jnp.sum(pos, axis=0, keepdims=True)
    top = jnp.max(top, axis=0, keepdims=True)
    total = jnp.zeros((8, edges), F32)
    for c in range(0, entities, step):
        e = jnp.exp(s_ref[c:c + step, :] - top)
        s_ref[c:c + step, :] = e
        for k in range(0, step, 8):
            total = total + e[k:k + 8, :]
    total = jnp.sum(total, axis=0, keepdims=True)
    share = 1.0 / total
    for c in range(0, entities, step):
        p = s_ref[c:c + step, :] * share
        q_ref[c:c + step, :] = jnp.where(iota == tail_row - c, p - 1.0, p).astype(BF16)
    gap = jnp.log(total) + top - positive
    low = jnp.exp(-jnp.abs(gap))
    loss = jnp.maximum(gap, 0.0) + jnp.log(1.0 + low)
    miss = jnp.where(gap >= 0.0, 1.0, low) / (1.0 + low)
    return loss, miss


def live_row(count, edges):
    group = jnp.where(lax.broadcasted_iota(jnp.int32, (1, edges), 1) < edges // 2, 0, 1)
    return jnp.where(group < count, 1.0, 0.0)


HEADS, TAILS, RELS, NEGS, LIVE = 0, 3, 6, 9, 12


def row_of(lists, kind, step):
    return lists[kind + step:kind + step + 1, :]


def split(x):
    high = x.astype(BF16)
    return high, (x - high.astype(F32)).astype(BF16)


def own_kernel(emb_in, rel_in, heads_in, tails_in, rels_in, negatives_in, live_in, lists, grad, sums,
               emb, rel, heads, tails, rels, negatives, live_groups, sems, hot, hf, rf, qf, sf, qq, log):
    pairs = ((rels_in, rels), (heads_in, heads), (tails_in, tails), (negatives_in, negatives),
             (live_in, live_groups), (emb_in, emb), (rel_in, rel))
    copies = [pltpu.make_async_copy(a, b, sems.at[k]) for k, (a, b) in enumerate(pairs)]
    for copy in copies:
        copy.start()
    for copy in copies[:5]:
        copy.wait()
    edges = heads.shape[1]
    half = edges // 2
    entities = emb.shape[1]
    lists[HEADS:HEADS + STEPS, :] = heads[...]
    lists[TAILS:TAILS + STEPS, :] = tails[...]
    lists[RELS:RELS + STEPS, :] = rels[...]
    for step in range(STEPS):
        for g in range(2):
            lists[NEGS + step:NEGS + step + 1, g * half:(g + 1) * half] = negatives[step, g:g + 1, :]
        lists[LIVE + step:LIVE + step + 1, :] = jnp.broadcast_to(live_groups[:, step:step + 1], (1, edges))
    lists[LIVE + STEPS:LIVE + STEPS + 1, :] = jnp.zeros((1, edges), jnp.int32)
    log_counts(halves(row_of(lists, NEGS, 0)), entities, log)
    head_hot = one_hot(row_of(lists, HEADS, 0), entities)
    copies[5].wait()
    hf[...] = dot(emb[...], head_hot, NN)
    copies[6].wait()
    rf[...] = gather_relations(rel, row_of(lists, RELS, 0), hot)
    make_query(hf, rf, qf)
    q = qf[...].astype(BF16)
    sf[...] = dot(emb[...], q, TN)
    loss, miss = softmax_terms(sf, log, row_of(lists, TAILS, 0), qq)
    live = live_row(row_of(lists, LIVE, 0), edges)
    scale = miss * live * (1.0 / 256.0)
    high, low = split(q.astype(F32) * scale)
    g = dot(high, qq[...], NT) + dot(low, qq[...], NT)
    hf[...] = dot(emb[...], qq[...], NN)
    head_grad(hf, rf, scale, qf)
    high, low = split(qf[...])
    grad[...] = g + dot(high, head_hot, NT) + dot(low, head_hot, NT)
    sums[0:1, :] = loss * live
    sums[1:2, :] = live


def prepare_kernel(emb, rel, lists, q1, q2, r1, r2, log1, log2, hot, hf, rf, qf):
    entities = emb.shape[1]
    for step, q_out, r_out, log in ((1, q1, r1, log1), (2, q2, r2, log2)):
        rf[...] = gather_relations(rel, row_of(lists, RELS, step), hot)
        head_hot = one_hot(row_of(lists, HEADS, step), entities)
        hf[...] = dot(emb[...], head_hot, NN)
        make_query(hf, rf, qf)
        log_counts(halves(row_of(lists, NEGS, step)), entities, log)
        r_out[...] = rf[...].astype(BF16)
        q_out[...] = qf[...].astype(BF16)


def far_kernel(rel, lists1, lists2, r1, r2, log1, log2, hot):
    entities = log1.shape[0]
    for step, lists, out, log in ((1, lists1, r1, log1), (2, lists2, r2, log2)):
        out[...] = gather_relations(rel, row_of(lists, RELS, step), hot).astype(BF16)
        log_counts(halves(row_of(lists, NEGS, step)), entities, log)


def head_bucket(step, tail, q_in, r_in, log, lists, acc, hf, rf, qf, sf, qq):
    edges, entities = lists.shape[1], tail.shape[1]
    sf[...] = dot(tail[...], q_in[...], TN)
    loss, miss = softmax_terms(sf, log, row_of(lists, TAILS, step), qq)
    live = live_row(row_of(lists, LIVE, step), edges)
    hf[...] = dot(tail[...], qq[...], NN)
    rf[...] = r_in[...].astype(F32)
    head_grad(hf, rf, miss * live * (1.0 / 256.0), qf)
    high, low = split(qf[...])
    head_hot = one_hot(row_of(lists, HEADS, step), entities)
    acc[...] += dot(high, head_hot, NT) + dot(low, head_hot, NT)
    return loss * live, live


def tail_bucket(step, emb, head, r_in, log, far, acc, hf, rf, qf, sf, qq):
    edges, entities = far.shape[1], emb.shape[1]
    hf[...] = dot(head[...], one_hot(row_of(far, HEADS, step), entities), NN)
    rf[...] = r_in[...].astype(F32)
    make_query(hf, rf, qf)
    q = qf[...].astype(BF16)
    sf[...] = dot(emb[...], q, TN)
    loss, miss = softmax_terms(sf, log, row_of(far, TAILS, step), qq)
    scale = miss * live_row(row_of(far, LIVE, step), edges) * (1.0 / 256.0)
    high, low = split(q.astype(F32) * scale)
    acc[...] += dot(high, qq[...], NT) + dot(low, qq[...], NT)


def second_kernel(emb, prev2, next2, q2, r2, log2, far_r2, far_log2, lists, lists2, part, sums,
                  grad, sums_out, hf, rf, qf, sf, qq):
    grad[...] = part[...]
    loss, live = head_bucket(2, prev2, q2, r2, log2, lists, grad, hf, rf, qf, sf, qq)
    sums_out[0:1, :] = sums[0:1, :] + loss
    sums_out[1:2, :] = sums[1:2, :] + live
    tail_bucket(2, emb, next2, far_r2, far_log2, lists2, grad, hf, rf, qf, sf, qq)


def first_kernel(core, emb, sibling, swapped, q1, r1, log1, far_r1, far_log1, lists, lists1, part, sums,
                 grad, rows, hf, rf, qf, sf, qq, acc, prev1, next1):
    even = core[0, 0] == 0
    prev1[...] = jnp.where(even, swapped[...], sibling[...])
    next1[...] = jnp.where(even, sibling[...], swapped[...])
    acc[...] = part[...]
    loss, live = head_bucket(1, prev1, q1, r1, log1, lists, acc, hf, rf, qf, sf, qq)
    lane = lax.broadcasted_iota(jnp.int32, (1, 128), 1)
    loss_all = jnp.sum(sums[0:1, :] + loss, axis=1, keepdims=True)
    live_all = jnp.sum(sums[1:2, :] + live, axis=1, keepdims=True)
    row = jnp.where(lane == 0, loss_all, jnp.where(lane == 1, live_all, 0.0))
    rows[...] = jnp.broadcast_to(row, rows.shape)
    tail_bucket(1, emb, next1, far_r1, far_log1, lists1, acc, hf, rf, qf, sf, qq)
    grad[...] = acc[...].astype(BF16)


def finish_kernel(own, other, rows, grad, mean):
    grad[...] = own[...].astype(F32) + other[...].astype(F32)
    total = jnp.sum(rows[...], axis=0, keepdims=True)
    mean[...] = total[:, 0:1] / total[:, 1:2]


def kernel(body, outs, scratch, flops, spaces, mib=48):
    return pl.pallas_call(
        body,
        out_shape=[jax.ShapeDtypeStruct(s, t) for s, t in outs],
        in_specs=[pl.BlockSpec(memory_space=m) for m in spaces],
        scratch_shapes=[pltpu.VMEM(*s) if isinstance(s, tuple) else s for s in scratch],
        compiler_params=pltpu.CompilerParams(vmem_limit_bytes=mib * 2**20),
        cost_estimate=pl.CostEstimate(flops=flops, bytes_accessed=4 * 2**20, transcendentals=0),
    )


def shifted(x, by):
    peers = lax.axis_size("blk")
    return lax.ppermute(x, "blk", [(i, (i + by) % peers) for i in range(peers)])


def exchanged(x):
    return lax.ppermute(x, "blk", [(i, i ^ 1) for i in range(lax.axis_size("blk"))])


def per_device(embeddings, relations, heads, tails, rels, negatives, live):
    edges = heads.shape[1]
    entities, width = embeddings.shape
    n_rel = relations.shape[0]
    devices = lax.axis_size("blk") * lax.axis_size("rep")
    core = lax.axis_index("blk") & 1
    emb = embeddings.T
    rel = relations.T
    prev2 = shifted(emb, 2)
    next2 = shifted(emb, -2)
    sibling = exchanged(emb)
    here = pltpu.VMEM
    big, grads, logs = (width, edges), (width, entities), (entities, 256)
    work = [(big, F32), (big, F32), (big, F32), ((entities, edges), F32), ((entities, edges), BF16)]
    hot = ((n_rel, edges), BF16)
    raw = (emb, rel, heads, tails, rels, negatives, live.T)
    lists, part, sums = kernel(
        own_kernel,
        [((16, edges), jnp.int32), (grads, F32), ((8, edges), F32)],
        [(x.shape, x.dtype) for x in raw] + [pltpu.SemaphoreType.DMA((len(raw),)), hot] + work + [(logs, F32)],
        3 * 10**9, [pltpu.HBM] * len(raw), 56,
    )(*raw)
    lists1 = shifted(lists, -1)
    lists2 = shifted(lists, -2)
    q1, q2, r1, r2, log1, log2 = kernel(
        prepare_kernel, [(big, BF16)] * 4 + [(logs, F32)] * 2, [hot] + work[:3], 4 * 10**9, [here] * 3)(emb, rel, lists)
    far_r1, far_r2, far_log1, far_log2 = kernel(
        far_kernel, [(big, BF16)] * 2 + [(logs, F32)] * 2, [hot], 3 * 10**9, [here] * 3)(rel, lists1, lists2)
    swapped = exchanged(jnp.where(core == 0, next2, prev2))
    part, sums = kernel(second_kernel, [(grads, F32), ((8, edges), F32)], work, 2 * 10**9, [here] * 12)(
        emb, prev2, next2, q2, r2, log2, far_r2, far_log2, lists, lists2, part, sums)
    own, rows = kernel(
        first_kernel, [(grads, BF16), ((devices, 128), F32)], work + [(grads, F32), (big, BF16), (big, BF16)],
        2 * 10**9, [pltpu.SMEM] + [here] * 12,
    )(core.reshape(1, 1), emb, sibling, swapped, q1, r1, log1, far_r1, far_log1, lists, lists1, part, sums)
    other = lax.ppermute(own, "rep", [(0, 1), (1, 0)])
    rows = lax.all_to_all(rows, ("blk", "rep"), 0, 0, tiled=True)
    grad, mean = kernel(finish_kernel, [(grads, F32), ((1, 1), F32)], [], 10**6, [here] * 3)(own, other, rows)
    return grad.T, mean[0, 0]


def solution(mesh):
    placed = (
        P("blk", None),
        P(),
        P(None, ("blk", "rep")),
        P(None, ("blk", "rep")),
        P(None, ("blk", "rep")),
        P(None, ("blk", "rep"), None),
        P(None, ("blk", "rep")),
    )
    return jax.shard_map(
        per_device, mesh=mesh, in_specs=placed, out_specs=(P("blk", None), P()), check_vma=False
    )
```

```python
import jax
import jax.numpy as jnp
from jax import lax
from jax.experimental import pallas as pl
from jax.experimental.pallas import tpu as pltpu
from jax.sharding import PartitionSpec as P

STEPS = 3
F32 = jnp.float32
BF16 = jnp.bfloat16
NEVER = -1e30
TN = (((0,), (0,)), ((), ()))
NN = (((1,), (0,)), ((), ()))
NT = (((1,), (1,)), ((), ()))


def dot(a, b, dims):
    return lax.dot_general(a, b, dims, preferred_element_type=F32)


def one_hot(row, size):
    hit = lax.broadcasted_iota(jnp.int32, (size, row.shape[1]), 0) == row
    return jnp.where(hit, 1.0, 0.0).astype(BF16)


def gather_relations(rel_t, row, hot_ref):
    block = 256
    low = one_hot(row & (block - 1), block)
    high = row >> 8
    for j in range(rel_t.shape[1] // block):
        here = jnp.where(high == j, 1.0, 0.0).astype(BF16)
        hot_ref[j * block:(j + 1) * block, :] = low * here
    return dot(rel_t[...], hot_ref[...], NN)


def make_query(h_ref, r_ref, q_ref):
    half = h_ref.shape[0] // 2
    step = 40
    for c in range(0, half, step):
        re, im = slice(c, c + step), slice(half + c, half + c + step)
        h_re, h_im, r_re, r_im = h_ref[re, :], h_ref[im, :], r_ref[re, :], r_ref[im, :]
        q_ref[re, :] = h_re * r_re - h_im * r_im
        q_ref[im, :] = h_re * r_im + h_im * r_re


def head_grad(d_ref, r_ref, scale, out_ref):
    half = d_ref.shape[0] // 2
    step = 40
    for c in range(0, half, step):
        re, im = slice(c, c + step), slice(half + c, half + c + step)
        d_re, d_im, r_re, r_im = d_ref[re, :] * scale, d_ref[im, :] * scale, r_ref[re, :], r_ref[im, :]
        out_ref[re, :] = d_re * r_re + d_im * r_im
        out_ref[im, :] = d_im * r_re - d_re * r_im


def halves(row):
    half = row.shape[1] // 2
    return row[:, :half], row[:, half:]


def log_counts(neg_rows, entities, out_ref):
    for g, neg_row in enumerate(neg_rows):
        hot = one_hot(neg_row, entities)
        count = dot(hot, jnp.ones((neg_row.shape[1], 128), BF16), NN)
        out_ref[:, g * 128:(g + 1) * 128] = jnp.where(count > 0.5, jnp.log(jnp.maximum(count, 1.0)), NEVER)


def softmax_terms(s_ref, log_ref, tail_row, q_ref):
    entities, edges = s_ref.shape
    step = 32
    iota = lax.broadcasted_iota(jnp.int32, (step, edges), 0)
    top = jnp.full((8, edges), NEVER, F32)
    pos = jnp.zeros((8, edges), F32)
    for c in range(0, entities, step):
        s = s_ref[c:c + step, :]
        hit = jnp.where(iota == tail_row - c, s, 0.0)
        first, second = log_ref[c:c + step, :128], log_ref[c:c + step, 128:]
        log = jnp.concatenate([first, first, second, second], axis=1)
        s = s + log
        s_ref[c:c + step, :] = s
        for k in range(0, step, 8):
            pos = pos + hit[k:k + 8, :]
            top = jnp.maximum(top, s[k:k + 8, :])
    positive = jnp.sum(pos, axis=0, keepdims=True)
    top = jnp.max(top, axis=0, keepdims=True)
    total = jnp.zeros((8, edges), F32)
    for c in range(0, entities, step):
        e = jnp.exp(s_ref[c:c + step, :] - top)
        s_ref[c:c + step, :] = e
        for k in range(0, step, 8):
            total = total + e[k:k + 8, :]
    total = jnp.sum(total, axis=0, keepdims=True)
    share = 1.0 / total
    for c in range(0, entities, step):
        p = s_ref[c:c + step, :] * share
        q_ref[c:c + step, :] = jnp.where(iota == tail_row - c, p - 1.0, p).astype(BF16)
    gap = jnp.log(total) + top - positive
    low = jnp.exp(-jnp.abs(gap))
    loss = jnp.maximum(gap, 0.0) + jnp.log(1.0 + low)
    miss = jnp.where(gap >= 0.0, 1.0, low) / (1.0 + low)
    return loss, miss


def live_row(count, edges):
    group = jnp.where(lax.broadcasted_iota(jnp.int32, (1, edges), 1) < edges // 2, 0, 1)
    return jnp.where(group < count, 1.0, 0.0)


HEADS, TAILS, RELS, NEGS, LIVE = 0, 3, 6, 9, 12


def row_of(lists, kind, step):
    return lists[kind + step:kind + step + 1, :]


def split(x):
    high = x.astype(BF16)
    return high, (x - high.astype(F32)).astype(BF16)


def pack_kernel(heads_in, tails_in, rels_in, negatives_in, live_in, lists, heads, tails, rels, negatives, live_groups, sems):
    pairs = ((heads_in, heads), (tails_in, tails), (rels_in, rels), (negatives_in, negatives), (live_in, live_groups))
    copies = [pltpu.make_async_copy(a, b, sems.at[k]) for k, (a, b) in enumerate(pairs)]
    for copy in copies:
        copy.start()
    for copy in copies:
        copy.wait()
    edges = heads.shape[1]
    half = edges // 2
    lists[HEADS:HEADS + STEPS, :] = heads[...]
    lists[TAILS:TAILS + STEPS, :] = tails[...]
    lists[RELS:RELS + STEPS, :] = rels[...]
    for step in range(STEPS):
        for g in range(2):
            lists[NEGS + step:NEGS + step + 1, g * half:(g + 1) * half] = negatives[step, g:g + 1, :]
        lists[LIVE + step:LIVE + step + 1, :] = jnp.broadcast_to(live_groups[:, step:step + 1], (1, edges))
    lists[LIVE + STEPS:LIVE + STEPS + 1, :] = jnp.zeros((1, edges), jnp.int32)


def prepare_kernel(emb, rel, lists, grad, sums, q1, q2, r1, r2, log1, log2, hot, hf, rf, qf, sf, qq, log):
    edges, entities = lists.shape[1], emb.shape[1]
    head_hot = one_hot(row_of(lists, HEADS, 0), entities)
    hf[...] = dot(emb[...], head_hot, NN)
    rf[...] = gather_relations(rel, row_of(lists, RELS, 0), hot)
    make_query(hf, rf, qf)
    q = qf[...].astype(BF16)
    sf[...] = dot(emb[...], q, TN)
    log_counts(halves(row_of(lists, NEGS, 0)), entities, log)
    loss, miss = softmax_terms(sf, log, row_of(lists, TAILS, 0), qq)
    live = live_row(row_of(lists, LIVE, 0), edges)
    scale = miss * live * (1.0 / 256.0)
    high, low = split(q.astype(F32) * scale)
    g = dot(high, qq[...], NT) + dot(low, qq[...], NT)
    hf[...] = dot(emb[...], qq[...], NN)
    head_grad(hf, rf, scale, qf)
    high, low = split(qf[...])
    grad[...] = g + dot(high, head_hot, NT) + dot(low, head_hot, NT)
    sums[0:1, :] = loss * live
    sums[1:2, :] = live
    for step, q_out, r_out, log_out in ((1, q1, r1, log1), (2, q2, r2, log2)):
        rf[...] = gather_relations(rel, row_of(lists, RELS, step), hot)
        hf[...] = dot(emb[...], one_hot(row_of(lists, HEADS, step), entities), NN)
        make_query(hf, rf, qf)
        log_counts(halves(row_of(lists, NEGS, step)), entities, log_out)
        r_out[...] = rf[...].astype(BF16)
        q_out[...] = qf[...].astype(BF16)


def far_kernel(rel, lists1, lists2, r1, r2, log1, log2, hot):
    entities = log1.shape[0]
    for step, lists, out, log in ((1, lists1, r1, log1), (2, lists2, r2, log2)):
        out[...] = gather_relations(rel, row_of(lists, RELS, step), hot).astype(BF16)
        log_counts(halves(row_of(lists, NEGS, step)), entities, log)


def head_bucket(step, tail, q_in, r_in, log, lists, acc, hf, rf, qf, sf, qq):
    edges, entities = lists.shape[1], tail.shape[1]
    sf[...] = dot(tail[...], q_in[...], TN)
    loss, miss = softmax_terms(sf, log, row_of(lists, TAILS, step), qq)
    live = live_row(row_of(lists, LIVE, step), edges)
    hf[...] = dot(tail[...], qq[...], NN)
    rf[...] = r_in[...].astype(F32)
    head_grad(hf, rf, miss * live * (1.0 / 256.0), qf)
    high, low = split(qf[...])
    head_hot = one_hot(row_of(lists, HEADS, step), entities)
    acc[...] += dot(high, head_hot, NT) + dot(low, head_hot, NT)
    return loss * live, live


def tail_bucket(step, emb, head, r_in, log, far, acc, hf, rf, qf, sf, qq):
    edges, entities = far.shape[1], emb.shape[1]
    hf[...] = dot(head[...], one_hot(row_of(far, HEADS, step), entities), NN)
    rf[...] = r_in[...].astype(F32)
    make_query(hf, rf, qf)
    q = qf[...].astype(BF16)
    sf[...] = dot(emb[...], q, TN)
    loss, miss = softmax_terms(sf, log, row_of(far, TAILS, step), qq)
    scale = miss * live_row(row_of(far, LIVE, step), edges) * (1.0 / 256.0)
    high, low = split(q.astype(F32) * scale)
    acc[...] += dot(high, qq[...], NT) + dot(low, qq[...], NT)


def heads_kernel(core, prev2, sibling, swapped, q1, q2, r1, r2, log1, log2, lists, part, sums, grad, row,
                 hf, rf, qf, sf, qq, prev1):
    grad[...] = part[...]
    loss2, live2 = head_bucket(2, prev2, q2, r2, log2, lists, grad, hf, rf, qf, sf, qq)
    prev1[...] = jnp.where(core[0, 0] == 0, swapped[...], sibling[...])
    loss1, live1 = head_bucket(1, prev1, q1, r1, log1, lists, grad, hf, rf, qf, sf, qq)
    loss_all = jnp.sum(sums[0:1, :] + loss1 + loss2, axis=1, keepdims=True)
    live_all = jnp.sum(sums[1:2, :] + live1 + live2, axis=1, keepdims=True)
    lane = lax.broadcasted_iota(jnp.int32, row.shape, 1)
    row[...] = jnp.where(lane == 0, loss_all, jnp.where(lane == 1, live_all, 0.0))


def tails2_kernel(emb, next2, far_r2, far_log2, lists2, part, grad, hf, rf, qf, sf, qq):
    grad[...] = part[...]
    tail_bucket(2, emb, next2, far_r2, far_log2, lists2, grad, hf, rf, qf, sf, qq)


def tails1_kernel(core, emb, sibling, swapped, far_r1, far_log1, lists1, part, row0, row1, row2, row3, grad, rows,
                  hf, rf, qf, sf, qq, acc, next1):
    next1[...] = jnp.where(core[0, 0] == 0, sibling[...], swapped[...])
    acc[...] = part[...]
    tail_bucket(1, emb, next1, far_r1, far_log1, lists1, acc, hf, rf, qf, sf, qq)
    grad[...] = acc[...].astype(BF16)
    row = (row0[...] + row1[...]) + (row2[...] + row3[...])
    rows[...] = jnp.broadcast_to(row[0:1, :], rows.shape)


def finish_kernel(own, other, rows, grad, mean):
    grad[...] = own[...].astype(F32) + other[...].astype(F32)
    total = jnp.sum(rows[...], axis=0, keepdims=True)
    mean[...] = total[:, 0:1] / total[:, 1:2]


def kernel(body, outs, scratch, flops, spaces, mib=24):
    return pl.pallas_call(
        body,
        out_shape=[jax.ShapeDtypeStruct(s, t) for s, t in outs],
        in_specs=[pl.BlockSpec(memory_space=m) for m in spaces],
        scratch_shapes=[pltpu.VMEM(*s) if isinstance(s, tuple) else s for s in scratch],
        compiler_params=pltpu.CompilerParams(vmem_limit_bytes=mib * 2**20),
        cost_estimate=pl.CostEstimate(flops=flops, bytes_accessed=4 * 2**20, transcendentals=0),
    )


def shifted(x, by):
    peers = lax.axis_size("blk")
    return lax.ppermute(x, "blk", [(i, (i + by) % peers) for i in range(peers)])


def exchanged(x):
    return lax.ppermute(x, "blk", [(i, i ^ 1) for i in range(lax.axis_size("blk"))])


def per_device(embeddings, relations, heads, tails, rels, negatives, live):
    edges = heads.shape[1]
    entities, width = embeddings.shape
    n_rel = relations.shape[0]
    blocks = lax.axis_size("blk")
    core = (lax.axis_index("blk") & 1).reshape(1, 1)
    emb = embeddings.T
    rel = relations.T
    here = pltpu.VMEM
    big, grads, logs, rows_of = (width, edges), (width, entities), (entities, 256), (8, 128)
    work = [(big, F32), (big, F32), (big, F32), ((entities, edges), F32), ((entities, edges), BF16)]
    hot = ((n_rel, edges), BF16)
    prev2 = shifted(emb, 2)
    next2 = shifted(emb, -2)
    sibling = exchanged(emb)
    raw = (heads, tails, rels, negatives, live.T)
    (lists,) = kernel(
        pack_kernel, [((16, edges), jnp.int32)],
        [(x.shape, x.dtype) for x in raw] + [pltpu.SemaphoreType.DMA((len(raw),))],
        2 * 10**9, [pltpu.HBM] * len(raw), 56,
    )(*raw)
    lists1 = shifted(lists, -1)
    lists2 = shifted(lists, -2)
    part, sums, q1, q2, r1, r2, log1, log2 = kernel(
        prepare_kernel,
        [(grads, F32), ((8, edges), F32)] + [(big, BF16)] * 4 + [(logs, F32)] * 2,
        [hot] + work + [(logs, F32)], 20 * 10**9, [here] * 3)(emb, rel, lists)
    far_r1, far_r2, far_log1, far_log2 = kernel(
        far_kernel, [(big, BF16)] * 2 + [(logs, F32)] * 2, [hot], 20 * 10**9, [here] * 3)(rel, lists1, lists2)
    swapped = exchanged(jnp.where(core[0, 0] == 0, next2, prev2))
    part, row = kernel(
        heads_kernel, [(grads, F32), (rows_of, F32)], work + [(big, BF16)], 3 * 10**9, [pltpu.SMEM] + [here] * 12,
    )(core, prev2, sibling, swapped, q1, q2, r1, r2, log1, log2, lists, part, sums)
    near = [lax.ppermute(row, ("blk", "rep"), [(i, i ^ k) for i in range(2 * blocks)]) for k in (2, 1, 3)]
    (part,) = kernel(tails2_kernel, [(grads, F32)], work, 2 * 10**9, [here] * 6)(
        emb, next2, far_r2, far_log2, lists2, part)
    own, rows = kernel(
        tails1_kernel, [(grads, BF16), ((blocks // 2, 128), F32)], work + [(grads, F32), (big, BF16)],
        2 * 10**9, [pltpu.SMEM] + [here] * 11,
    )(core, emb, sibling, swapped, far_r1, far_log1, lists1, part, row, *near)
    other = lax.ppermute(own, "rep", [(0, 1), (1, 0)])
    rows = lax.all_to_all(rows, "blk", 0, 0, tiled=True,
                          axis_index_groups=[[k + 2 * i for i in range(blocks // 2)] for k in (0, 1)])
    grad, mean = kernel(finish_kernel, [(grads, F32), ((1, 1), F32)], [], 10**6, [here] * 3)(own, other, rows)
    return grad.T, mean[0, 0]


def solution(mesh):
    placed = (
        P("blk", None),
        P(),
        P(None, ("blk", "rep")),
        P(None, ("blk", "rep")),
        P(None, ("blk", "rep")),
        P(None, ("blk", "rep"), None),
        P(None, ("blk", "rep")),
    )
    return jax.shard_map(
        per_device, mesh=mesh, in_specs=placed, out_specs=(P("blk", None), P()), check_vma=False
    )
```

```python
import jax
import jax.numpy as jnp
from jax import lax
from jax.experimental import pallas as pl
from jax.experimental.pallas import tpu as pltpu
from jax.sharding import PartitionSpec as P

STEPS = 3
F32 = jnp.float32
BF16 = jnp.bfloat16
NEVER = -1e30
TN = (((0,), (0,)), ((), ()))
NN = (((1,), (0,)), ((), ()))
NT = (((1,), (1,)), ((), ()))


def dot(a, b, dims):
    return lax.dot_general(a, b, dims, preferred_element_type=F32)


def one_hot(row, size):
    hit = lax.broadcasted_iota(jnp.int32, (size, row.shape[1]), 0) == row
    return jnp.where(hit, 1.0, 0.0).astype(BF16)


def gather_relations(rel_t, row, hot_ref):
    block = 256
    low = one_hot(row & (block - 1), block)
    high = row >> 8
    for j in range(rel_t.shape[1] // block):
        here = jnp.where(high == j, 1.0, 0.0).astype(BF16)
        hot_ref[j * block:(j + 1) * block, :] = low * here
    return dot(rel_t[...], hot_ref[...], NN)


def make_query(h_ref, r_ref, q_ref):
    half = h_ref.shape[0] // 2
    step = 40
    for c in range(0, half, step):
        re, im = slice(c, c + step), slice(half + c, half + c + step)
        h_re, h_im, r_re, r_im = h_ref[re, :], h_ref[im, :], r_ref[re, :], r_ref[im, :]
        q_ref[re, :] = h_re * r_re - h_im * r_im
        q_ref[im, :] = h_re * r_im + h_im * r_re


def head_grad(d_ref, r_ref, scale, out_ref):
    half = d_ref.shape[0] // 2
    step = 40
    for c in range(0, half, step):
        re, im = slice(c, c + step), slice(half + c, half + c + step)
        d_re, d_im, r_re, r_im = d_ref[re, :] * scale, d_ref[im, :] * scale, r_ref[re, :], r_ref[im, :]
        out_ref[re, :] = d_re * r_re + d_im * r_im
        out_ref[im, :] = d_im * r_re - d_re * r_im


def halves(row):
    half = row.shape[1] // 2
    return row[:, :half], row[:, half:]


def log_counts(neg_rows, entities, out_ref):
    for g, neg_row in enumerate(neg_rows):
        hot = one_hot(neg_row, entities)
        count = dot(hot, jnp.ones((neg_row.shape[1], 128), BF16), NN)
        out_ref[:, g * 128:(g + 1) * 128] = jnp.where(count > 0.5, jnp.log(jnp.maximum(count, 1.0)), NEVER)


def softmax_terms(s_ref, log_ref, tail_row, q_ref):
    entities, edges = s_ref.shape
    step = 32
    iota = lax.broadcasted_iota(jnp.int32, (step, edges), 0)
    top = jnp.full((8, edges), NEVER, F32)
    pos = jnp.zeros((8, edges), F32)
    for c in range(0, entities, step):
        s = s_ref[c:c + step, :]
        hit = jnp.where(iota == tail_row - c, s, 0.0)
        first, second = log_ref[c:c + step, :128], log_ref[c:c + step, 128:]
        log = jnp.concatenate([first, first, second, second], axis=1)
        s = s + log
        s_ref[c:c + step, :] = s
        for k in range(0, step, 8):
            pos = pos + hit[k:k + 8, :]
            top = jnp.maximum(top, s[k:k + 8, :])
    positive = jnp.sum(pos, axis=0, keepdims=True)
    top = jnp.max(top, axis=0, keepdims=True)
    total = jnp.zeros((8, edges), F32)
    for c in range(0, entities, step):
        e = jnp.exp(s_ref[c:c + step, :] - top)
        s_ref[c:c + step, :] = e
        for k in range(0, step, 8):
            total = total + e[k:k + 8, :]
    total = jnp.sum(total, axis=0, keepdims=True)
    share = 1.0 / total
    for c in range(0, entities, step):
        p = s_ref[c:c + step, :] * share
        q_ref[c:c + step, :] = jnp.where(iota == tail_row - c, p - 1.0, p).astype(BF16)
    gap = jnp.log(total) + top - positive
    low = jnp.exp(-jnp.abs(gap))
    loss = jnp.maximum(gap, 0.0) + jnp.log(1.0 + low)
    miss = jnp.where(gap >= 0.0, 1.0, low) / (1.0 + low)
    return loss, miss


def live_row(count, edges):
    group = jnp.where(lax.broadcasted_iota(jnp.int32, (1, edges), 1) < edges // 2, 0, 1)
    return jnp.where(group < count, 1.0, 0.0)


HEADS, TAILS, RELS, NEGS, LIVE = 0, 3, 6, 9, 12


def row_of(lists, kind, step):
    return lists[kind + step:kind + step + 1, :]


def split(x):
    high = x.astype(BF16)
    return high, (x - high.astype(F32)).astype(BF16)


def pack_kernel(heads_in, tails_in, rels_in, negatives_in, live_in, lists, heads, tails, rels, negatives, live_groups, sems):
    pairs = ((heads_in, heads), (tails_in, tails), (rels_in, rels), (negatives_in, negatives), (live_in, live_groups))
    copies = [pltpu.make_async_copy(a, b, sems.at[k]) for k, (a, b) in enumerate(pairs)]
    for copy in copies:
        copy.start()
    for copy in copies:
        copy.wait()
    edges = heads.shape[1]
    half = edges // 2
    lists[HEADS:HEADS + STEPS, :] = heads[...]
    lists[TAILS:TAILS + STEPS, :] = tails[...]
    lists[RELS:RELS + STEPS, :] = rels[...]
    for step in range(STEPS):
        for g in range(2):
            lists[NEGS + step:NEGS + step + 1, g * half:(g + 1) * half] = negatives[step, g:g + 1, :]
        lists[LIVE + step:LIVE + step + 1, :] = jnp.broadcast_to(live_groups[:, step:step + 1], (1, edges))
    lists[LIVE + STEPS:LIVE + STEPS + 1, :] = jnp.zeros((1, edges), jnp.int32)


def prepare_kernel(emb, rel, heads, tails, rels, negatives, live_groups, grad, sums, q1, q2, r1, r2, log1, log2, hot, hf, rf, qf, sf, qq, log):
    edges, entities = heads.shape[1], emb.shape[1]
    head_hot = one_hot(heads[0:1, :], entities)
    hf[...] = dot(emb[...], head_hot, NN)
    rf[...] = gather_relations(rel, rels[0:1, :], hot)
    make_query(hf, rf, qf)
    q = qf[...].astype(BF16)
    sf[...] = dot(emb[...], q, TN)
    log_counts([negatives[0, g:g + 1, :] for g in range(2)], entities, log)
    loss, miss = softmax_terms(sf, log, tails[0:1, :], qq)
    live = live_row(live_groups[:, 0:1], edges)
    scale = miss * live * (1.0 / 256.0)
    high, low = split(q.astype(F32) * scale)
    g = dot(high, qq[...], NT) + dot(low, qq[...], NT)
    hf[...] = dot(emb[...], qq[...], NN)
    head_grad(hf, rf, scale, qf)
    high, low = split(qf[...])
    grad[...] = g + dot(high, head_hot, NT) + dot(low, head_hot, NT)
    sums[0:1, :] = loss * live
    sums[1:2, :] = live
    for step, q_out, r_out, log_out in ((1, q1, r1, log1), (2, q2, r2, log2)):
        rf[...] = gather_relations(rel, rels[step:step + 1, :], hot)
        hf[...] = dot(emb[...], one_hot(heads[step:step + 1, :], entities), NN)
        make_query(hf, rf, qf)
        log_counts([negatives[step, g:g + 1, :] for g in range(2)], entities, log_out)
        r_out[...] = rf[...].astype(BF16)
        q_out[...] = qf[...].astype(BF16)


def far_kernel(rel, lists1, lists2, r1, r2, log1, log2, hot):
    entities = log1.shape[0]
    for step, lists, out, log in ((1, lists1, r1, log1), (2, lists2, r2, log2)):
        out[...] = gather_relations(rel, row_of(lists, RELS, step), hot).astype(BF16)
        log_counts(halves(row_of(lists, NEGS, step)), entities, log)


def choose_kernel(even, odd, out):
    out[...] = jnp.where(lax.axis_index("blk") & 1 == 0, even[...], odd[...])


def head_bucket(step, tail, q_in, r_in, log, heads, tails, live_groups, acc, hf, rf, qf, sf, qq):
    edges, entities = heads.shape[1], tail.shape[1]
    sf[...] = dot(tail[...], q_in[...], TN)
    loss, miss = softmax_terms(sf, log, tails[step:step + 1, :], qq)
    live = live_row(live_groups[:, step:step + 1], edges)
    hf[...] = dot(tail[...], qq[...], NN)
    rf[...] = r_in[...].astype(F32)
    head_grad(hf, rf, miss * live * (1.0 / 256.0), qf)
    high, low = split(qf[...])
    head_hot = one_hot(heads[step:step + 1, :], entities)
    acc[...] += dot(high, head_hot, NT) + dot(low, head_hot, NT)
    return loss * live, live


def tail_bucket(step, emb, head, r_in, log, far, acc, hf, rf, qf, sf, qq):
    edges, entities = far.shape[1], emb.shape[1]
    hf[...] = dot(head[...], one_hot(row_of(far, HEADS, step), entities), NN)
    rf[...] = r_in[...].astype(F32)
    make_query(hf, rf, qf)
    q = qf[...].astype(BF16)
    sf[...] = dot(emb[...], q, TN)
    loss, miss = softmax_terms(sf, log, row_of(far, TAILS, step), qq)
    scale = miss * live_row(row_of(far, LIVE, step), edges) * (1.0 / 256.0)
    high, low = split(q.astype(F32) * scale)
    acc[...] += dot(high, qq[...], NT) + dot(low, qq[...], NT)


def heads_kernel(prev2, sibling, swapped, q1, q2, r1, r2, log1, log2, heads, tails, live_groups, part, sums, grad, row,
                 hf, rf, qf, sf, qq, prev1):
    grad[...] = part[...]
    loss2, live2 = head_bucket(2, prev2, q2, r2, log2, heads, tails, live_groups, grad, hf, rf, qf, sf, qq)
    prev1[...] = jnp.where(lax.axis_index("blk") & 1 == 0, swapped[...], sibling[...])
    loss1, live1 = head_bucket(1, prev1, q1, r1, log1, heads, tails, live_groups, grad, hf, rf, qf, sf, qq)
    loss_all = jnp.sum(sums[0:1, :] + loss1 + loss2, axis=1, keepdims=True)
    live_all = jnp.sum(sums[1:2, :] + live1 + live2, axis=1, keepdims=True)
    lane = lax.broadcasted_iota(jnp.int32, row.shape, 1)
    row[...] = jnp.where(lane == 0, loss_all, jnp.where(lane == 1, live_all, 0.0))


def tails2_kernel(emb, next2, far_r2, far_log2, lists2, part, grad, hf, rf, qf, sf, qq):
    grad[...] = part[...]
    tail_bucket(2, emb, next2, far_r2, far_log2, lists2, grad, hf, rf, qf, sf, qq)


def tails1_kernel(emb, sibling, swapped, far_r1, far_log1, lists1, part, row, core_row, grad, rows,
                  hf, rf, qf, sf, qq, acc, next1):
    next1[...] = jnp.where(lax.axis_index("blk") & 1 == 0, sibling[...], swapped[...])
    acc[...] = part[...]
    tail_bucket(1, emb, next1, far_r1, far_log1, lists1, acc, hf, rf, qf, sf, qq)
    grad[...] = acc[...].astype(BF16)
    rows[...] = jnp.broadcast_to(row[0:1, :] + core_row[0:1, :], rows.shape)


def finish_kernel(own, other, rows, grad, mean):
    grad[...] = own[...].astype(F32) + other[...].astype(F32)
    total = jnp.sum(rows[...], axis=0, keepdims=True)
    mean[...] = total[:, 0:1] / total[:, 1:2]


def kernel(body, outs, scratch, flops, spaces, mib=48):
    return pl.pallas_call(
        body,
        out_shape=[jax.ShapeDtypeStruct(s, t) for s, t in outs],
        in_specs=[pl.BlockSpec(memory_space=m) for m in spaces],
        scratch_shapes=[pltpu.VMEM(*s) if isinstance(s, tuple) else s for s in scratch],
        compiler_params=pltpu.CompilerParams(vmem_limit_bytes=mib * 2**20),
        cost_estimate=pl.CostEstimate(flops=flops, bytes_accessed=4 * 2**20, transcendentals=0),
    )


def shifted(x, by):
    peers = lax.axis_size("blk")
    return lax.ppermute(x, "blk", [(i, (i + by) % peers) for i in range(peers)])


def exchanged(x):
    return lax.ppermute(x, "blk", [(i, i ^ 1) for i in range(lax.axis_size("blk"))])


def per_device(embeddings, relations, heads, tails, rels, negatives, live):
    edges = heads.shape[1]
    entities, width = embeddings.shape
    n_rel = relations.shape[0]
    blocks = lax.axis_size("blk")
    emb = embeddings.T
    rel = relations.T
    here = pltpu.VMEM
    big, grads, logs, rows_of = (width, edges), (width, entities), (entities, 256), (8, 128)
    work = [(big, F32), (big, F32), (big, F32), ((entities, edges), F32), ((entities, edges), BF16)]
    hot = ((n_rel, edges), BF16)
    prev2 = shifted(emb, 2)
    next2 = shifted(emb, -2)
    sibling = exchanged(emb)
    raw = (heads, tails, rels, negatives, live.T)
    (lists,) = kernel(
        pack_kernel, [((16, edges), jnp.int32)],
        [(x.shape, x.dtype) for x in raw] + [pltpu.SemaphoreType.DMA((len(raw),))],
        2 * 10**9, [pltpu.HBM] * len(raw), 56,
    )(*raw)
    lists1 = shifted(lists, -1)
    lists2 = shifted(lists, -2)
    part, sums, q1, q2, r1, r2, log1, log2 = kernel(
        prepare_kernel,
        [(grads, F32), ((8, edges), F32)] + [(big, BF16)] * 4 + [(logs, F32)] * 2,
        [hot] + work + [(logs, F32)], 20 * 10**9, [here] * 7)(emb, rel, *raw)
    far_r1, far_r2, far_log1, far_log2 = kernel(
        far_kernel, [(big, BF16)] * 2 + [(logs, F32)] * 2, [hot], 7 * 10**9, [here] * 3)(rel, lists1, lists2)
    (passed,) = kernel(choose_kernel, [(big, BF16)], [], 10**6, [here] * 2)(next2, prev2)
    swapped = exchanged(passed)
    part, row = kernel(
        heads_kernel, [(grads, F32), (rows_of, F32)], work + [(big, BF16)], 3 * 10**9, [here] * 14,
    )(prev2, sibling, swapped, q1, q2, r1, r2, log1, log2, heads, tails, live.T, part, sums)
    core_row = exchanged(row)
    (part,) = kernel(tails2_kernel, [(grads, F32)], work, 2 * 10**9, [here] * 6)(
        emb, next2, far_r2, far_log2, lists2, part)
    own, rows = kernel(
        tails1_kernel, [(grads, BF16), ((blocks, 128), F32)], work + [(grads, F32), (big, BF16)],
        2 * 10**9, [here] * 9,
    )(emb, sibling, swapped, far_r1, far_log1, lists1, part, row, core_row)
    other = lax.ppermute(own, "rep", [(0, 1), (1, 0)])
    rows = lax.all_to_all(rows, ("blk", "rep"), 0, 0, tiled=True,
                          axis_index_groups=[[4 * i + 2 * k + r for i in range(blocks // 2) for r in (0, 1)] for k in (0, 1)])
    grad, mean = kernel(finish_kernel, [(grads, F32), ((1, 1), F32)], [], 10**6, [here] * 3)(own, other, rows)
    return grad.T, mean[0, 0]


def solution(mesh):
    placed = (
        P("blk", None),
        P(),
        P(None, ("blk", "rep")),
        P(None, ("blk", "rep")),
        P(None, ("blk", "rep")),
        P(None, ("blk", "rep"), None),
        P(None, ("blk", "rep")),
    )
    return jax.shard_map(
        per_device, mesh=mesh, in_specs=placed, out_specs=(P("blk", None), P()), check_vma=False
    )
```

```python
import jax
import jax.numpy as jnp
from jax import lax
from jax.experimental import pallas as pl
from jax.experimental.pallas import tpu as pltpu
from jax.sharding import PartitionSpec as P

STEPS = 3
F32 = jnp.float32
BF16 = jnp.bfloat16
NEVER = -1e30
TN = (((0,), (0,)), ((), ()))
NN = (((1,), (0,)), ((), ()))
NT = (((1,), (1,)), ((), ()))


def dot(a, b, dims):
    return lax.dot_general(a, b, dims, preferred_element_type=F32)


def one_hot(row, size):
    hit = lax.broadcasted_iota(jnp.int32, (size, row.shape[1]), 0) == row
    return jnp.where(hit, 1.0, 0.0).astype(BF16)


def gather_relations(rel_t, row, hot_ref):
    block = 256
    low = one_hot(row & (block - 1), block)
    high = row >> 8
    for j in range(rel_t.shape[1] // block):
        here = jnp.where(high == j, 1.0, 0.0).astype(BF16)
        hot_ref[j * block:(j + 1) * block, :] = low * here
    return dot(rel_t[...], hot_ref[...], NN)


def make_query(h_ref, r_ref, q_ref):
    half = h_ref.shape[0] // 2
    step = 40
    for c in range(0, half, step):
        re, im = slice(c, c + step), slice(half + c, half + c + step)
        h_re, h_im, r_re, r_im = h_ref[re, :], h_ref[im, :], r_ref[re, :], r_ref[im, :]
        q_ref[re, :] = h_re * r_re - h_im * r_im
        q_ref[im, :] = h_re * r_im + h_im * r_re


def head_grad(d_ref, r_ref, scale, out_ref):
    half = d_ref.shape[0] // 2
    step = 40
    for c in range(0, half, step):
        re, im = slice(c, c + step), slice(half + c, half + c + step)
        d_re, d_im, r_re, r_im = d_ref[re, :] * scale, d_ref[im, :] * scale, r_ref[re, :], r_ref[im, :]
        out_ref[re, :] = d_re * r_re + d_im * r_im
        out_ref[im, :] = d_im * r_re - d_re * r_im


def halves(row):
    half = row.shape[1] // 2
    return row[:, :half], row[:, half:]


def log_counts(neg_rows, entities, out_ref):
    for g, neg_row in enumerate(neg_rows):
        hot = one_hot(neg_row, entities)
        count = dot(hot, jnp.ones((neg_row.shape[1], 128), BF16), NN)
        out_ref[:, g * 128:(g + 1) * 128] = jnp.where(count > 0.5, jnp.log(jnp.maximum(count, 1.0)), NEVER)


def softmax_terms(s_ref, log_ref, tail_row, q_ref):
    entities, edges = s_ref.shape
    step = 32
    iota = lax.broadcasted_iota(jnp.int32, (step, edges), 0)
    top = jnp.full((8, edges), NEVER, F32)
    pos = jnp.zeros((8, edges), F32)
    for c in range(0, entities, step):
        s = s_ref[c:c + step, :]
        hit = jnp.where(iota == tail_row - c, s, 0.0)
        first, second = log_ref[c:c + step, :128], log_ref[c:c + step, 128:]
        log = jnp.concatenate([first, first, second, second], axis=1)
        s = s + log
        s_ref[c:c + step, :] = s
        for k in range(0, step, 8):
            pos = pos + hit[k:k + 8, :]
            top = jnp.maximum(top, s[k:k + 8, :])
    positive = jnp.sum(pos, axis=0, keepdims=True)
    top = jnp.max(top, axis=0, keepdims=True)
    total = jnp.zeros((8, edges), F32)
    for c in range(0, entities, step):
        e = jnp.exp(s_ref[c:c + step, :] - top)
        s_ref[c:c + step, :] = e
        for k in range(0, step, 8):
            total = total + e[k:k + 8, :]
    total = jnp.sum(total, axis=0, keepdims=True)
    share = 1.0 / total
    for c in range(0, entities, step):
        p = s_ref[c:c + step, :] * share
        q_ref[c:c + step, :] = jnp.where(iota == tail_row - c, p - 1.0, p).astype(BF16)
    gap = jnp.log(total) + top - positive
    low = jnp.exp(-jnp.abs(gap))
    loss = jnp.maximum(gap, 0.0) + jnp.log(1.0 + low)
    miss = jnp.where(gap >= 0.0, 1.0, low) / (1.0 + low)
    return loss, miss


def live_row(count, edges):
    group = jnp.where(lax.broadcasted_iota(jnp.int32, (1, edges), 1) < edges // 2, 0, 1)
    return jnp.where(group < count, 1.0, 0.0)


HEADS, TAILS, RELS, NEGS, LIVE, EXTRA = 0, 1, 2, 3, 16, 32


def unpacked(block, width, kind, step):
    rows = block[width:width + EXTRA, :].astype(F32)
    k = (kind * 2 + step - 1) * 2
    return (rows[k:k + 1, :] * 256.0 + rows[k + 1:k + 2, :]).astype(jnp.int32)


def live_counts(block, width, step):
    k = LIVE + step - 1
    return block[width:width + EXTRA, :].astype(F32)[k:k + 1, :].astype(jnp.int32)


def split(x):
    high = x.astype(BF16)
    return high, (x - high.astype(F32)).astype(BF16)


def pack_kernel(emb_in, heads_in, tails_in, rels_in, negatives_in, live_in, block,
                heads, tails, rels, negatives, live_groups, rows, sems):
    width = emb_in.shape[0]
    pairs = ((heads_in, heads), (tails_in, tails), (rels_in, rels), (negatives_in, negatives), (live_in, live_groups),
             (emb_in, block.at[:width, :]))
    copies = [pltpu.make_async_copy(a, b, sems.at[k]) for k, (a, b) in enumerate(pairs)]
    for copy in copies:
        copy.start()
    for copy in copies[:5]:
        copy.wait()
    edges = heads.shape[1]
    half = edges // 2
    rows[...] = jnp.zeros(rows.shape, F32)
    for step in (1, 2):
        for kind, ref in ((HEADS, heads), (TAILS, tails), (RELS, rels)):
            k = (kind * 2 + step - 1) * 2
            row = ref[step:step + 1, :]
            rows[k:k + 1, :] = (row >> 8).astype(F32)
            rows[k + 1:k + 2, :] = (row & 255).astype(F32)
        k = (NEGS * 2 + step - 1) * 2
        for g in range(2):
            row = negatives[step, g:g + 1, :]
            rows[k:k + 1, g * half:(g + 1) * half] = (row >> 8).astype(F32)
            rows[k + 1:k + 2, g * half:(g + 1) * half] = (row & 255).astype(F32)
        k = LIVE + step - 1
        rows[k:k + 1, :] = jnp.broadcast_to(live_groups[:, step:step + 1], (1, edges)).astype(F32)
    block[width:width + EXTRA, :] = rows[...].astype(BF16)
    copies[5].wait()


def prepare_kernel(emb, rel, heads, tails, rels, negatives, live_groups, grad, sums, q1, q2, r1, r2, log1, log2, hot, hf, rf, qf, sf, qq, log):
    edges, entities = heads.shape[1], emb.shape[1]
    head_hot = one_hot(heads[0:1, :], entities)
    hf[...] = dot(emb[...], head_hot, NN)
    rf[...] = gather_relations(rel, rels[0:1, :], hot)
    make_query(hf, rf, qf)
    q = qf[...].astype(BF16)
    sf[...] = dot(emb[...], q, TN)
    log_counts([negatives[0, g:g + 1, :] for g in range(2)], entities, log)
    loss, miss = softmax_terms(sf, log, tails[0:1, :], qq)
    live = live_row(live_groups[:, 0:1], edges)
    scale = miss * live * (1.0 / 256.0)
    high, low = split(q.astype(F32) * scale)
    g = dot(high, qq[...], NT) + dot(low, qq[...], NT)
    hf[...] = dot(emb[...], qq[...], NN)
    head_grad(hf, rf, scale, qf)
    high, low = split(qf[...])
    grad[...] = g + dot(high, head_hot, NT) + dot(low, head_hot, NT)
    sums[0:1, :] = loss * live
    sums[1:2, :] = live
    for step, q_out, r_out, log_out in ((1, q1, r1, log1), (2, q2, r2, log2)):
        rf[...] = gather_relations(rel, rels[step:step + 1, :], hot)
        hf[...] = dot(emb[...], one_hot(heads[step:step + 1, :], entities), NN)
        make_query(hf, rf, qf)
        log_counts([negatives[step, g:g + 1, :] for g in range(2)], entities, log_out)
        r_out[...] = rf[...].astype(BF16)
        q_out[...] = qf[...].astype(BF16)


def choose_kernel(even, odd, out):
    out[...] = jnp.where(lax.axis_index("blk") & 1 == 0, even[...], odd[...])


def head_bucket(step, tail, q_in, r_in, log, heads, tails, live_groups, acc, hf, rf, qf, sf, qq):
    edges, (width, entities) = heads.shape[1], acc.shape
    sf[...] = dot(tail[:width, :], q_in[...], TN)
    loss, miss = softmax_terms(sf, log, tails[step:step + 1, :], qq)
    live = live_row(live_groups[:, step:step + 1], edges)
    hf[...] = dot(tail[:width, :], qq[...], NN)
    rf[...] = r_in[...].astype(F32)
    head_grad(hf, rf, miss * live * (1.0 / 256.0), qf)
    high, low = split(qf[...])
    head_hot = one_hot(heads[step:step + 1, :], entities)
    acc[...] += dot(high, head_hot, NT) + dot(low, head_hot, NT)
    return loss * live, live


def far_terms(step, rel, block, r_out, log_out, hot):
    width, entities = rel.shape[0], log_out.shape[0]
    r_out[...] = gather_relations(rel, unpacked(block, width, RELS, step), hot)
    log_counts(halves(unpacked(block, width, NEGS, step)), entities, log_out)


def tail_bucket(step, emb, block, rf, log, acc, hf, qf, sf, qq):
    (width, entities), edges = emb.shape, block.shape[1]
    hf[...] = dot(block[:width, :], one_hot(unpacked(block, width, HEADS, step), entities), NN)
    make_query(hf, rf, qf)
    q = qf[...].astype(BF16)
    sf[...] = dot(emb[...], q, TN)
    loss, miss = softmax_terms(sf, log, unpacked(block, width, TAILS, step), qq)
    scale = miss * live_row(live_counts(block, width, step), edges) * (1.0 / 256.0)
    high, low = split(q.astype(F32) * scale)
    acc[...] += dot(high, qq[...], NT) + dot(low, qq[...], NT)


def second_kernel(rel, prev2, next2, q2, r2, log2, heads, tails, live_groups, part, sums, grad, sums_out, far_r2, far_log2,
                  hot, hf, rf, qf, sf, qq, far):
    far_terms(2, rel, next2, far, far_log2, hot)
    far_r2[...] = far[...].astype(BF16)
    grad[...] = part[...]
    loss, live = head_bucket(2, prev2, q2, r2, log2, heads, tails, live_groups, grad, hf, rf, qf, sf, qq)
    sums_out[0:1, :] = sums[0:1, :] + loss
    sums_out[1:2, :] = sums[1:2, :] + live


def first_kernel(sibling, swapped, q1, r1, log1, heads, tails, live_groups, part, sums, grad, row,
                 hf, rf, qf, sf, qq, prev1):
    grad[...] = part[...]
    prev1[...] = jnp.where(lax.axis_index("blk") & 1 == 0, swapped[...], sibling[...])
    loss, live = head_bucket(1, prev1, q1, r1, log1, heads, tails, live_groups, grad, hf, rf, qf, sf, qq)
    loss_all = jnp.sum(sums[0:1, :] + loss, axis=1, keepdims=True)
    live_all = jnp.sum(sums[1:2, :] + live, axis=1, keepdims=True)
    lane = lax.broadcasted_iota(jnp.int32, row.shape, 1)
    row[...] = jnp.where(lane == 0, loss_all, jnp.where(lane == 1, live_all, 0.0))


def tails2_kernel(emb, next2, far_r2, far_log2, part, grad, hf, rf, qf, sf, qq):
    grad[...] = part[...]
    rf[...] = far_r2[...].astype(F32)
    tail_bucket(2, emb, next2, rf, far_log2, grad, hf, qf, sf, qq)


def tails1_kernel(rel, emb, sibling, swapped, part, row, core_row, grad, rows, hot, hf, rf, qf, sf, qq, acc, next1, log):
    next1[...] = jnp.where(lax.axis_index("blk") & 1 == 0, sibling[...], swapped[...])
    acc[...] = part[...]
    far_terms(1, rel, next1, rf, log, hot)
    tail_bucket(1, emb, next1, rf, log, acc, hf, qf, sf, qq)
    grad[...] = acc[...].astype(BF16)
    rows[...] = jnp.broadcast_to(row[0:1, :] + core_row[0:1, :], rows.shape)


def finish_kernel(own, other, rows, grad, mean):
    grad[...] = own[...].astype(F32) + other[...].astype(F32)
    total = jnp.sum(rows[...], axis=0, keepdims=True)
    mean[...] = total[:, 0:1] / total[:, 1:2]


def kernel(body, outs, scratch, flops, spaces, mib=48):
    return pl.pallas_call(
        body,
        out_shape=[jax.ShapeDtypeStruct(s, t) for s, t in outs],
        in_specs=[pl.BlockSpec(memory_space=m) for m in spaces],
        scratch_shapes=[pltpu.VMEM(*s) if isinstance(s, tuple) else s for s in scratch],
        compiler_params=pltpu.CompilerParams(vmem_limit_bytes=mib * 2**20),
        cost_estimate=pl.CostEstimate(flops=flops, bytes_accessed=4 * 2**20, transcendentals=0),
    )


def shifted(x, by):
    peers = lax.axis_size("blk")
    return lax.ppermute(x, "blk", [(i, (i + by) % peers) for i in range(peers)])


def exchanged(x):
    return lax.ppermute(x, "blk", [(i, i ^ 1) for i in range(lax.axis_size("blk"))])


def per_device(embeddings, relations, heads, tails, rels, negatives, live):
    edges = heads.shape[1]
    entities, width = embeddings.shape
    n_rel = relations.shape[0]
    blocks = lax.axis_size("blk")
    emb = embeddings.T
    rel = relations.T
    here = pltpu.VMEM
    big, grads, logs, rows_of = (width, edges), (width, entities), (entities, 256), (8, 128)
    work = [(big, F32), (big, F32), (big, F32), ((entities, edges), F32), ((entities, edges), BF16)]
    hot = ((n_rel, edges), BF16)
    raw = (heads, tails, rels, negatives, live.T)
    sent = ((width + EXTRA, edges), BF16)
    (block,) = kernel(
        pack_kernel, [sent],
        [(x.shape, x.dtype) for x in raw] + [((EXTRA, edges), F32), pltpu.SemaphoreType.DMA((len(raw) + 1,))],
        2 * 10**9, [pltpu.HBM] * (len(raw) + 1), 56,
    )(emb, *raw)
    prev2 = shifted(block, 2)
    next2 = shifted(block, -2)
    sibling = exchanged(block)
    part, sums, q1, q2, r1, r2, log1, log2 = kernel(
        prepare_kernel,
        [(grads, F32), ((8, edges), F32)] + [(big, BF16)] * 4 + [(logs, F32)] * 2,
        [hot] + work + [(logs, F32)], 20 * 10**9, [here] * 7)(emb, rel, *raw)
    (passed,) = kernel(choose_kernel, [sent], [], 10**6, [here] * 2)(next2, prev2)
    swapped = exchanged(passed)
    own_lists = (heads, tails, live.T)
    part, sums, far_r2, far_log2 = kernel(
        second_kernel, [(grads, F32), ((8, edges), F32), (big, BF16), (logs, F32)], [hot] + work + [(big, F32)],
        7 * 10**9, [here] * 11)(rel, prev2, next2, q2, r2, log2, *own_lists, part, sums)
    part, row = kernel(
        first_kernel, [(grads, F32), (rows_of, F32)], work + [sent], 2 * 10**9, [here] * 10,
    )(sibling, swapped, q1, r1, log1, *own_lists, part, sums)
    core_row = exchanged(row)
    (part,) = kernel(tails2_kernel, [(grads, F32)], work, 2 * 10**9, [here] * 5)(emb, next2, far_r2, far_log2, part)
    own, rows = kernel(
        tails1_kernel, [(grads, BF16), ((blocks, 128), F32)], [hot] + work + [(grads, F32), sent, (logs, F32)],
        3 * 10**9, [here] * 7,
    )(rel, emb, sibling, swapped, part, row, core_row)
    other = lax.ppermute(own, "rep", [(0, 1), (1, 0)])
    rows = lax.all_to_all(rows, ("blk", "rep"), 0, 0, tiled=True,
                          axis_index_groups=[[4 * i + 2 * k + r for i in range(blocks // 2) for r in (0, 1)] for k in (0, 1)])
    grad, mean = kernel(finish_kernel, [(grads, F32), ((1, 1), F32)], [], 10**6, [here] * 3)(own, other, rows)
    return grad.T, mean[0, 0]


def solution(mesh):
    placed = (
        P("blk", None),
        P(),
        P(None, ("blk", "rep")),
        P(None, ("blk", "rep")),
        P(None, ("blk", "rep")),
        P(None, ("blk", "rep"), None),
        P(None, ("blk", "rep")),
    )
    return jax.shard_map(
        per_device, mesh=mesh, in_specs=placed, out_specs=(P("blk", None), P()), check_vma=False
    )
```

```python
import jax
import jax.numpy as jnp
from jax import lax
from jax.experimental import pallas as pl
from jax.experimental.pallas import tpu as pltpu
from jax.sharding import PartitionSpec as P

STEPS = 3
F32 = jnp.float32
BF16 = jnp.bfloat16
NEVER = -1e30
TN = (((0,), (0,)), ((), ()))
NN = (((1,), (0,)), ((), ()))
NT = (((1,), (1,)), ((), ()))


def dot(a, b, dims):
    return lax.dot_general(a, b, dims, preferred_element_type=F32)


def one_hot(row, size):
    hit = lax.broadcasted_iota(jnp.int32, (size, row.shape[1]), 0) == row
    return jnp.where(hit, 1.0, 0.0).astype(BF16)


def gather_relations(rel_t, row, hot_ref):
    block = 256
    low = one_hot(row & (block - 1), block)
    high = row >> 8
    for j in range(rel_t.shape[1] // block):
        here = jnp.where(high == j, 1.0, 0.0).astype(BF16)
        hot_ref[j * block:(j + 1) * block, :] = low * here
    return dot(rel_t[...], hot_ref[...], NN)


def make_query(h_ref, r_ref, q_ref):
    half = h_ref.shape[0] // 2
    step = 40
    for c in range(0, half, step):
        re, im = slice(c, c + step), slice(half + c, half + c + step)
        h_re, h_im, r_re, r_im = h_ref[re, :], h_ref[im, :], r_ref[re, :], r_ref[im, :]
        q_ref[re, :] = h_re * r_re - h_im * r_im
        q_ref[im, :] = h_re * r_im + h_im * r_re


def head_grad(d_ref, r_ref, scale, out_ref):
    half = d_ref.shape[0] // 2
    step = 40
    for c in range(0, half, step):
        re, im = slice(c, c + step), slice(half + c, half + c + step)
        d_re, d_im, r_re, r_im = d_ref[re, :] * scale, d_ref[im, :] * scale, r_ref[re, :], r_ref[im, :]
        out_ref[re, :] = d_re * r_re + d_im * r_im
        out_ref[im, :] = d_im * r_re - d_re * r_im


def halves(row):
    half = row.shape[1] // 2
    return row[:, :half], row[:, half:]


def log_counts(neg_rows, entities, out_ref):
    for g, neg_row in enumerate(neg_rows):
        hot = one_hot(neg_row, entities)
        count = dot(hot, jnp.ones((neg_row.shape[1], 128), BF16), NN)
        out_ref[:, g * 128:(g + 1) * 128] = jnp.where(count > 0.5, jnp.log(jnp.maximum(count, 1.0)), NEVER)


def softmax_terms(s_ref, log_ref, tail_row, q_ref):
    entities, edges = s_ref.shape
    step = 32
    iota = lax.broadcasted_iota(jnp.int32, (step, edges), 0)
    top = jnp.full((8, edges), NEVER, F32)
    pos = jnp.zeros((8, edges), F32)
    for c in range(0, entities, step):
        s = s_ref[c:c + step, :]
        hit = jnp.where(iota == tail_row - c, s, 0.0)
        first, second = log_ref[c:c + step, :128], log_ref[c:c + step, 128:]
        log = jnp.concatenate([first, first, second, second], axis=1)
        s = s + log
        s_ref[c:c + step, :] = s
        for k in range(0, step, 8):
            pos = pos + hit[k:k + 8, :]
            top = jnp.maximum(top, s[k:k + 8, :])
    positive = jnp.sum(pos, axis=0, keepdims=True)
    top = jnp.max(top, axis=0, keepdims=True)
    total = jnp.zeros((8, edges), F32)
    for c in range(0, entities, step):
        e = jnp.exp(s_ref[c:c + step, :] - top)
        s_ref[c:c + step, :] = e
        for k in range(0, step, 8):
            total = total + e[k:k + 8, :]
    total = jnp.sum(total, axis=0, keepdims=True)
    share = 1.0 / total
    for c in range(0, entities, step):
        p = s_ref[c:c + step, :] * share
        q_ref[c:c + step, :] = jnp.where(iota == tail_row - c, p - 1.0, p).astype(BF16)
    gap = jnp.log(total) + top - positive
    low = jnp.exp(-jnp.abs(gap))
    loss = jnp.maximum(gap, 0.0) + jnp.log(1.0 + low)
    miss = jnp.where(gap >= 0.0, 1.0, low) / (1.0 + low)
    return loss, miss


def live_row(count, edges):
    group = jnp.where(lax.broadcasted_iota(jnp.int32, (1, edges), 1) < edges // 2, 0, 1)
    return jnp.where(group < count, 1.0, 0.0)


HEADS, TAILS, RELS, NEGS, LIVE, EXTRA = 0, 1, 2, 3, 16, 32


def unpacked(block, width, kind, step):
    rows = block[width:width + EXTRA, :].astype(F32)
    k = (kind * 2 + step - 1) * 2
    return (rows[k:k + 1, :] * 256.0 + rows[k + 1:k + 2, :]).astype(jnp.int32)


def live_counts(block, width, step):
    k = LIVE + step - 1
    return block[width:width + EXTRA, :].astype(F32)[k:k + 1, :].astype(jnp.int32)


def split(x):
    high = x.astype(BF16)
    return high, (x - high.astype(F32)).astype(BF16)


def pack_kernel(emb_in, heads_in, tails_in, rels_in, negatives_in, live_in, block,
                heads, tails, rels, negatives, live_groups, rows, sems):
    width = emb_in.shape[0]
    pairs = ((heads_in, heads), (tails_in, tails), (rels_in, rels), (negatives_in, negatives), (live_in, live_groups),
             (emb_in, block.at[:width, :]))
    copies = [pltpu.make_async_copy(a, b, sems.at[k]) for k, (a, b) in enumerate(pairs)]
    for copy in copies:
        copy.start()
    for copy in copies[:5]:
        copy.wait()
    edges = heads.shape[1]
    half = edges // 2
    rows[...] = jnp.zeros(rows.shape, F32)
    for step in (1, 2):
        for kind, ref in ((HEADS, heads), (TAILS, tails), (RELS, rels)):
            k = (kind * 2 + step - 1) * 2
            row = ref[step:step + 1, :]
            rows[k:k + 1, :] = (row >> 8).astype(F32)
            rows[k + 1:k + 2, :] = (row & 255).astype(F32)
        k = (NEGS * 2 + step - 1) * 2
        for g in range(2):
            row = negatives[step, g:g + 1, :]
            rows[k:k + 1, g * half:(g + 1) * half] = (row >> 8).astype(F32)
            rows[k + 1:k + 2, g * half:(g + 1) * half] = (row & 255).astype(F32)
        k = LIVE + step - 1
        rows[k:k + 1, :] = jnp.broadcast_to(live_groups[:, step:step + 1], (1, edges)).astype(F32)
    block[width:width + EXTRA, :] = rows[...].astype(BF16)
    copies[5].wait()


def prepare_kernel(emb, rel, heads, tails, rels, negatives, live_groups, grad, sums, q1, q2, r1, r2, log1, log2, hot, hf, rf, qf, sf, qq, log):
    edges, entities = heads.shape[1], emb.shape[1]
    head_hot = one_hot(heads[0:1, :], entities)
    hf[...] = dot(emb[...], head_hot, NN)
    rf[...] = gather_relations(rel, rels[0:1, :], hot)
    make_query(hf, rf, qf)
    q = qf[...].astype(BF16)
    sf[...] = dot(emb[...], q, TN)
    log_counts([negatives[0, g:g + 1, :] for g in range(2)], entities, log)
    loss, miss = softmax_terms(sf, log, tails[0:1, :], qq)
    live = live_row(live_groups[:, 0:1], edges)
    scale = miss * live * (1.0 / 256.0)
    high, low = split(q.astype(F32) * scale)
    g = dot(high, qq[...], NT) + dot(low, qq[...], NT)
    hf[...] = dot(emb[...], qq[...], NN)
    head_grad(hf, rf, scale, qf)
    high, low = split(qf[...])
    grad[...] = g + dot(high, head_hot, NT) + dot(low, head_hot, NT)
    sums[0:1, :] = loss * live
    sums[1:2, :] = live
    for step, q_out, r_out, log_out in ((1, q1, r1, log1), (2, q2, r2, log2)):
        rf[...] = gather_relations(rel, rels[step:step + 1, :], hot)
        hf[...] = dot(emb[...], one_hot(heads[step:step + 1, :], entities), NN)
        make_query(hf, rf, qf)
        log_counts([negatives[step, g:g + 1, :] for g in range(2)], entities, log_out)
        r_out[...] = rf[...].astype(BF16)
        q_out[...] = qf[...].astype(BF16)


def head_bucket(step, tail, q_in, r_in, log, heads, tails, live_groups, acc, hf, rf, qf, sf, qq):
    edges, (width, entities) = heads.shape[1], acc.shape
    sf[...] = dot(tail[:width, :], q_in[...], TN)
    loss, miss = softmax_terms(sf, log, tails[step:step + 1, :], qq)
    live = live_row(live_groups[:, step:step + 1], edges)
    hf[...] = dot(tail[:width, :], qq[...], NN)
    rf[...] = r_in[...].astype(F32)
    head_grad(hf, rf, miss * live * (1.0 / 256.0), qf)
    high, low = split(qf[...])
    head_hot = one_hot(heads[step:step + 1, :], entities)
    acc[...] += dot(high, head_hot, NT) + dot(low, head_hot, NT)
    return loss * live, live


def far_terms(step, rel, block, r_out, log_out, hot):
    width, entities = rel.shape[0], log_out.shape[0]
    r_out[...] = gather_relations(rel, unpacked(block, width, RELS, step), hot)
    log_counts(halves(unpacked(block, width, NEGS, step)), entities, log_out)


def tail_bucket(step, emb, block, rf, log, acc, hf, qf, sf, qq):
    (width, entities), edges = emb.shape, block.shape[1]
    hf[...] = dot(block[:width, :], one_hot(unpacked(block, width, HEADS, step), entities), NN)
    make_query(hf, rf, qf)
    q = qf[...].astype(BF16)
    sf[...] = dot(emb[...], q, TN)
    loss, miss = softmax_terms(sf, log, unpacked(block, width, TAILS, step), qq)
    scale = miss * live_row(live_counts(block, width, step), edges) * (1.0 / 256.0)
    high, low = split(q.astype(F32) * scale)
    acc[...] += dot(high, qq[...], NT) + dot(low, qq[...], NT)


def heads2_kernel(prev2, q2, r2, log2, heads, tails, live_groups, part, sums, grad, sums_out, hf, rf, qf, sf, qq):
    grad[...] = part[...]
    loss, live = head_bucket(2, prev2, q2, r2, log2, heads, tails, live_groups, grad, hf, rf, qf, sf, qq)
    sums_out[0:1, :] = sums[0:1, :] + loss
    sums_out[1:2, :] = sums[1:2, :] + live


def heads1_kernel(sibling, swapped, q1, r1, log1, heads, tails, live_groups, part, sums, grad, row,
                  hf, rf, qf, sf, qq, prev1):
    grad[...] = part[...]
    prev1[...] = jnp.where(lax.axis_index("blk") & 1 == 0, swapped[...], sibling[...])
    loss, live = head_bucket(1, prev1, q1, r1, log1, heads, tails, live_groups, grad, hf, rf, qf, sf, qq)
    loss_all = jnp.sum(sums[0:1, :] + loss, axis=1, keepdims=True)
    live_all = jnp.sum(sums[1:2, :] + live, axis=1, keepdims=True)
    lane = lax.broadcasted_iota(jnp.int32, row.shape, 1)
    row[...] = jnp.where(lane == 0, loss_all, jnp.where(lane == 1, live_all, 0.0))


def after_kernel(block, row, block_out):
    pass


def tails2_kernel(rel, emb, next2, part, grad, hot, hf, rf, qf, sf, qq, log):
    grad[...] = part[...]
    far_terms(2, rel, next2, rf, log, hot)
    tail_bucket(2, emb, next2, rf, log, grad, hf, qf, sf, qq)


def tails1_kernel(rel, emb, sibling, swapped, part, row, core_row, grad, rows, hot, hf, rf, qf, sf, qq, acc, next1, log):
    next1[...] = jnp.where(lax.axis_index("blk") & 1 == 0, sibling[...], swapped[...])
    acc[...] = part[...]
    far_terms(1, rel, next1, rf, log, hot)
    tail_bucket(1, emb, next1, rf, log, acc, hf, qf, sf, qq)
    grad[...] = acc[...].astype(BF16)
    rows[...] = jnp.broadcast_to(row[0:1, :] + core_row[0:1, :], rows.shape)


def finish_kernel(own, other, rows, grad, mean):
    grad[...] = own[...].astype(F32) + other[...].astype(F32)
    total = jnp.sum(rows[...], axis=0, keepdims=True)
    mean[...] = total[:, 0:1] / total[:, 1:2]


def kernel(body, outs, scratch, flops, spaces, mib=48, aliases={}):
    return pl.pallas_call(
        body,
        out_shape=[jax.ShapeDtypeStruct(s, t) for s, t in outs],
        in_specs=[pl.BlockSpec(memory_space=m) for m in spaces],
        input_output_aliases=aliases,
        scratch_shapes=[pltpu.VMEM(*s) if isinstance(s, tuple) else s for s in scratch],
        compiler_params=pltpu.CompilerParams(vmem_limit_bytes=mib * 2**20),
        cost_estimate=pl.CostEstimate(flops=flops, bytes_accessed=4 * 2**20, transcendentals=0),
    )


def shifted(x, by):
    peers = lax.axis_size("blk")
    return lax.ppermute(x, "blk", [(i, (i + by) % peers) for i in range(peers)])


def exchanged(x):
    return lax.ppermute(x, "blk", [(i, i ^ 1) for i in range(lax.axis_size("blk"))])


def per_device(embeddings, relations, heads, tails, rels, negatives, live):
    edges = heads.shape[1]
    entities, width = embeddings.shape
    n_rel = relations.shape[0]
    blocks = lax.axis_size("blk")
    emb = embeddings.T
    rel = relations.T
    here = pltpu.VMEM
    big, grads, logs, rows_of = (width, edges), (width, entities), (entities, 256), (8, 128)
    work = [(big, F32), (big, F32), (big, F32), ((entities, edges), F32), ((entities, edges), BF16)]
    hot = ((n_rel, edges), BF16)
    raw = (heads, tails, rels, negatives, live.T)
    sent = ((width + EXTRA, edges), BF16)
    (block,) = kernel(
        pack_kernel, [sent],
        [(x.shape, x.dtype) for x in raw] + [((EXTRA, edges), F32), pltpu.SemaphoreType.DMA((len(raw) + 1,))],
        2 * 10**9, [pltpu.HBM] * (len(raw) + 1), 56,
    )(emb, *raw)
    prev2 = shifted(block, 2)
    next2 = shifted(block, -2)
    sibling = exchanged(block)
    part, sums, q1, q2, r1, r2, log1, log2 = kernel(
        prepare_kernel,
        [(grads, F32), ((8, edges), F32)] + [(big, BF16)] * 4 + [(logs, F32)] * 2,
        [hot] + work + [(logs, F32)], 20 * 10**9, [here] * 7)(emb, rel, *raw)
    own_lists = (heads, tails, live.T)
    swapped_prev = exchanged(prev2)
    part, sums = kernel(heads2_kernel, [(grads, F32), ((8, edges), F32)], work, 8 * 10**9, [here] * 9)(
        prev2, q2, r2, log2, *own_lists, part, sums)
    part, row = kernel(heads1_kernel, [(grads, F32), (rows_of, F32)], work + [sent], 3 * 10**9, [here] * 10)(
        sibling, swapped_prev, q1, r1, log1, *own_lists, part, sums)
    core_row = exchanged(row)
    (next2,) = kernel(after_kernel, [sent], [], 10**6, [here] * 2, aliases={0: 0})(next2, row)
    swapped_next = exchanged(next2)
    (part,) = kernel(tails2_kernel, [(grads, F32)], [hot] + work + [(logs, F32)], 10 * 10**9, [here] * 4)(
        rel, emb, next2, part)
    own, rows = kernel(
        tails1_kernel, [(grads, BF16), ((blocks, 128), F32)], [hot] + work + [(grads, F32), sent, (logs, F32)],
        3 * 10**9, [here] * 7,
    )(rel, emb, sibling, swapped_next, part, row, core_row)
    other = lax.ppermute(own, "rep", [(0, 1), (1, 0)])
    rows = lax.all_to_all(rows, ("blk", "rep"), 0, 0, tiled=True,
                          axis_index_groups=[[4 * i + 2 * k + r for i in range(blocks // 2) for r in (0, 1)] for k in (0, 1)])
    grad, mean = kernel(finish_kernel, [(grads, F32), ((1, 1), F32)], [], 10**6, [here] * 3)(own, other, rows)
    return grad.T, mean[0, 0]


def solution(mesh):
    placed = (
        P("blk", None),
        P(),
        P(None, ("blk", "rep")),
        P(None, ("blk", "rep")),
        P(None, ("blk", "rep")),
        P(None, ("blk", "rep"), None),
        P(None, ("blk", "rep")),
    )
    return jax.shard_map(
        per_device, mesh=mesh, in_specs=placed, out_specs=(P("blk", None), P()), check_vma=False
    )
```

```python
import jax
import jax.numpy as jnp
from jax import lax
from jax.experimental import pallas as pl
from jax.experimental.pallas import tpu as pltpu
from jax.sharding import PartitionSpec as P

STEPS = 3
F32 = jnp.float32
BF16 = jnp.bfloat16
NEVER = -1e30
TN = (((0,), (0,)), ((), ()))
NN = (((1,), (0,)), ((), ()))
NT = (((1,), (1,)), ((), ()))


def dot(a, b, dims):
    return lax.dot_general(a, b, dims, preferred_element_type=F32)


def one_hot(row, size):
    hit = lax.broadcasted_iota(jnp.int32, (size, row.shape[1]), 0) == row
    return jnp.where(hit, 1.0, 0.0).astype(BF16)


def gather_relations(rel_t, row, hot_ref):
    block = 256
    low = one_hot(row & (block - 1), block)
    high = row >> 8
    for j in range(rel_t.shape[1] // block):
        here = jnp.where(high == j, 1.0, 0.0).astype(BF16)
        hot_ref[j * block:(j + 1) * block, :] = low * here
    return dot(rel_t[...], hot_ref[...], NN)


def make_query(h_ref, r_ref, q_ref):
    half = h_ref.shape[0] // 2
    step = 40
    for c in range(0, half, step):
        re, im = slice(c, c + step), slice(half + c, half + c + step)
        h_re, h_im, r_re, r_im = h_ref[re, :], h_ref[im, :], r_ref[re, :], r_ref[im, :]
        q_ref[re, :] = h_re * r_re - h_im * r_im
        q_ref[im, :] = h_re * r_im + h_im * r_re


def head_grad(d_ref, r_ref, scale, out_ref):
    half = d_ref.shape[0] // 2
    step = 40
    for c in range(0, half, step):
        re, im = slice(c, c + step), slice(half + c, half + c + step)
        d_re, d_im, r_re, r_im = d_ref[re, :] * scale, d_ref[im, :] * scale, r_ref[re, :], r_ref[im, :]
        out_ref[re, :] = d_re * r_re + d_im * r_im
        out_ref[im, :] = d_im * r_re - d_re * r_im


def halves(row):
    half = row.shape[1] // 2
    return row[:, :half], row[:, half:]


def log_counts(neg_rows, entities, out_ref):
    for g, neg_row in enumerate(neg_rows):
        hot = one_hot(neg_row, entities)
        count = dot(hot, jnp.ones((neg_row.shape[1], 128), BF16), NN)
        out_ref[:, g * 128:(g + 1) * 128] = jnp.where(count > 0.5, jnp.log(jnp.maximum(count, 1.0)), NEVER)


def softmax_terms(s_ref, log_ref, tail_row, q_ref):
    entities, edges = s_ref.shape
    step = 32
    iota = lax.broadcasted_iota(jnp.int32, (step, edges), 0)
    top = jnp.full((8, edges), NEVER, F32)
    pos = jnp.zeros((8, edges), F32)
    for c in range(0, entities, step):
        s = s_ref[c:c + step, :]
        hit = jnp.where(iota == tail_row - c, s, 0.0)
        first, second = log_ref[c:c + step, :128], log_ref[c:c + step, 128:]
        log = jnp.concatenate([first, first, second, second], axis=1)
        s = s + log
        s_ref[c:c + step, :] = s
        for k in range(0, step, 8):
            pos = pos + hit[k:k + 8, :]
            top = jnp.maximum(top, s[k:k + 8, :])
    positive = jnp.sum(pos, axis=0, keepdims=True)
    top = jnp.max(top, axis=0, keepdims=True)
    total = jnp.zeros((8, edges), F32)
    for c in range(0, entities, step):
        e = jnp.exp(s_ref[c:c + step, :] - top)
        s_ref[c:c + step, :] = e
        for k in range(0, step, 8):
            total = total + e[k:k + 8, :]
    total = jnp.sum(total, axis=0, keepdims=True)
    share = 1.0 / total
    for c in range(0, entities, step):
        p = s_ref[c:c + step, :] * share
        q_ref[c:c + step, :] = jnp.where(iota == tail_row - c, p - 1.0, p).astype(BF16)
    gap = jnp.log(total) + top - positive
    low = jnp.exp(-jnp.abs(gap))
    loss = jnp.maximum(gap, 0.0) + jnp.log(1.0 + low)
    miss = jnp.where(gap >= 0.0, 1.0, low) / (1.0 + low)
    return loss, miss


def live_row(count, edges):
    group = jnp.where(lax.broadcasted_iota(jnp.int32, (1, edges), 1) < edges // 2, 0, 1)
    return jnp.where(group < count, 1.0, 0.0)


HEADS, TAILS, RELS, NEGS, LIVE, EXTRA = 0, 1, 2, 3, 16, 32


def unpacked(block, width, kind, step):
    rows = block[width:width + EXTRA, :].astype(F32)
    k = (kind * 2 + step - 1) * 2
    return (rows[k:k + 1, :] * 256.0 + rows[k + 1:k + 2, :]).astype(jnp.int32)


def live_counts(block, width, step):
    k = LIVE + step - 1
    return block[width:width + EXTRA, :].astype(F32)[k:k + 1, :].astype(jnp.int32)


def split(x):
    high = x.astype(BF16)
    return high, (x - high.astype(F32)).astype(BF16)


def pack_kernel(emb_in, heads_in, tails_in, rels_in, negatives_in, live_in, block,
                heads, tails, rels, negatives, live_groups, rows, sems):
    width = emb_in.shape[0]
    pairs = ((heads_in, heads), (tails_in, tails), (rels_in, rels), (negatives_in, negatives), (live_in, live_groups),
             (emb_in, block.at[:width, :]))
    copies = [pltpu.make_async_copy(a, b, sems.at[k]) for k, (a, b) in enumerate(pairs)]
    for copy in copies:
        copy.start()
    for copy in copies[:5]:
        copy.wait()
    edges = heads.shape[1]
    half = edges // 2
    rows[...] = jnp.zeros(rows.shape, F32)
    for step in (1, 2):
        for kind, ref in ((HEADS, heads), (TAILS, tails), (RELS, rels)):
            k = (kind * 2 + step - 1) * 2
            row = ref[step:step + 1, :]
            rows[k:k + 1, :] = (row >> 8).astype(F32)
            rows[k + 1:k + 2, :] = (row & 255).astype(F32)
        k = (NEGS * 2 + step - 1) * 2
        for g in range(2):
            row = negatives[step, g:g + 1, :]
            rows[k:k + 1, g * half:(g + 1) * half] = (row >> 8).astype(F32)
            rows[k + 1:k + 2, g * half:(g + 1) * half] = (row & 255).astype(F32)
        k = LIVE + step - 1
        rows[k:k + 1, :] = jnp.broadcast_to(live_groups[:, step:step + 1], (1, edges)).astype(F32)
    block[width:width + EXTRA, :] = rows[...].astype(BF16)
    copies[5].wait()


def prepare_kernel(emb, rel, heads, tails, rels, negatives, live_groups, grad, sums, q1, q2, r1, r2, log1, log2, hot, hf, rf, qf, sf, qq, log):
    edges, entities = heads.shape[1], emb.shape[1]
    head_hot = one_hot(heads[0:1, :], entities)
    hf[...] = dot(emb[...], head_hot, NN)
    rf[...] = gather_relations(rel, rels[0:1, :], hot)
    make_query(hf, rf, qf)
    q = qf[...].astype(BF16)
    sf[...] = dot(emb[...], q, TN)
    log_counts([negatives[0, g:g + 1, :] for g in range(2)], entities, log)
    loss, miss = softmax_terms(sf, log, tails[0:1, :], qq)
    live = live_row(live_groups[:, 0:1], edges)
    scale = miss * live * (1.0 / 256.0)
    high, low = split(q.astype(F32) * scale)
    g = dot(high, qq[...], NT) + dot(low, qq[...], NT)
    hf[...] = dot(emb[...], qq[...], NN)
    head_grad(hf, rf, scale, qf)
    high, low = split(qf[...])
    grad[...] = g + dot(high, head_hot, NT) + dot(low, head_hot, NT)
    sums[0:1, :] = loss * live
    sums[1:2, :] = live
    for step, q_out, r_out, log_out in ((1, q1, r1, log1), (2, q2, r2, log2)):
        rf[...] = gather_relations(rel, rels[step:step + 1, :], hot)
        hf[...] = dot(emb[...], one_hot(heads[step:step + 1, :], entities), NN)
        make_query(hf, rf, qf)
        log_counts([negatives[step, g:g + 1, :] for g in range(2)], entities, log_out)
        r_out[...] = rf[...].astype(BF16)
        q_out[...] = qf[...].astype(BF16)


def head_bucket(step, tail, q_in, r_in, log, heads, tails, live_groups, acc, hf, rf, qf, sf, qq):
    edges, (width, entities) = heads.shape[1], acc.shape
    sf[...] = dot(tail[:width, :], q_in[...], TN)
    loss, miss = softmax_terms(sf, log, tails[step:step + 1, :], qq)
    live = live_row(live_groups[:, step:step + 1], edges)
    hf[...] = dot(tail[:width, :], qq[...], NN)
    rf[...] = r_in[...].astype(F32)
    head_grad(hf, rf, miss * live * (1.0 / 256.0), qf)
    high, low = split(qf[...])
    head_hot = one_hot(heads[step:step + 1, :], entities)
    acc[...] += dot(high, head_hot, NT) + dot(low, head_hot, NT)
    return loss * live, live


def far_terms(step, rel, block, r_out, log_out, hot):
    width, entities = rel.shape[0], log_out.shape[0]
    r_out[...] = gather_relations(rel, unpacked(block, width, RELS, step), hot)
    log_counts(halves(unpacked(block, width, NEGS, step)), entities, log_out)


def tail_bucket(step, emb, block, rf, log, acc, hf, qf, sf, qq):
    (width, entities), edges = emb.shape, block.shape[1]
    hf[...] = dot(block[:width, :], one_hot(unpacked(block, width, HEADS, step), entities), NN)
    make_query(hf, rf, qf)
    q = qf[...].astype(BF16)
    sf[...] = dot(emb[...], q, TN)
    loss, miss = softmax_terms(sf, log, unpacked(block, width, TAILS, step), qq)
    scale = miss * live_row(live_counts(block, width, step), edges) * (1.0 / 256.0)
    high, low = split(q.astype(F32) * scale)
    acc[...] += dot(high, qq[...], NT) + dot(low, qq[...], NT)


def heads2_kernel(prev2, q2, r2, log2, heads, tails, live_groups, part, sums, grad, sums_out, hf, rf, qf, sf, qq):
    grad[...] = part[...]
    loss, live = head_bucket(2, prev2, q2, r2, log2, heads, tails, live_groups, grad, hf, rf, qf, sf, qq)
    sums_out[0:1, :] = sums[0:1, :] + loss
    sums_out[1:2, :] = sums[1:2, :] + live


def heads1_kernel(sibling, swapped, q1, r1, log1, heads, tails, live_groups, part, sums, grad, row,
                  hf, rf, qf, sf, qq, prev1):
    grad[...] = part[...]
    prev1[...] = jnp.where(lax.axis_index("blk") & 1 == 0, swapped[...], sibling[:prev1.shape[0], :])
    loss, live = head_bucket(1, prev1, q1, r1, log1, heads, tails, live_groups, grad, hf, rf, qf, sf, qq)
    loss_all = jnp.sum(sums[0:1, :] + loss, axis=1, keepdims=True)
    live_all = jnp.sum(sums[1:2, :] + live, axis=1, keepdims=True)
    lane = lax.broadcasted_iota(jnp.int32, row.shape, 1)
    row[...] = jnp.where(lane == 0, loss_all, jnp.where(lane == 1, live_all, 0.0))


def after_kernel(block, row, block_out):
    pass


def tails2_kernel(rel, emb, next2, part, grad, hot, hf, rf, qf, sf, qq, log):
    grad[...] = part[...]
    far_terms(2, rel, next2, rf, log, hot)
    tail_bucket(2, emb, next2, rf, log, grad, hf, qf, sf, qq)


def tails1_kernel(rel, emb, sibling, swapped, part, row, core_row, grad, rows, hot, hf, rf, qf, sf, qq, acc, next1, log):
    next1[...] = jnp.where(lax.axis_index("blk") & 1 == 0, sibling[...], swapped[...])
    acc[...] = part[...]
    far_terms(1, rel, next1, rf, log, hot)
    tail_bucket(1, emb, next1, rf, log, acc, hf, qf, sf, qq)
    grad[...] = acc[...].astype(BF16)
    rows[...] = jnp.broadcast_to(row[0:1, :] + core_row[0:1, :], rows.shape)


def finish_kernel(own, other, rows, grad, mean):
    grad[...] = own[...].astype(F32) + other[...].astype(F32)
    total = jnp.sum(rows[...], axis=0, keepdims=True)
    mean[...] = total[:, 0:1] / total[:, 1:2]


def kernel(body, outs, scratch, flops, spaces, mib=48, aliases={}):
    return pl.pallas_call(
        body,
        out_shape=[jax.ShapeDtypeStruct(s, t) for s, t in outs],
        in_specs=[pl.BlockSpec(memory_space=m) for m in spaces],
        input_output_aliases=aliases,
        scratch_shapes=[pltpu.VMEM(*s) if isinstance(s, tuple) else s for s in scratch],
        compiler_params=pltpu.CompilerParams(vmem_limit_bytes=mib * 2**20),
        cost_estimate=pl.CostEstimate(flops=flops, bytes_accessed=4 * 2**20, transcendentals=0),
    )


def shifted(x, by):
    peers = lax.axis_size("blk")
    return lax.ppermute(x, "blk", [(i, (i + by) % peers) for i in range(peers)])


def exchanged(x):
    return lax.ppermute(x, "blk", [(i, i ^ 1) for i in range(lax.axis_size("blk"))])


def per_device(embeddings, relations, heads, tails, rels, negatives, live):
    edges = heads.shape[1]
    entities, width = embeddings.shape
    n_rel = relations.shape[0]
    blocks = lax.axis_size("blk")
    emb = embeddings.T
    rel = relations.T
    here = pltpu.VMEM
    big, grads, logs, rows_of = (width, edges), (width, entities), (entities, 256), (8, 128)
    work = [(big, F32), (big, F32), (big, F32), ((entities, edges), F32), ((entities, edges), BF16)]
    hot = ((n_rel, edges), BF16)
    raw = (heads, tails, rels, negatives, live.T)
    sent = ((width + EXTRA, edges), BF16)
    (block,) = kernel(
        pack_kernel, [sent],
        [(x.shape, x.dtype) for x in raw] + [((EXTRA, edges), F32), pltpu.SemaphoreType.DMA((len(raw) + 1,))],
        2 * 10**9, [pltpu.HBM] * (len(raw) + 1), 56,
    )(emb, *raw)
    prev2 = shifted(emb, 2)
    next2 = shifted(block, -2)
    sibling = exchanged(block)
    part, sums, q1, q2, r1, r2, log1, log2 = kernel(
        prepare_kernel,
        [(grads, F32), ((8, edges), F32)] + [(big, BF16)] * 4 + [(logs, F32)] * 2,
        [hot] + work + [(logs, F32)], 20 * 10**9, [here] * 7)(emb, rel, *raw)
    own_lists = (heads, tails, live.T)
    swapped_prev = exchanged(prev2)
    part, sums = kernel(heads2_kernel, [(grads, F32), ((8, edges), F32)], work, 8 * 10**9, [here] * 9)(
        prev2, q2, r2, log2, *own_lists, part, sums)
    part, row = kernel(heads1_kernel, [(grads, F32), (rows_of, F32)], work + [(big, BF16)], 3 * 10**9, [here] * 10)(
        sibling, swapped_prev, q1, r1, log1, *own_lists, part, sums)
    core_row = exchanged(row)
    (next2,) = kernel(after_kernel, [sent], [], 10**6, [here] * 2, aliases={0: 0})(next2, row)
    swapped_next = exchanged(next2)
    (part,) = kernel(tails2_kernel, [(grads, F32)], [hot] + work + [(logs, F32)], 10 * 10**9, [here] * 4)(
        rel, emb, next2, part)
    own, rows = kernel(
        tails1_kernel, [(grads, BF16), ((blocks, 128), F32)], [hot] + work + [(grads, F32), sent, (logs, F32)],
        3 * 10**9, [here] * 7,
    )(rel, emb, sibling, swapped_next, part, row, core_row)
    other = lax.ppermute(own, "rep", [(0, 1), (1, 0)])
    rows = lax.all_to_all(rows, ("blk", "rep"), 0, 0, tiled=True,
                          axis_index_groups=[[4 * i + 2 * k + r for i in range(blocks // 2) for r in (0, 1)] for k in (0, 1)])
    grad, mean = kernel(finish_kernel, [(grads, F32), ((1, 1), F32)], [], 10**6, [here] * 3)(own, other, rows)
    return grad.T, mean[0, 0]


def solution(mesh):
    placed = (
        P("blk", None),
        P(),
        P(None, ("blk", "rep")),
        P(None, ("blk", "rep")),
        P(None, ("blk", "rep")),
        P(None, ("blk", "rep"), None),
        P(None, ("blk", "rep")),
    )
    return jax.shard_map(
        per_device, mesh=mesh, in_specs=placed, out_specs=(P("blk", None), P()), check_vma=False
    )
```

```python
import jax
import jax.numpy as jnp
from jax import lax
from jax.experimental import pallas as pl
from jax.experimental.pallas import tpu as pltpu
from jax.sharding import PartitionSpec as P

STEPS = 3
F32 = jnp.float32
BF16 = jnp.bfloat16
NEVER = -1e30
TN = (((0,), (0,)), ((), ()))
NN = (((1,), (0,)), ((), ()))
NT = (((1,), (1,)), ((), ()))


def dot(a, b, dims):
    return lax.dot_general(a, b, dims, preferred_element_type=F32)


def one_hot(row, size):
    hit = lax.broadcasted_iota(jnp.int32, (size, row.shape[1]), 0) == row
    return jnp.where(hit, 1.0, 0.0).astype(BF16)


def gather_relations(rel_t, row, hot_ref):
    block = 256
    low = one_hot(row & (block - 1), block)
    high = row >> 8
    for j in range(rel_t.shape[1] // block):
        here = jnp.where(high == j, 1.0, 0.0).astype(BF16)
        hot_ref[j * block:(j + 1) * block, :] = low * here
    return dot(rel_t[...], hot_ref[...], NN)


def make_query(h_ref, r_ref, q_ref):
    half = h_ref.shape[0] // 2
    step = 40
    for c in range(0, half, step):
        re, im = slice(c, c + step), slice(half + c, half + c + step)
        h_re, h_im, r_re, r_im = h_ref[re, :], h_ref[im, :], r_ref[re, :], r_ref[im, :]
        q_ref[re, :] = h_re * r_re - h_im * r_im
        q_ref[im, :] = h_re * r_im + h_im * r_re


def head_grad(d_ref, r_ref, scale, out_ref):
    half = d_ref.shape[0] // 2
    step = 40
    for c in range(0, half, step):
        re, im = slice(c, c + step), slice(half + c, half + c + step)
        d_re, d_im, r_re, r_im = d_ref[re, :] * scale, d_ref[im, :] * scale, r_ref[re, :], r_ref[im, :]
        out_ref[re, :] = d_re * r_re + d_im * r_im
        out_ref[im, :] = d_im * r_re - d_re * r_im


def halves(row):
    half = row.shape[1] // 2
    return row[:, :half], row[:, half:]


def log_counts(neg_rows, entities, out_ref):
    for g, neg_row in enumerate(neg_rows):
        hot = one_hot(neg_row, entities)
        count = dot(hot, jnp.ones((neg_row.shape[1], 128), BF16), NN)
        out_ref[:, g * 128:(g + 1) * 128] = jnp.where(count > 0.5, jnp.log(jnp.maximum(count, 1.0)), NEVER)


def softmax_terms(s_ref, log_ref, tail_row, q_ref):
    entities, edges = s_ref.shape
    step = 32
    iota = lax.broadcasted_iota(jnp.int32, (step, edges), 0)
    top = jnp.full((8, edges), NEVER, F32)
    pos = jnp.zeros((8, edges), F32)
    for c in range(0, entities, step):
        s = s_ref[c:c + step, :]
        hit = jnp.where(iota == tail_row - c, s, 0.0)
        first, second = log_ref[c:c + step, :128], log_ref[c:c + step, 128:]
        log = jnp.concatenate([first, first, second, second], axis=1)
        s = s + log
        s_ref[c:c + step, :] = s
        for k in range(0, step, 8):
            pos = pos + hit[k:k + 8, :]
            top = jnp.maximum(top, s[k:k + 8, :])
    positive = jnp.sum(pos, axis=0, keepdims=True)
    top = jnp.max(top, axis=0, keepdims=True)
    total = jnp.zeros((8, edges), F32)
    for c in range(0, entities, step):
        e = jnp.exp(s_ref[c:c + step, :] - top)
        s_ref[c:c + step, :] = e
        for k in range(0, step, 8):
            total = total + e[k:k + 8, :]
    total = jnp.sum(total, axis=0, keepdims=True)
    share = 1.0 / total
    for c in range(0, entities, step):
        p = s_ref[c:c + step, :] * share
        q_ref[c:c + step, :] = jnp.where(iota == tail_row - c, p - 1.0, p).astype(BF16)
    gap = jnp.log(total) + top - positive
    low = jnp.exp(-jnp.abs(gap))
    loss = jnp.maximum(gap, 0.0) + jnp.log(1.0 + low)
    miss = jnp.where(gap >= 0.0, 1.0, low) / (1.0 + low)
    return loss, miss


def live_row(count, edges):
    group = jnp.where(lax.broadcasted_iota(jnp.int32, (1, edges), 1) < edges // 2, 0, 1)
    return jnp.where(group < count, 1.0, 0.0)


HEADS, TAILS, RELS, NEGS, LIVE, EXTRA = 0, 1, 2, 3, 16, 32


def unpacked(block, width, kind, step):
    rows = block[width:width + EXTRA, :].astype(F32)
    k = (kind * 2 + step - 1) * 2
    return (rows[k:k + 1, :] * 256.0 + rows[k + 1:k + 2, :]).astype(jnp.int32)


def live_counts(block, width, step):
    k = LIVE + step - 1
    return block[width:width + EXTRA, :].astype(F32)[k:k + 1, :].astype(jnp.int32)


def split(x):
    high = x.astype(BF16)
    return high, (x - high.astype(F32)).astype(BF16)


def pack_kernel(emb_in, heads_in, tails_in, rels_in, negatives_in, live_in, block,
                heads, tails, rels, negatives, live_groups, rows, packed, sems):
    width = emb_in.shape[0]
    pairs = ((heads_in, heads), (tails_in, tails), (rels_in, rels), (negatives_in, negatives), (live_in, live_groups),
             (emb_in, block.at[:width, :]))
    copies = [pltpu.make_async_copy(a, b, sems.at[k]) for k, (a, b) in enumerate(pairs)]
    for copy in copies:
        copy.start()
    for copy in copies[:5]:
        copy.wait()
    edges = heads.shape[1]
    half = edges // 2
    rows[...] = jnp.zeros(rows.shape, F32)
    for step in (1, 2):
        for kind, ref in ((HEADS, heads), (TAILS, tails), (RELS, rels)):
            k = (kind * 2 + step - 1) * 2
            row = ref[step:step + 1, :]
            rows[k:k + 1, :] = (row >> 8).astype(F32)
            rows[k + 1:k + 2, :] = (row & 255).astype(F32)
        k = (NEGS * 2 + step - 1) * 2
        for g in range(2):
            row = negatives[step, g:g + 1, :]
            rows[k:k + 1, g * half:(g + 1) * half] = (row >> 8).astype(F32)
            rows[k + 1:k + 2, g * half:(g + 1) * half] = (row & 255).astype(F32)
        k = LIVE + step - 1
        rows[k:k + 1, :] = jnp.broadcast_to(live_groups[:, step:step + 1], (1, edges)).astype(F32)
    packed[...] = rows[...].astype(BF16)
    last = pltpu.make_async_copy(packed, block.at[width:width + EXTRA, :], sems.at[6])
    last.start()
    copies[5].wait()
    last.wait()


def prepare_kernel(emb, rel, heads, tails, rels, negatives, live_groups, grad, sums, q1, q2, r1, r2, log1, log2, hot, hf, rf, qf, sf, qq, log):
    edges, entities = heads.shape[1], emb.shape[1]
    head_hot = one_hot(heads[0:1, :], entities)
    hf[...] = dot(emb[...], head_hot, NN)
    rf[...] = gather_relations(rel, rels[0:1, :], hot)
    make_query(hf, rf, qf)
    q = qf[...].astype(BF16)
    sf[...] = dot(emb[...], q, TN)
    log_counts([negatives[0, g:g + 1, :] for g in range(2)], entities, log)
    loss, miss = softmax_terms(sf, log, tails[0:1, :], qq)
    live = live_row(live_groups[:, 0:1], edges)
    scale = miss * live * (1.0 / 256.0)
    high, low = split(q.astype(F32) * scale)
    g = dot(high, qq[...], NT) + dot(low, qq[...], NT)
    hf[...] = dot(emb[...], qq[...], NN)
    head_grad(hf, rf, scale, qf)
    high, low = split(qf[...])
    grad[...] = g + dot(high, head_hot, NT) + dot(low, head_hot, NT)
    sums[0:1, :] = loss * live
    sums[1:2, :] = live
    for step, q_out, r_out, log_out in ((1, q1, r1, log1), (2, q2, r2, log2)):
        rf[...] = gather_relations(rel, rels[step:step + 1, :], hot)
        hf[...] = dot(emb[...], one_hot(heads[step:step + 1, :], entities), NN)
        make_query(hf, rf, qf)
        log_counts([negatives[step, g:g + 1, :] for g in range(2)], entities, log_out)
        r_out[...] = rf[...].astype(BF16)
        q_out[...] = qf[...].astype(BF16)


def head_bucket(step, tail, q_in, r_in, log, heads, tails, live_groups, acc, hf, rf, qf, sf, qq):
    edges, (width, entities) = heads.shape[1], acc.shape
    sf[...] = dot(tail[:width, :], q_in[...], TN)
    loss, miss = softmax_terms(sf, log, tails[step:step + 1, :], qq)
    live = live_row(live_groups[:, step:step + 1], edges)
    hf[...] = dot(tail[:width, :], qq[...], NN)
    rf[...] = r_in[...].astype(F32)
    head_grad(hf, rf, miss * live * (1.0 / 256.0), qf)
    high, low = split(qf[...])
    head_hot = one_hot(heads[step:step + 1, :], entities)
    acc[...] += dot(high, head_hot, NT) + dot(low, head_hot, NT)
    return loss * live, live


def far_terms(step, rel, block, r_out, log_out, hot):
    width, entities = rel.shape[0], log_out.shape[0]
    r_out[...] = gather_relations(rel, unpacked(block, width, RELS, step), hot)
    log_counts(halves(unpacked(block, width, NEGS, step)), entities, log_out)


def tail_bucket(step, emb, block, rf, log, acc, hf, qf, sf, qq):
    (width, entities), edges = emb.shape, block.shape[1]
    hf[...] = dot(block[:width, :], one_hot(unpacked(block, width, HEADS, step), entities), NN)
    make_query(hf, rf, qf)
    q = qf[...].astype(BF16)
    sf[...] = dot(emb[...], q, TN)
    loss, miss = softmax_terms(sf, log, unpacked(block, width, TAILS, step), qq)
    scale = miss * live_row(live_counts(block, width, step), edges) * (1.0 / 256.0)
    high, low = split(q.astype(F32) * scale)
    acc[...] += dot(high, qq[...], NT) + dot(low, qq[...], NT)


def heads2_kernel(prev2, q2, r2, log2, heads, tails, live_groups, part, sums, grad, sums_out, hf, rf, qf, sf, qq):
    grad[...] = part[...]
    loss, live = head_bucket(2, prev2, q2, r2, log2, heads, tails, live_groups, grad, hf, rf, qf, sf, qq)
    sums_out[0:1, :] = sums[0:1, :] + loss
    sums_out[1:2, :] = sums[1:2, :] + live


def heads1_kernel(sibling, swapped, q1, r1, log1, heads, tails, live_groups, part, sums, grad, row,
                  hf, rf, qf, sf, qq, prev1):
    grad[...] = part[...]
    prev1[...] = jnp.where(lax.axis_index("blk") & 1 == 0, swapped[...], sibling[:prev1.shape[0], :])
    loss, live = head_bucket(1, prev1, q1, r1, log1, heads, tails, live_groups, grad, hf, rf, qf, sf, qq)
    loss_all = jnp.sum(sums[0:1, :] + loss, axis=1, keepdims=True)
    live_all = jnp.sum(sums[1:2, :] + live, axis=1, keepdims=True)
    lane = lax.broadcasted_iota(jnp.int32, row.shape, 1)
    row[...] = jnp.where(lane == 0, loss_all, jnp.where(lane == 1, live_all, 0.0))


def after_kernel(block, row, block_out):
    pass


def tails2_kernel(rel, emb, next2, part, grad, hot, hf, rf, qf, sf, qq, log):
    grad[...] = part[...]
    far_terms(2, rel, next2, rf, log, hot)
    tail_bucket(2, emb, next2, rf, log, grad, hf, qf, sf, qq)


def tails1_kernel(rel, emb, sibling, swapped, part, row, grad, hot, hf, rf, qf, sf, qq, acc, next1, log):
    next1[...] = jnp.where(lax.axis_index("blk") & 1 == 0, sibling[...], swapped[...])
    acc[...] = part[...]
    far_terms(1, rel, next1, rf, log, hot)
    tail_bucket(1, emb, next1, rf, log, acc, hf, qf, sf, qq)
    grad[...] = acc[...].astype(BF16)


def add_kernel(row, other, out):
    out[...] = row[...] + other[...]


def rows_kernel(own, row, other, own_out, rows):
    rows[...] = jnp.broadcast_to(row[0:1, :] + other[0:1, :], rows.shape)


def finish_kernel(own, other, rows, grad, mean):
    grad[...] = own[...].astype(F32) + other[...].astype(F32)
    total = jnp.sum(rows[...], axis=0, keepdims=True)
    mean[...] = total[:, 0:1] / total[:, 1:2]


def kernel(body, outs, scratch, flops, spaces, mib=48, aliases={}, out_space=pltpu.VMEM):
    return pl.pallas_call(
        body,
        out_shape=[jax.ShapeDtypeStruct(s, t) for s, t in outs],
        in_specs=[pl.BlockSpec(memory_space=m) for m in spaces],
        out_specs=[pl.BlockSpec(memory_space=out_space)] * len(outs),
        input_output_aliases=aliases,
        scratch_shapes=[pltpu.VMEM(*s) if isinstance(s, tuple) else s for s in scratch],
        compiler_params=pltpu.CompilerParams(vmem_limit_bytes=mib * 2**20),
        cost_estimate=pl.CostEstimate(flops=flops, bytes_accessed=4 * 2**20, transcendentals=0),
    )


def shifted(x, by):
    peers = lax.axis_size("blk")
    return lax.ppermute(x, "blk", [(i, (i + by) % peers) for i in range(peers)])


def exchanged(x):
    return lax.ppermute(x, "blk", [(i, i ^ 1) for i in range(lax.axis_size("blk"))])


def per_device(embeddings, relations, heads, tails, rels, negatives, live):
    edges = heads.shape[1]
    entities, width = embeddings.shape
    n_rel = relations.shape[0]
    blocks = lax.axis_size("blk")
    emb = embeddings.T
    rel = relations.T
    here = pltpu.VMEM
    big, grads, logs, rows_of = (width, edges), (width, entities), (entities, 256), (8, 128)
    work = [(big, F32), (big, F32), (big, F32), ((entities, edges), F32), ((entities, edges), BF16)]
    hot = ((n_rel, edges), BF16)
    raw = (heads, tails, rels, negatives, live.T)
    sent = ((width + EXTRA, edges), BF16)
    (block,) = kernel(
        pack_kernel, [sent],
        [(x.shape, x.dtype) for x in raw] + [((EXTRA, edges), F32), ((EXTRA, edges), BF16), pltpu.SemaphoreType.DMA((len(raw) + 2,))],
        2 * 10**9, [pltpu.HBM] * (len(raw) + 1), 56, out_space=pltpu.HBM,
    )(emb, *raw)
    prev2 = shifted(emb, 2)
    next2 = shifted(block, -2)
    sibling = exchanged(block)
    part, sums, q1, q2, r1, r2, log1, log2 = kernel(
        prepare_kernel,
        [(grads, F32), ((8, edges), F32)] + [(big, BF16)] * 4 + [(logs, F32)] * 2,
        [hot] + work + [(logs, F32)], 20 * 10**9, [here] * 7)(emb, rel, *raw)
    own_lists = (heads, tails, live.T)
    swapped_prev = exchanged(prev2)
    part, sums = kernel(heads2_kernel, [(grads, F32), ((8, edges), F32)], work, 8 * 10**9, [here] * 9)(
        prev2, q2, r2, log2, *own_lists, part, sums)
    part, row = kernel(heads1_kernel, [(grads, F32), (rows_of, F32)], work + [(big, BF16)], 3 * 10**9, [here] * 10)(
        sibling, swapped_prev, q1, r1, log1, *own_lists, part, sums)
    core_row = exchanged(row)
    (next2,) = kernel(after_kernel, [sent], [], 10**6, [here] * 2, aliases={0: 0})(next2, row)
    swapped_next = exchanged(next2)
    (part,) = kernel(tails2_kernel, [(grads, F32)], [hot] + work + [(logs, F32)], 10 * 10**9, [here] * 4)(
        rel, emb, next2, part)
    (row,) = kernel(add_kernel, [(rows_of, F32)], [], 10**6, [here] * 2)(row, core_row)
    rep_row = lax.ppermute(row, "rep", [(0, 1), (1, 0)])
    (own,) = kernel(
        tails1_kernel, [(grads, BF16)], [hot] + work + [(grads, F32), sent, (logs, F32)], 10 * 10**9, [here] * 6,
    )(rel, emb, sibling, swapped_next, part, row)
    own, rows = kernel(rows_kernel, [(grads, BF16), ((blocks // 2, 128), F32)], [], 10**6, [here] * 3, aliases={0: 0})(
        own, row, rep_row)
    other = lax.ppermute(own, "rep", [(0, 1), (1, 0)])
    rows = lax.all_to_all(rows, "blk", 0, 0, tiled=True,
                          axis_index_groups=[[k + 2 * i for i in range(blocks // 2)] for k in (0, 1)])
    grad, mean = kernel(finish_kernel, [(grads, F32), ((1, 1), F32)], [], 10**6, [here] * 3)(own, other, rows)
    return grad.T, mean[0, 0]


def solution(mesh):
    placed = (
        P("blk", None),
        P(),
        P(None, ("blk", "rep")),
        P(None, ("blk", "rep")),
        P(None, ("blk", "rep")),
        P(None, ("blk", "rep"), None),
        P(None, ("blk", "rep")),
    )
    return jax.shard_map(
        per_device, mesh=mesh, in_specs=placed, out_specs=(P("blk", None), P()), check_vma=False
    )
```

```python
import jax
import jax.numpy as jnp
from jax import lax
from jax.experimental import pallas as pl
from jax.experimental.pallas import tpu as pltpu
from jax.sharding import PartitionSpec as P

STEPS = 3
F32 = jnp.float32
BF16 = jnp.bfloat16
NEVER = -1e30
TN = (((0,), (0,)), ((), ()))
NN = (((1,), (0,)), ((), ()))
NT = (((1,), (1,)), ((), ()))


def dot(a, b, dims):
    return lax.dot_general(a, b, dims, preferred_element_type=F32)


def one_hot(row, size):
    hit = lax.broadcasted_iota(jnp.int32, (size, row.shape[1]), 0) == row
    return jnp.where(hit, 1.0, 0.0).astype(BF16)


def gather_relations(rel_t, row, hot_ref):
    block = 256
    low = one_hot(row & (block - 1), block)
    high = row >> 8
    for j in range(rel_t.shape[1] // block):
        here = jnp.where(high == j, 1.0, 0.0).astype(BF16)
        hot_ref[j * block:(j + 1) * block, :] = low * here
    return dot(rel_t[...], hot_ref[...], NN)


def make_query(h_ref, r_ref, q_ref):
    half = h_ref.shape[0] // 2
    step = 40
    for c in range(0, half, step):
        re, im = slice(c, c + step), slice(half + c, half + c + step)
        h_re, h_im, r_re, r_im = h_ref[re, :], h_ref[im, :], r_ref[re, :], r_ref[im, :]
        q_ref[re, :] = h_re * r_re - h_im * r_im
        q_ref[im, :] = h_re * r_im + h_im * r_re


def head_grad(d_ref, r_ref, scale, out_ref):
    half = d_ref.shape[0] // 2
    step = 40
    for c in range(0, half, step):
        re, im = slice(c, c + step), slice(half + c, half + c + step)
        d_re, d_im, r_re, r_im = d_ref[re, :] * scale, d_ref[im, :] * scale, r_ref[re, :], r_ref[im, :]
        out_ref[re, :] = d_re * r_re + d_im * r_im
        out_ref[im, :] = d_im * r_re - d_re * r_im


def halves(row):
    half = row.shape[1] // 2
    return row[:, :half], row[:, half:]


def log_counts(neg_rows, entities, out_ref):
    for g, neg_row in enumerate(neg_rows):
        hot = one_hot(neg_row, entities)
        count = dot(hot, jnp.ones((neg_row.shape[1], 128), BF16), NN)
        out_ref[:, g * 128:(g + 1) * 128] = jnp.where(count > 0.5, jnp.log(jnp.maximum(count, 1.0)), NEVER)


def softmax_terms(s_ref, log_ref, tail_row, q_ref):
    entities, edges = s_ref.shape
    step = 32
    iota = lax.broadcasted_iota(jnp.int32, (step, edges), 0)
    top = jnp.full((8, edges), NEVER, F32)
    pos = jnp.zeros((8, edges), F32)
    for c in range(0, entities, step):
        s = s_ref[c:c + step, :]
        hit = jnp.where(iota == tail_row - c, s, 0.0)
        first, second = log_ref[c:c + step, :128], log_ref[c:c + step, 128:]
        log = jnp.concatenate([first, first, second, second], axis=1)
        s = s + log
        s_ref[c:c + step, :] = s
        for k in range(0, step, 8):
            pos = pos + hit[k:k + 8, :]
            top = jnp.maximum(top, s[k:k + 8, :])
    positive = jnp.sum(pos, axis=0, keepdims=True)
    top = jnp.max(top, axis=0, keepdims=True)
    total = jnp.zeros((8, edges), F32)
    for c in range(0, entities, step):
        e = jnp.exp(s_ref[c:c + step, :] - top)
        s_ref[c:c + step, :] = e
        for k in range(0, step, 8):
            total = total + e[k:k + 8, :]
    total = jnp.sum(total, axis=0, keepdims=True)
    share = 1.0 / total
    for c in range(0, entities, step):
        p = s_ref[c:c + step, :] * share
        q_ref[c:c + step, :] = jnp.where(iota == tail_row - c, p - 1.0, p).astype(BF16)
    gap = jnp.log(total) + top - positive
    low = jnp.exp(-jnp.abs(gap))
    loss = jnp.maximum(gap, 0.0) + jnp.log(1.0 + low)
    miss = jnp.where(gap >= 0.0, 1.0, low) / (1.0 + low)
    return loss, miss


def live_row(count, edges):
    group = jnp.where(lax.broadcasted_iota(jnp.int32, (1, edges), 1) < edges // 2, 0, 1)
    return jnp.where(group < count, 1.0, 0.0)


HEADS, TAILS, RELS, NEGS, LIVE, EXTRA = 0, 1, 2, 3, 16, 32


def unpacked(lists, kind, step):
    rows = lists[...].astype(F32)
    k = (kind * 2 + step - 1) * 2
    return (rows[k:k + 1, :] * 256.0 + rows[k + 1:k + 2, :]).astype(jnp.int32)


def live_counts(lists, step):
    k = LIVE + step - 1
    return lists[...].astype(F32)[k:k + 1, :].astype(jnp.int32)


def split(x):
    high = x.astype(BF16)
    return high, (x - high.astype(F32)).astype(BF16)


def pack_kernel(heads_in, tails_in, rels_in, negatives_in, live_in, packed,
                heads, tails, rels, negatives, live_groups, rows, sems):
    pairs = ((heads_in, heads), (tails_in, tails), (rels_in, rels), (negatives_in, negatives), (live_in, live_groups))
    copies = [pltpu.make_async_copy(a, b, sems.at[k]) for k, (a, b) in enumerate(pairs)]
    for copy in copies:
        copy.start()
    for copy in copies:
        copy.wait()
    edges = heads.shape[1]
    half = edges // 2
    rows[...] = jnp.zeros(rows.shape, F32)
    for step in (1, 2):
        for kind, ref in ((HEADS, heads), (TAILS, tails), (RELS, rels)):
            k = (kind * 2 + step - 1) * 2
            row = ref[step:step + 1, :]
            rows[k:k + 1, :] = (row >> 8).astype(F32)
            rows[k + 1:k + 2, :] = (row & 255).astype(F32)
        k = (NEGS * 2 + step - 1) * 2
        for g in range(2):
            row = negatives[step, g:g + 1, :]
            rows[k:k + 1, g * half:(g + 1) * half] = (row >> 8).astype(F32)
            rows[k + 1:k + 2, g * half:(g + 1) * half] = (row & 255).astype(F32)
        k = LIVE + step - 1
        rows[k:k + 1, :] = jnp.broadcast_to(live_groups[:, step:step + 1], (1, edges)).astype(F32)
    packed[...] = rows[...].astype(BF16)


def prepare_kernel(emb, rel, heads, tails, rels, negatives, live_groups, grad, sums, q1, q2, r1, r2, log1, log2, hot, hf, rf, qf, sf, qq, log):
    edges, entities = heads.shape[1], emb.shape[1]
    head_hot = one_hot(heads[0:1, :], entities)
    hf[...] = dot(emb[...], head_hot, NN)
    rf[...] = gather_relations(rel, rels[0:1, :], hot)
    make_query(hf, rf, qf)
    q = qf[...].astype(BF16)
    sf[...] = dot(emb[...], q, TN)
    log_counts([negatives[0, g:g + 1, :] for g in range(2)], entities, log)
    loss, miss = softmax_terms(sf, log, tails[0:1, :], qq)
    live = live_row(live_groups[:, 0:1], edges)
    scale = miss * live * (1.0 / 256.0)
    high, low = split(q.astype(F32) * scale)
    g = dot(high, qq[...], NT) + dot(low, qq[...], NT)
    hf[...] = dot(emb[...], qq[...], NN)
    head_grad(hf, rf, scale, qf)
    high, low = split(qf[...])
    grad[...] = g + dot(high, head_hot, NT) + dot(low, head_hot, NT)
    sums[0:1, :] = loss * live
    sums[1:2, :] = live
    for step, q_out, r_out, log_out in ((1, q1, r1, log1), (2, q2, r2, log2)):
        rf[...] = gather_relations(rel, rels[step:step + 1, :], hot)
        hf[...] = dot(emb[...], one_hot(heads[step:step + 1, :], entities), NN)
        make_query(hf, rf, qf)
        log_counts([negatives[step, g:g + 1, :] for g in range(2)], entities, log_out)
        r_out[...] = rf[...].astype(BF16)
        q_out[...] = qf[...].astype(BF16)


def head_bucket(step, tail, q_in, r_in, log, heads, tails, live_groups, acc, hf, rf, qf, sf, qq):
    edges, (width, entities) = heads.shape[1], acc.shape
    sf[...] = dot(tail[:width, :], q_in[...], TN)
    loss, miss = softmax_terms(sf, log, tails[step:step + 1, :], qq)
    live = live_row(live_groups[:, step:step + 1], edges)
    hf[...] = dot(tail[:width, :], qq[...], NN)
    rf[...] = r_in[...].astype(F32)
    head_grad(hf, rf, miss * live * (1.0 / 256.0), qf)
    high, low = split(qf[...])
    head_hot = one_hot(heads[step:step + 1, :], entities)
    acc[...] += dot(high, head_hot, NT) + dot(low, head_hot, NT)
    return loss * live, live


def far_terms(step, rel, lists, r_out, log_out, hot):
    r_out[...] = gather_relations(rel, unpacked(lists, RELS, step), hot)
    log_counts(halves(unpacked(lists, NEGS, step)), log_out.shape[0], log_out)


def tail_bucket(step, emb, head, lists, rf, log, acc, hf, qf, sf, qq):
    entities, edges = emb.shape[1], lists.shape[1]
    hf[...] = dot(head[...], one_hot(unpacked(lists, HEADS, step), entities), NN)
    make_query(hf, rf, qf)
    q = qf[...].astype(BF16)
    sf[...] = dot(emb[...], q, TN)
    loss, miss = softmax_terms(sf, log, unpacked(lists, TAILS, step), qq)
    scale = miss * live_row(live_counts(lists, step), edges) * (1.0 / 256.0)
    high, low = split(q.astype(F32) * scale)
    acc[...] += dot(high, qq[...], NT) + dot(low, qq[...], NT)


def heads2_kernel(prev2, q2, r2, log2, heads, tails, live_groups, part, sums, grad, sums_out, hf, rf, qf, sf, qq):
    grad[...] = part[...]
    loss, live = head_bucket(2, prev2, q2, r2, log2, heads, tails, live_groups, grad, hf, rf, qf, sf, qq)
    sums_out[0:1, :] = sums[0:1, :] + loss
    sums_out[1:2, :] = sums[1:2, :] + live


def heads1_kernel(sibling, swapped, q1, r1, log1, heads, tails, live_groups, part, sums, grad, row,
                  hf, rf, qf, sf, qq, prev1):
    grad[...] = part[...]
    prev1[...] = jnp.where(lax.axis_index("blk") & 1 == 0, swapped[...], sibling[...])
    loss, live = head_bucket(1, prev1, q1, r1, log1, heads, tails, live_groups, grad, hf, rf, qf, sf, qq)
    loss_all = jnp.sum(sums[0:1, :] + loss, axis=1, keepdims=True)
    live_all = jnp.sum(sums[1:2, :] + live, axis=1, keepdims=True)
    lane = lax.broadcasted_iota(jnp.int32, row.shape, 1)
    row[...] = jnp.where(lane == 0, loss_all, jnp.where(lane == 1, live_all, 0.0))


def after_kernel(block, row, block_out):
    pass


def tails2_kernel(rel, emb, next2, lists, part, grad, hot, hf, rf, qf, sf, qq, log):
    grad[...] = part[...]
    far_terms(2, rel, lists, rf, log, hot)
    tail_bucket(2, emb, next2, lists, rf, log, grad, hf, qf, sf, qq)


def tails1_kernel(rel, emb, sibling, swapped, sibling_lists, swapped_lists, part, row, core_row, grad, rows,
                  hot, hf, rf, qf, sf, qq, acc, next1, lists, log):
    even = lax.axis_index("blk") & 1 == 0
    next1[...] = jnp.where(even, sibling[...], swapped[...])
    lists[...] = jnp.where(even, sibling_lists[...], swapped_lists[...])
    acc[...] = part[...]
    far_terms(1, rel, lists, rf, log, hot)
    tail_bucket(1, emb, next1, lists, rf, log, acc, hf, qf, sf, qq)
    grad[...] = acc[...].astype(BF16)
    rows[...] = jnp.broadcast_to(row[0:1, :] + core_row[0:1, :], rows.shape)


def finish_kernel(own, other, rows, grad, mean):
    grad[...] = own[...].astype(F32) + other[...].astype(F32)
    total = jnp.sum(rows[...], axis=0, keepdims=True)
    mean[...] = total[:, 0:1] / total[:, 1:2]


def kernel(body, outs, scratch, flops, spaces, mib=48, aliases={}):
    return pl.pallas_call(
        body,
        out_shape=[jax.ShapeDtypeStruct(s, t) for s, t in outs],
        in_specs=[pl.BlockSpec(memory_space=m) for m in spaces],
        input_output_aliases=aliases,
        scratch_shapes=[pltpu.VMEM(*s) if isinstance(s, tuple) else s for s in scratch],
        compiler_params=pltpu.CompilerParams(vmem_limit_bytes=mib * 2**20),
        cost_estimate=pl.CostEstimate(flops=flops, bytes_accessed=4 * 2**20, transcendentals=0),
    )


def shifted(x, by):
    peers = lax.axis_size("blk")
    return lax.ppermute(x, "blk", [(i, (i + by) % peers) for i in range(peers)])


def exchanged(x):
    return lax.ppermute(x, "blk", [(i, i ^ 1) for i in range(lax.axis_size("blk"))])


def per_device(embeddings, relations, heads, tails, rels, negatives, live):
    edges = heads.shape[1]
    entities, width = embeddings.shape
    n_rel = relations.shape[0]
    blocks = lax.axis_size("blk")
    emb = embeddings.T
    rel = relations.T
    here = pltpu.VMEM
    big, grads, logs, rows_of = (width, edges), (width, entities), (entities, 256), (8, 128)
    work = [(big, F32), (big, F32), (big, F32), ((entities, edges), F32), ((entities, edges), BF16)]
    hot = ((n_rel, edges), BF16)
    raw = (heads, tails, rels, negatives, live.T)
    prev2 = shifted(emb, 2)
    next2 = shifted(emb, -2)
    sibling = exchanged(emb)
    sent = ((EXTRA, edges), BF16)
    (lists,) = kernel(
        pack_kernel, [sent],
        [(x.shape, x.dtype) for x in raw] + [((EXTRA, edges), F32), pltpu.SemaphoreType.DMA((len(raw),))],
        2 * 10**9, [pltpu.HBM] * len(raw), 56,
    )(*raw)
    next2_lists = shifted(lists, -2)
    sibling_lists = exchanged(lists)
    part, sums, q1, q2, r1, r2, log1, log2 = kernel(
        prepare_kernel,
        [(grads, F32), ((8, edges), F32)] + [(big, BF16)] * 4 + [(logs, F32)] * 2,
        [hot] + work + [(logs, F32)], 20 * 10**9, [here] * 7)(emb, rel, *raw)
    own_lists = (heads, tails, live.T)
    swapped_prev = exchanged(prev2)
    part, sums = kernel(heads2_kernel, [(grads, F32), ((8, edges), F32)], work, 8 * 10**9, [here] * 9)(
        prev2, q2, r2, log2, *own_lists, part, sums)
    part, row = kernel(heads1_kernel, [(grads, F32), (rows_of, F32)], work + [(big, BF16)], 3 * 10**9, [here] * 10)(
        sibling, swapped_prev, q1, r1, log1, *own_lists, part, sums)
    core_row = exchanged(row)
    (next2,) = kernel(after_kernel, [(big, BF16)], [], 10**6, [here] * 2, aliases={0: 0})(next2, row)
    swapped_next = exchanged(next2)
    swapped_lists = exchanged(next2_lists)
    (part,) = kernel(tails2_kernel, [(grads, F32)], [hot] + work + [(logs, F32)], 10 * 10**9, [here] * 5)(
        rel, emb, next2, next2_lists, part)
    own, rows = kernel(
        tails1_kernel, [(grads, BF16), ((blocks, 128), F32)],
        [hot] + work + [(grads, F32), (big, BF16), sent, (logs, F32)], 3 * 10**9, [here] * 9,
    )(rel, emb, sibling, swapped_next, sibling_lists, swapped_lists, part, row, core_row)
    other = lax.ppermute(own, "rep", [(0, 1), (1, 0)])
    rows = lax.all_to_all(rows, ("blk", "rep"), 0, 0, tiled=True,
                          axis_index_groups=[[4 * i + 2 * k + r for i in range(blocks // 2) for r in (0, 1)] for k in (0, 1)])
    grad, mean = kernel(finish_kernel, [(grads, F32), ((1, 1), F32)], [], 10**6, [here] * 3)(own, other, rows)
    return grad.T, mean[0, 0]


def solution(mesh):
    placed = (
        P("blk", None),
        P(),
        P(None, ("blk", "rep")),
        P(None, ("blk", "rep")),
        P(None, ("blk", "rep")),
        P(None, ("blk", "rep"), None),
        P(None, ("blk", "rep")),
    )
    return jax.shard_map(
        per_device, mesh=mesh, in_specs=placed, out_specs=(P("blk", None), P()), check_vma=False
    )
```

```python
import jax
import jax.numpy as jnp
from jax import lax
from jax.experimental import pallas as pl
from jax.experimental.pallas import tpu as pltpu
from jax.sharding import PartitionSpec as P

STEPS = 3
F32 = jnp.float32
BF16 = jnp.bfloat16
NEVER = -1e30
TN = (((0,), (0,)), ((), ()))
NN = (((1,), (0,)), ((), ()))
NT = (((1,), (1,)), ((), ()))


def dot(a, b, dims):
    return lax.dot_general(a, b, dims, preferred_element_type=F32)


def one_hot(row, size):
    hit = lax.broadcasted_iota(jnp.int32, (size, row.shape[1]), 0) == row
    return jnp.where(hit, 1.0, 0.0).astype(BF16)


def gather_relations(rel_t, row, hot_ref):
    block = 256
    low = one_hot(row & (block - 1), block)
    high = row >> 8
    for j in range(rel_t.shape[1] // block):
        here = jnp.where(high == j, 1.0, 0.0).astype(BF16)
        hot_ref[j * block:(j + 1) * block, :] = low * here
    return dot(rel_t[...], hot_ref[...], NN)


def make_query(h_ref, r_ref, q_ref):
    half = h_ref.shape[0] // 2
    step = 40
    for c in range(0, half, step):
        re, im = slice(c, c + step), slice(half + c, half + c + step)
        h_re, h_im, r_re, r_im = h_ref[re, :], h_ref[im, :], r_ref[re, :], r_ref[im, :]
        q_ref[re, :] = h_re * r_re - h_im * r_im
        q_ref[im, :] = h_re * r_im + h_im * r_re


def head_grad(d_ref, r_ref, scale, out_ref):
    half = d_ref.shape[0] // 2
    step = 40
    for c in range(0, half, step):
        re, im = slice(c, c + step), slice(half + c, half + c + step)
        d_re, d_im, r_re, r_im = d_ref[re, :] * scale, d_ref[im, :] * scale, r_ref[re, :], r_ref[im, :]
        out_ref[re, :] = d_re * r_re + d_im * r_im
        out_ref[im, :] = d_im * r_re - d_re * r_im


def halves(row):
    half = row.shape[1] // 2
    return row[:, :half], row[:, half:]


def log_counts(neg_rows, entities, out_ref):
    for g, neg_row in enumerate(neg_rows):
        hot = one_hot(neg_row, entities)
        count = dot(hot, jnp.ones((neg_row.shape[1], 128), BF16), NN)
        out_ref[:, g * 128:(g + 1) * 128] = jnp.where(count > 0.5, jnp.log(jnp.maximum(count, 1.0)), NEVER)


def softmax_terms(s_ref, log_ref, tail_row, q_ref):
    entities, edges = s_ref.shape
    step = 32
    iota = lax.broadcasted_iota(jnp.int32, (step, edges), 0)
    top = jnp.full((8, edges), NEVER, F32)
    pos = jnp.zeros((8, edges), F32)
    for c in range(0, entities, step):
        s = s_ref[c:c + step, :]
        hit = jnp.where(iota == tail_row - c, s, 0.0)
        first, second = log_ref[c:c + step, :128], log_ref[c:c + step, 128:]
        log = jnp.concatenate([first, first, second, second], axis=1)
        s = s + log
        s_ref[c:c + step, :] = s
        for k in range(0, step, 8):
            pos = pos + hit[k:k + 8, :]
            top = jnp.maximum(top, s[k:k + 8, :])
    positive = jnp.sum(pos, axis=0, keepdims=True)
    top = jnp.max(top, axis=0, keepdims=True)
    total = jnp.zeros((8, edges), F32)
    for c in range(0, entities, step):
        e = jnp.exp(s_ref[c:c + step, :] - top)
        s_ref[c:c + step, :] = e
        for k in range(0, step, 8):
            total = total + e[k:k + 8, :]
    total = jnp.sum(total, axis=0, keepdims=True)
    share = 1.0 / total
    for c in range(0, entities, step):
        p = s_ref[c:c + step, :] * share
        q_ref[c:c + step, :] = jnp.where(iota == tail_row - c, p - 1.0, p).astype(BF16)
    gap = jnp.log(total) + top - positive
    low = jnp.exp(-jnp.abs(gap))
    loss = jnp.maximum(gap, 0.0) + jnp.log(1.0 + low)
    miss = jnp.where(gap >= 0.0, 1.0, low) / (1.0 + low)
    return loss, miss


def live_row(count, edges):
    group = jnp.where(lax.broadcasted_iota(jnp.int32, (1, edges), 1) < edges // 2, 0, 1)
    return jnp.where(group < count, 1.0, 0.0)


HEADS, TAILS, RELS, NEGS, LIVE, EXTRA = 0, 1, 2, 3, 16, 32


def unpacked(lists, kind, step):
    rows = lists[...].astype(F32)
    k = (kind * 2 + step - 1) * 2
    return (rows[k:k + 1, :] * 256.0 + rows[k + 1:k + 2, :]).astype(jnp.int32)


def live_counts(lists, step):
    k = LIVE + step - 1
    return lists[...].astype(F32)[k:k + 1, :].astype(jnp.int32)


def split(x):
    high = x.astype(BF16)
    return high, (x - high.astype(F32)).astype(BF16)


def pack_kernel(heads_in, tails_in, rels_in, negatives_in, live_in, packed,
                heads, tails, rels, negatives, live_groups, rows, sems):
    pairs = ((heads_in, heads), (tails_in, tails), (rels_in, rels), (negatives_in, negatives), (live_in, live_groups))
    copies = [pltpu.make_async_copy(a, b, sems.at[k]) for k, (a, b) in enumerate(pairs)]
    for copy in copies:
        copy.start()
    for copy in copies:
        copy.wait()
    edges = heads.shape[1]
    half = edges // 2
    rows[...] = jnp.zeros(rows.shape, F32)
    for step in (1, 2):
        for kind, ref in ((HEADS, heads), (TAILS, tails), (RELS, rels)):
            k = (kind * 2 + step - 1) * 2
            row = ref[step:step + 1, :]
            rows[k:k + 1, :] = (row >> 8).astype(F32)
            rows[k + 1:k + 2, :] = (row & 255).astype(F32)
        k = (NEGS * 2 + step - 1) * 2
        for g in range(2):
            row = negatives[step, g:g + 1, :]
            rows[k:k + 1, g * half:(g + 1) * half] = (row >> 8).astype(F32)
            rows[k + 1:k + 2, g * half:(g + 1) * half] = (row & 255).astype(F32)
        k = LIVE + step - 1
        rows[k:k + 1, :] = jnp.broadcast_to(live_groups[:, step:step + 1], (1, edges)).astype(F32)
    packed[...] = rows[...].astype(BF16)


def prepare_kernel(emb, rel, heads, tails, rels, negatives, live_groups, grad, sums, q1, q2, r1, r2, log1, log2, hot, hf, rf, qf, sf, qq, log):
    edges, entities = heads.shape[1], emb.shape[1]
    head_hot = one_hot(heads[0:1, :], entities)
    hf[...] = dot(emb[...], head_hot, NN)
    rf[...] = gather_relations(rel, rels[0:1, :], hot)
    make_query(hf, rf, qf)
    q = qf[...].astype(BF16)
    sf[...] = dot(emb[...], q, TN)
    log_counts([negatives[0, g:g + 1, :] for g in range(2)], entities, log)
    loss, miss = softmax_terms(sf, log, tails[0:1, :], qq)
    live = live_row(live_groups[:, 0:1], edges)
    scale = miss * live * (1.0 / 256.0)
    high, low = split(q.astype(F32) * scale)
    g = dot(high, qq[...], NT) + dot(low, qq[...], NT)
    hf[...] = dot(emb[...], qq[...], NN)
    head_grad(hf, rf, scale, qf)
    high, low = split(qf[...])
    grad[...] = g + dot(high, head_hot, NT) + dot(low, head_hot, NT)
    sums[0:1, :] = loss * live
    sums[1:2, :] = live
    for step, q_out, r_out, log_out in ((1, q1, r1, log1), (2, q2, r2, log2)):
        rf[...] = gather_relations(rel, rels[step:step + 1, :], hot)
        hf[...] = dot(emb[...], one_hot(heads[step:step + 1, :], entities), NN)
        make_query(hf, rf, qf)
        log_counts([negatives[step, g:g + 1, :] for g in range(2)], entities, log_out)
        r_out[...] = rf[...].astype(BF16)
        q_out[...] = qf[...].astype(BF16)


def head_bucket(step, tail, q_in, r_in, log, heads, tails, live_groups, acc, hf, rf, qf, sf, qq):
    edges, (width, entities) = heads.shape[1], acc.shape
    sf[...] = dot(tail[:width, :], q_in[...], TN)
    loss, miss = softmax_terms(sf, log, tails[step:step + 1, :], qq)
    live = live_row(live_groups[:, step:step + 1], edges)
    hf[...] = dot(tail[:width, :], qq[...], NN)
    rf[...] = r_in[...].astype(F32)
    head_grad(hf, rf, miss * live * (1.0 / 256.0), qf)
    high, low = split(qf[...])
    head_hot = one_hot(heads[step:step + 1, :], entities)
    acc[...] += dot(high, head_hot, NT) + dot(low, head_hot, NT)
    return loss * live, live


def far_terms(step, rel, lists, r_out, log_out, hot):
    r_out[...] = gather_relations(rel, unpacked(lists, RELS, step), hot)
    log_counts(halves(unpacked(lists, NEGS, step)), log_out.shape[0], log_out)


def tail_bucket(step, emb, head, lists, rf, log, acc, hf, qf, sf, qq):
    entities, edges = emb.shape[1], lists.shape[1]
    hf[...] = dot(head[...], one_hot(unpacked(lists, HEADS, step), entities), NN)
    make_query(hf, rf, qf)
    q = qf[...].astype(BF16)
    sf[...] = dot(emb[...], q, TN)
    loss, miss = softmax_terms(sf, log, unpacked(lists, TAILS, step), qq)
    scale = miss * live_row(live_counts(lists, step), edges) * (1.0 / 256.0)
    high, low = split(q.astype(F32) * scale)
    acc[...] += dot(high, qq[...], NT) + dot(low, qq[...], NT)


def heads2_kernel(prev2, q2, r2, log2, heads, tails, live_groups, part, sums, grad, sums_out, hf, rf, qf, sf, qq):
    grad[...] = part[...]
    loss, live = head_bucket(2, prev2, q2, r2, log2, heads, tails, live_groups, grad, hf, rf, qf, sf, qq)
    sums_out[0:1, :] = sums[0:1, :] + loss
    sums_out[1:2, :] = sums[1:2, :] + live


def heads1_kernel(sibling, swapped, q1, r1, log1, heads, tails, live_groups, part, sums, grad, row,
                  hf, rf, qf, sf, qq, prev1):
    grad[...] = part[...]
    prev1[...] = jnp.where(lax.axis_index("blk") & 1 == 0, swapped[...], sibling[...])
    loss, live = head_bucket(1, prev1, q1, r1, log1, heads, tails, live_groups, grad, hf, rf, qf, sf, qq)
    loss_all = jnp.sum(sums[0:1, :] + loss, axis=1, keepdims=True)
    live_all = jnp.sum(sums[1:2, :] + live, axis=1, keepdims=True)
    lane = lax.broadcasted_iota(jnp.int32, row.shape, 1)
    row[...] = jnp.where(lane == 0, loss_all, jnp.where(lane == 1, live_all, 0.0))


def after_kernel(block, lists, row, block_out, lists_out):
    pass


def tails2_kernel(rel, emb, next2, lists, part, grad, hot, hf, rf, qf, sf, qq, log):
    grad[...] = part[...]
    far_terms(2, rel, lists, rf, log, hot)
    tail_bucket(2, emb, next2, lists, rf, log, grad, hf, qf, sf, qq)


def tails1_kernel(rel, emb, sibling, swapped, sibling_lists, swapped_lists, part, row, core_row, grad, rows,
                  hot, hf, rf, qf, sf, qq, acc, next1, lists, log):
    even = lax.axis_index("blk") & 1 == 0
    next1[...] = jnp.where(even, sibling[...], swapped[...])
    lists[...] = jnp.where(even, sibling_lists[...], swapped_lists[...])
    acc[...] = part[...]
    far_terms(1, rel, lists, rf, log, hot)
    tail_bucket(1, emb, next1, lists, rf, log, acc, hf, qf, sf, qq)
    grad[...] = acc[...].astype(BF16)
    rows[...] = jnp.broadcast_to(row[0:1, :] + core_row[0:1, :], rows.shape)


def finish_kernel(own, other, rows, grad, mean):
    grad[...] = own[...].astype(F32) + other[...].astype(F32)
    total = jnp.sum(rows[...], axis=0, keepdims=True)
    mean[...] = total[:, 0:1] / total[:, 1:2]


def kernel(body, outs, scratch, flops, spaces, mib=48, aliases={}):
    return pl.pallas_call(
        body,
        out_shape=[jax.ShapeDtypeStruct(s, t) for s, t in outs],
        in_specs=[pl.BlockSpec(memory_space=m) for m in spaces],
        input_output_aliases=aliases,
        scratch_shapes=[pltpu.VMEM(*s) if isinstance(s, tuple) else s for s in scratch],
        compiler_params=pltpu.CompilerParams(vmem_limit_bytes=mib * 2**20),
        cost_estimate=pl.CostEstimate(flops=flops, bytes_accessed=4 * 2**20, transcendentals=0),
    )


def shifted(x, by):
    peers = lax.axis_size("blk")
    return lax.ppermute(x, "blk", [(i, (i + by) % peers) for i in range(peers)])


def exchanged(x):
    return lax.ppermute(x, "blk", [(i, i ^ 1) for i in range(lax.axis_size("blk"))])


def per_device(embeddings, relations, heads, tails, rels, negatives, live):
    edges = heads.shape[1]
    entities, width = embeddings.shape
    n_rel = relations.shape[0]
    blocks = lax.axis_size("blk")
    emb = embeddings.T
    rel = relations.T
    here = pltpu.VMEM
    big, grads, logs, rows_of = (width, edges), (width, entities), (entities, 256), (8, 128)
    work = [(big, F32), (big, F32), (big, F32), ((entities, edges), F32), ((entities, edges), BF16)]
    hot = ((n_rel, edges), BF16)
    raw = (heads, tails, rels, negatives, live.T)
    prev2 = shifted(emb, 2)
    next2 = shifted(emb, -2)
    sibling = exchanged(emb)
    sent = ((EXTRA, edges), BF16)
    (lists,) = kernel(
        pack_kernel, [sent],
        [(x.shape, x.dtype) for x in raw] + [((EXTRA, edges), F32), pltpu.SemaphoreType.DMA((len(raw),))],
        2 * 10**9, [pltpu.HBM] * len(raw), 56,
    )(*raw)
    next2_lists = shifted(lists, -2)
    sibling_lists = exchanged(lists)
    part, sums, q1, q2, r1, r2, log1, log2 = kernel(
        prepare_kernel,
        [(grads, F32), ((8, edges), F32)] + [(big, BF16)] * 4 + [(logs, F32)] * 2,
        [hot] + work + [(logs, F32)], 20 * 10**9, [here] * 7)(emb, rel, *raw)
    own_lists = (heads, tails, live.T)
    swapped_prev = exchanged(prev2)
    part, sums = kernel(heads2_kernel, [(grads, F32), ((8, edges), F32)], work, 8 * 10**9, [here] * 9)(
        prev2, q2, r2, log2, *own_lists, part, sums)
    part, row = kernel(heads1_kernel, [(grads, F32), (rows_of, F32)], work + [(big, BF16)], 3 * 10**9, [here] * 10)(
        sibling, swapped_prev, q1, r1, log1, *own_lists, part, sums)
    core_row = exchanged(row)
    next2, next2_lists = kernel(after_kernel, [(big, BF16), sent], [], 10**6, [here] * 3, aliases={0: 0, 1: 1})(
        next2, next2_lists, row)
    swapped_next = exchanged(next2)
    swapped_lists = exchanged(next2_lists)
    (part,) = kernel(tails2_kernel, [(grads, F32)], [hot] + work + [(logs, F32)], 10 * 10**9, [here] * 5)(
        rel, emb, next2, next2_lists, part)
    own, rows = kernel(
        tails1_kernel, [(grads, BF16), ((blocks, 128), F32)],
        [hot] + work + [(grads, F32), (big, BF16), sent, (logs, F32)], 3 * 10**9, [here] * 9,
    )(rel, emb, sibling, swapped_next, sibling_lists, swapped_lists, part, row, core_row)
    other = lax.ppermute(own, "rep", [(0, 1), (1, 0)])
    rows = lax.all_to_all(rows, ("blk", "rep"), 0, 0, tiled=True,
                          axis_index_groups=[[4 * i + 2 * k + r for i in range(blocks // 2) for r in (0, 1)] for k in (0, 1)])
    grad, mean = kernel(finish_kernel, [(grads, F32), ((1, 1), F32)], [], 10**6, [here] * 3)(own, other, rows)
    return grad.T, mean[0, 0]


def solution(mesh):
    placed = (
        P("blk", None),
        P(),
        P(None, ("blk", "rep")),
        P(None, ("blk", "rep")),
        P(None, ("blk", "rep")),
        P(None, ("blk", "rep"), None),
        P(None, ("blk", "rep")),
    )
    return jax.shard_map(
        per_device, mesh=mesh, in_specs=placed, out_specs=(P("blk", None), P()), check_vma=False
    )
```

```python
import jax
import jax.numpy as jnp
from jax import lax
from jax.experimental import pallas as pl
from jax.experimental.pallas import tpu as pltpu
from jax.sharding import PartitionSpec as P

STEPS = 3
F32 = jnp.float32
BF16 = jnp.bfloat16
NEVER = -1e30
TN = (((0,), (0,)), ((), ()))
NN = (((1,), (0,)), ((), ()))
NT = (((1,), (1,)), ((), ()))


def dot(a, b, dims):
    return lax.dot_general(a, b, dims, preferred_element_type=F32)


def one_hot(row, size):
    hit = lax.broadcasted_iota(jnp.int32, (size, row.shape[1]), 0) == row
    return jnp.where(hit, 1.0, 0.0).astype(BF16)


def gather_relations(rel_t, row, hot_ref):
    block = 256
    low = one_hot(row & (block - 1), block)
    high = row >> 8
    for j in range(rel_t.shape[1] // block):
        here = jnp.where(high == j, 1.0, 0.0).astype(BF16)
        hot_ref[j * block:(j + 1) * block, :] = low * here
    return dot(rel_t[...], hot_ref[...], NN)


def make_query(h_ref, r_ref, q_ref):
    half = h_ref.shape[0] // 2
    step = 40
    for c in range(0, half, step):
        re, im = slice(c, c + step), slice(half + c, half + c + step)
        h_re, h_im, r_re, r_im = h_ref[re, :], h_ref[im, :], r_ref[re, :], r_ref[im, :]
        q_ref[re, :] = h_re * r_re - h_im * r_im
        q_ref[im, :] = h_re * r_im + h_im * r_re


def head_grad(d_ref, r_ref, scale, out_ref):
    half = d_ref.shape[0] // 2
    step = 40
    for c in range(0, half, step):
        re, im = slice(c, c + step), slice(half + c, half + c + step)
        d_re, d_im, r_re, r_im = d_ref[re, :] * scale, d_ref[im, :] * scale, r_ref[re, :], r_ref[im, :]
        out_ref[re, :] = d_re * r_re + d_im * r_im
        out_ref[im, :] = d_im * r_re - d_re * r_im


def halves(row):
    half = row.shape[1] // 2
    return row[:, :half], row[:, half:]


def log_counts(neg_rows, entities, out_ref):
    for g, neg_row in enumerate(neg_rows):
        hot = one_hot(neg_row, entities)
        count = dot(hot, jnp.ones((neg_row.shape[1], 128), BF16), NN)
        out_ref[:, g * 128:(g + 1) * 128] = jnp.where(count > 0.5, jnp.log(jnp.maximum(count, 1.0)), NEVER)


def softmax_terms(s_ref, log_ref, tail_row, q_ref):
    entities, edges = s_ref.shape
    step = 16384 // edges
    iota = lax.broadcasted_iota(jnp.int32, (step, edges), 0)
    top = jnp.full((8, edges), NEVER, F32)
    pos = jnp.zeros((8, edges), F32)
    for c in range(0, entities, step):
        s = s_ref[c:c + step, :]
        hit = jnp.where(iota == tail_row - c, s, 0.0)
        log = log_ref[c:c + step, :]
        tiles = edges // log.shape[1]
        log = jnp.concatenate([log[:, k // tiles * 128:k // tiles * 128 + 128] for k in range(edges // 128)], axis=1)
        s = s + log
        s_ref[c:c + step, :] = s
        for k in range(0, step, 8):
            pos = pos + hit[k:k + 8, :]
            top = jnp.maximum(top, s[k:k + 8, :])
    positive = jnp.sum(pos, axis=0, keepdims=True)
    top = jnp.max(top, axis=0, keepdims=True)
    total = jnp.zeros((8, edges), F32)
    for c in range(0, entities, step):
        e = jnp.exp(s_ref[c:c + step, :] - top)
        s_ref[c:c + step, :] = e
        for k in range(0, step, 8):
            total = total + e[k:k + 8, :]
    total = jnp.sum(total, axis=0, keepdims=True)
    share = 1.0 / total
    for c in range(0, entities, step):
        p = s_ref[c:c + step, :] * share
        q_ref[c:c + step, :] = jnp.where(iota == tail_row - c, p - 1.0, p).astype(BF16)
    gap = jnp.log(total) + top - positive
    low = jnp.exp(-jnp.abs(gap))
    loss = jnp.maximum(gap, 0.0) + jnp.log(1.0 + low)
    miss = jnp.where(gap >= 0.0, 1.0, low) / (1.0 + low)
    return loss, miss


def live_row(count, edges):
    group = jnp.where(lax.broadcasted_iota(jnp.int32, (1, edges), 1) < edges // 2, 0, 1)
    return jnp.where(group < count, 1.0, 0.0)


HEADS, TAILS, RELS, NEGS, LIVE, EXTRA = 0, 1, 2, 3, 16, 32


def unpacked(lists, kind, step):
    rows = lists[...].astype(F32)
    k = (kind * 2 + step - 1) * 2
    return (rows[k:k + 1, :] * 256.0 + rows[k + 1:k + 2, :]).astype(jnp.int32)


def live_counts(lists, step):
    k = LIVE + step - 1
    return lists[...].astype(F32)[k:k + 1, :].astype(jnp.int32)


def split(x):
    high = x.astype(BF16)
    return high, (x - high.astype(F32)).astype(BF16)


def pack_kernel(heads_in, tails_in, rels_in, negatives_in, live_in, packed,
                heads, tails, rels, negatives, live_groups, rows, sems):
    pairs = ((heads_in, heads), (tails_in, tails), (rels_in, rels), (negatives_in, negatives), (live_in, live_groups))
    copies = [pltpu.make_async_copy(a, b, sems.at[k]) for k, (a, b) in enumerate(pairs)]
    for copy in copies:
        copy.start()
    for copy in copies:
        copy.wait()
    edges = heads.shape[1]
    half = edges // 2
    rows[...] = jnp.zeros(rows.shape, F32)
    for step in (1, 2):
        for kind, ref in ((HEADS, heads), (TAILS, tails), (RELS, rels)):
            k = (kind * 2 + step - 1) * 2
            row = ref[step:step + 1, :]
            rows[k:k + 1, :] = (row >> 8).astype(F32)
            rows[k + 1:k + 2, :] = (row & 255).astype(F32)
        k = (NEGS * 2 + step - 1) * 2
        for g in range(2):
            row = negatives[step, g:g + 1, :]
            rows[k:k + 1, g * half:(g + 1) * half] = (row >> 8).astype(F32)
            rows[k + 1:k + 2, g * half:(g + 1) * half] = (row & 255).astype(F32)
        k = LIVE + step - 1
        rows[k:k + 1, :] = jnp.broadcast_to(live_groups[:, step:step + 1], (1, edges)).astype(F32)
    packed[...] = rows[...].astype(BF16)


def prepare_kernel(emb, rel, heads, tails, rels, negatives, live_groups, grad, sums, q1, q2, r1, r2, log1, log2, hot, hf, rf, qf, sf, qq, log):
    edges, entities = heads.shape[1], emb.shape[1]
    head_hot = one_hot(heads[0:1, :], entities)
    hf[...] = dot(emb[...], head_hot, NN)
    rf[...] = gather_relations(rel, rels[0:1, :], hot)
    make_query(hf, rf, qf)
    q = qf[...].astype(BF16)
    sf[...] = dot(emb[...], q, TN)
    log_counts([negatives[0, g:g + 1, :] for g in range(2)], entities, log)
    loss, miss = softmax_terms(sf, log, tails[0:1, :], qq)
    live = live_row(live_groups[:, 0:1], edges)
    scale = miss * live * (1.0 / 256.0)
    high, low = split(q.astype(F32) * scale)
    g = dot(high, qq[...], NT) + dot(low, qq[...], NT)
    hf[...] = dot(emb[...], qq[...], NN)
    head_grad(hf, rf, scale, qf)
    high, low = split(qf[...])
    grad[...] = g + dot(high, head_hot, NT) + dot(low, head_hot, NT)
    sums[0:1, :] = loss * live
    sums[1:2, :] = live
    for step, q_out, r_out, log_out in ((1, q1, r1, log1), (2, q2, r2, log2)):
        rf[...] = gather_relations(rel, rels[step:step + 1, :], hot)
        hf[...] = dot(emb[...], one_hot(heads[step:step + 1, :], entities), NN)
        make_query(hf, rf, qf)
        log_counts([negatives[step, g:g + 1, :] for g in range(2)], entities, log_out)
        r_out[...] = rf[...].astype(BF16)
        q_out[...] = qf[...].astype(BF16)


def head_bucket(step, tail, q_in, r_in, log, heads, tails, live_groups, acc, hf, rf, qf, sf, qq):
    edges, (width, entities) = heads.shape[1], acc.shape
    half = edges // 2
    groups = [slice(g * half, (g + 1) * half) for g in range(2)]
    row = slice(step, step + 1)
    for g in groups:
        sf[:, g] = dot(tail[...], q_in[:, g], TN)
    terms = [softmax_terms(sf.at[:, g], log.at[:, k * 128:(k + 1) * 128], tails[row, g], qq.at[:, g])
             for k, g in enumerate(groups)]
    live = live_row(live_groups[:, row], edges)
    loss = jnp.concatenate([t[0] for t in terms], axis=1) * live
    for g in groups:
        hf[:, g] = dot(tail[...], qq[:, g], NN)
    rf[...] = r_in[...].astype(F32)
    for k, g in enumerate(groups):
        head_grad(hf.at[:, g], rf.at[:, g], terms[k][1] * live[:, g] * (1.0 / 256.0), qf.at[:, g])
    for g in groups:
        high, low = split(qf[:, g])
        head_hot = one_hot(heads[row, g], entities)
        acc[...] += dot(high, head_hot, NT) + dot(low, head_hot, NT)
    return loss, live


def far_terms(step, rel, lists, r_out, log_out, hot):
    r_out[...] = gather_relations(rel, unpacked(lists, RELS, step), hot)
    log_counts(halves(unpacked(lists, NEGS, step)), log_out.shape[0], log_out)


def tail_bucket(step, emb, head, lists, rf, log, acc, hf, qf, sf, qq):
    entities, edges = emb.shape[1], lists.shape[1]
    hf[...] = dot(head[...], one_hot(unpacked(lists, HEADS, step), entities), NN)
    make_query(hf, rf, qf)
    q = qf[...].astype(BF16)
    sf[...] = dot(emb[...], q, TN)
    loss, miss = softmax_terms(sf, log, unpacked(lists, TAILS, step), qq)
    scale = miss * live_row(live_counts(lists, step), edges) * (1.0 / 256.0)
    high, low = split(q.astype(F32) * scale)
    acc[...] += dot(high, qq[...], NT) + dot(low, qq[...], NT)


def heads2_kernel(prev2, q2, r2, log2, heads, tails, live_groups, part, sums, grad, sums_out, hf, rf, qf, sf, qq):
    loss, live = head_bucket(2, prev2, q2, r2, log2, heads, tails, live_groups, grad, hf, rf, qf, sf, qq)
    sums_out[0:1, :] = sums[0:1, :] + loss
    sums_out[1:2, :] = sums[1:2, :] + live


def heads1_kernel(sibling, swapped, q1, r1, log1, heads, tails, live_groups, part, sums, grad, row,
                  hf, rf, qf, sf, qq, prev1):
    prev1[...] = jnp.where(lax.axis_index("blk") & 1 == 0, swapped[...], sibling[...])
    loss, live = head_bucket(1, prev1, q1, r1, log1, heads, tails, live_groups, grad, hf, rf, qf, sf, qq)
    loss_all = jnp.sum(sums[0:1, :] + loss, axis=1, keepdims=True)
    live_all = jnp.sum(sums[1:2, :] + live, axis=1, keepdims=True)
    lane = lax.broadcasted_iota(jnp.int32, row.shape, 1)
    row[...] = jnp.where(lane == 0, loss_all, jnp.where(lane == 1, live_all, 0.0))


def after_kernel(block, lists, row, block_out, lists_out):
    pass


def tails2_kernel(rel, emb, next2, lists, part, grad, hot, hf, rf, qf, sf, qq, log):
    far_terms(2, rel, lists, rf, log, hot)
    tail_bucket(2, emb, next2, lists, rf, log, grad, hf, qf, sf, qq)


def tails1_kernel(rel, emb, sibling, swapped, sibling_lists, swapped_lists, part, row, core_row, grad, rows,
                  hot, hf, rf, qf, sf, qq, acc, next1, lists, log):
    even = lax.axis_index("blk") & 1 == 0
    next1[...] = jnp.where(even, sibling[...], swapped[...])
    lists[...] = jnp.where(even, sibling_lists[...], swapped_lists[...])
    acc[...] = part[...]
    far_terms(1, rel, lists, rf, log, hot)
    tail_bucket(1, emb, next1, lists, rf, log, acc, hf, qf, sf, qq)
    grad[...] = acc[...].astype(BF16)
    rows[...] = jnp.broadcast_to(row[0:1, :] + core_row[0:1, :], rows.shape)


def finish_kernel(own, other, rows, grad, mean):
    grad[...] = own[...].astype(F32) + other[...].astype(F32)
    total = jnp.sum(rows[...], axis=0, keepdims=True)
    mean[...] = total[:, 0:1] / total[:, 1:2]


def kernel(body, outs, scratch, flops, spaces, mib=48, aliases={}):
    return pl.pallas_call(
        body,
        out_shape=[jax.ShapeDtypeStruct(s, t) for s, t in outs],
        in_specs=[pl.BlockSpec(memory_space=m) for m in spaces],
        input_output_aliases=aliases,
        scratch_shapes=[pltpu.VMEM(*s) if isinstance(s, tuple) else s for s in scratch],
        compiler_params=pltpu.CompilerParams(vmem_limit_bytes=mib * 2**20),
        cost_estimate=pl.CostEstimate(flops=flops, bytes_accessed=4 * 2**20, transcendentals=0),
    )


def shifted(x, by):
    peers = lax.axis_size("blk")
    return lax.ppermute(x, "blk", [(i, (i + by) % peers) for i in range(peers)])


def exchanged(x):
    return lax.ppermute(x, "blk", [(i, i ^ 1) for i in range(lax.axis_size("blk"))])


def per_device(embeddings, relations, heads, tails, rels, negatives, live):
    edges = heads.shape[1]
    entities, width = embeddings.shape
    n_rel = relations.shape[0]
    blocks = lax.axis_size("blk")
    emb = embeddings.T
    rel = relations.T
    here = pltpu.VMEM
    big, grads, logs, rows_of = (width, edges), (width, entities), (entities, 256), (8, 128)
    work = [(big, F32), (big, F32), (big, F32), ((entities, edges), F32), ((entities, edges), BF16)]
    hot = ((n_rel, edges), BF16)
    raw = (heads, tails, rels, negatives, live.T)
    prev2 = shifted(emb, 2)
    next2 = shifted(emb, -2)
    sibling = exchanged(emb)
    sent = ((EXTRA, edges), BF16)
    (lists,) = kernel(
        pack_kernel, [sent],
        [(x.shape, x.dtype) for x in raw] + [((EXTRA, edges), F32), pltpu.SemaphoreType.DMA((len(raw),))],
        2 * 10**9, [pltpu.HBM] * len(raw), 56,
    )(*raw)
    next2_lists = shifted(lists, -2)
    sibling_lists = exchanged(lists)
    part, sums, q1, q2, r1, r2, log1, log2 = kernel(
        prepare_kernel,
        [(grads, F32), ((8, edges), F32)] + [(big, BF16)] * 4 + [(logs, F32)] * 2,
        [hot] + work + [(logs, F32)], 20 * 10**9, [here] * 7)(emb, rel, *raw)
    own_lists = (heads, tails, live.T)
    swapped_prev = exchanged(prev2)
    part, sums = kernel(heads2_kernel, [(grads, F32), ((8, edges), F32)], work, 8 * 10**9, [here] * 9, aliases={7: 0})(
        prev2, q2, r2, log2, *own_lists, part, sums)
    part, row = kernel(heads1_kernel, [(grads, F32), (rows_of, F32)], work + [(big, BF16)], 3 * 10**9, [here] * 10, aliases={8: 0})(
        sibling, swapped_prev, q1, r1, log1, *own_lists, part, sums)
    core_row = exchanged(row)
    next2, next2_lists = kernel(after_kernel, [(big, BF16), sent], [], 10**6, [here] * 3, aliases={0: 0, 1: 1})(
        next2, next2_lists, row)
    swapped_next = exchanged(next2)
    swapped_lists = exchanged(next2_lists)
    (part,) = kernel(tails2_kernel, [(grads, F32)], [hot] + work + [(logs, F32)], 10 * 10**9, [here] * 5, aliases={4: 0})(
        rel, emb, next2, next2_lists, part)
    own, rows = kernel(
        tails1_kernel, [(grads, BF16), ((blocks, 128), F32)],
        [hot] + work + [(grads, F32), (big, BF16), sent, (logs, F32)], 3 * 10**9, [here] * 9,
    )(rel, emb, sibling, swapped_next, sibling_lists, swapped_lists, part, row, core_row)
    other = lax.ppermute(own, "rep", [(0, 1), (1, 0)])
    rows = lax.all_to_all(rows, ("blk", "rep"), 0, 0, tiled=True,
                          axis_index_groups=[[4 * i + 2 * k + r for i in range(blocks // 2) for r in (0, 1)] for k in (0, 1)])
    grad, mean = kernel(finish_kernel, [(grads, F32), ((1, 1), F32)], [], 10**6, [here] * 3)(own, other, rows)
    return grad.T, mean[0, 0]


def solution(mesh):
    placed = (
        P("blk", None),
        P(),
        P(None, ("blk", "rep")),
        P(None, ("blk", "rep")),
        P(None, ("blk", "rep")),
        P(None, ("blk", "rep"), None),
        P(None, ("blk", "rep")),
    )
    return jax.shard_map(
        per_device, mesh=mesh, in_specs=placed, out_specs=(P("blk", None), P()), check_vma=False
    )
```

```python
import jax
import jax.numpy as jnp
from jax import lax
from jax.experimental import pallas as pl
from jax.experimental.pallas import tpu as pltpu
from jax.sharding import PartitionSpec as P

STEPS = 3
F32 = jnp.float32
BF16 = jnp.bfloat16
NEVER = -1e30
TN = (((0,), (0,)), ((), ()))
NN = (((1,), (0,)), ((), ()))
NT = (((1,), (1,)), ((), ()))


def dot(a, b, dims):
    return lax.dot_general(a, b, dims, preferred_element_type=F32)


def one_hot(row, size):
    hit = lax.broadcasted_iota(jnp.int32, (size, row.shape[1]), 0) == row
    return jnp.where(hit, 1.0, 0.0).astype(BF16)


def gather_relations(rel_t, row, hot_ref):
    block = 256
    low = one_hot(row & (block - 1), block)
    high = row >> 8
    for j in range(rel_t.shape[1] // block):
        here = jnp.where(high == j, 1.0, 0.0).astype(BF16)
        hot_ref[j * block:(j + 1) * block, :] = low * here
    return dot(rel_t[...], hot_ref[...], NN)


def make_query(h_ref, r_ref, q_ref):
    half = h_ref.shape[0] // 2
    step = 40
    for c in range(0, half, step):
        re, im = slice(c, c + step), slice(half + c, half + c + step)
        h_re, h_im, r_re, r_im = h_ref[re, :], h_ref[im, :], r_ref[re, :], r_ref[im, :]
        q_ref[re, :] = h_re * r_re - h_im * r_im
        q_ref[im, :] = h_re * r_im + h_im * r_re


def head_grad(d_ref, r_ref, scale, out_ref):
    half = d_ref.shape[0] // 2
    step = 40
    for c in range(0, half, step):
        re, im = slice(c, c + step), slice(half + c, half + c + step)
        d_re, d_im, r_re, r_im = d_ref[re, :] * scale, d_ref[im, :] * scale, r_ref[re, :], r_ref[im, :]
        out_ref[re, :] = d_re * r_re + d_im * r_im
        out_ref[im, :] = d_im * r_re - d_re * r_im


def halves(row):
    half = row.shape[1] // 2
    return row[:, :half], row[:, half:]


def log_counts(neg_rows, entities, out_ref):
    for g, neg_row in enumerate(neg_rows):
        hot = one_hot(neg_row, entities)
        count = dot(hot, jnp.ones((neg_row.shape[1], 128), BF16), NN)
        out_ref[:, g * 128:(g + 1) * 128] = jnp.where(count > 0.5, jnp.log(jnp.maximum(count, 1.0)), NEVER)


def softmax_terms(s_ref, log_ref, tail_row, q_ref):
    entities, edges = s_ref.shape
    step = 16384 // edges
    iota = lax.broadcasted_iota(jnp.int32, (step, edges), 0)
    top = jnp.full((8, edges), NEVER, F32)
    pos = jnp.zeros((8, edges), F32)
    for c in range(0, entities, step):
        s = s_ref[c:c + step, :]
        hit = jnp.where(iota == tail_row - c, s, 0.0)
        log = log_ref[c:c + step, :]
        tiles = edges // log.shape[1]
        log = jnp.concatenate([log[:, k // tiles * 128:k // tiles * 128 + 128] for k in range(edges // 128)], axis=1)
        s = s + log
        s_ref[c:c + step, :] = s
        for k in range(0, step, 8):
            pos = pos + hit[k:k + 8, :]
            top = jnp.maximum(top, s[k:k + 8, :])
    positive = jnp.sum(pos, axis=0, keepdims=True)
    top = jnp.max(top, axis=0, keepdims=True)
    total = jnp.zeros((8, edges), F32)
    for c in range(0, entities, step):
        e = jnp.exp(s_ref[c:c + step, :] - top)
        s_ref[c:c + step, :] = e
        for k in range(0, step, 8):
            total = total + e[k:k + 8, :]
    total = jnp.sum(total, axis=0, keepdims=True)
    share = 1.0 / total
    for c in range(0, entities, step):
        p = s_ref[c:c + step, :] * share
        q_ref[c:c + step, :] = jnp.where(iota == tail_row - c, p - 1.0, p).astype(BF16)
    gap = jnp.log(total) + top - positive
    low = jnp.exp(-jnp.abs(gap))
    loss = jnp.maximum(gap, 0.0) + jnp.log(1.0 + low)
    miss = jnp.where(gap >= 0.0, 1.0, low) / (1.0 + low)
    return loss, miss


def live_row(count, edges):
    group = jnp.where(lax.broadcasted_iota(jnp.int32, (1, edges), 1) < edges // 2, 0, 1)
    return jnp.where(group < count, 1.0, 0.0)


HEADS, TAILS, RELS, NEGS, LIVE, EXTRA = 0, 1, 2, 3, 16, 32


def unpacked(lists, kind, step):
    rows = lists[...].astype(F32)
    k = (kind * 2 + step - 1) * 2
    return (rows[k:k + 1, :] * 256.0 + rows[k + 1:k + 2, :]).astype(jnp.int32)


def live_counts(lists, step):
    k = LIVE + step - 1
    return lists[...].astype(F32)[k:k + 1, :].astype(jnp.int32)


def split(x):
    high = x.astype(BF16)
    return high, (x - high.astype(F32)).astype(BF16)


def pack_kernel(heads_in, tails_in, rels_in, negatives_in, live_in, packed,
                heads, tails, rels, negatives, live_groups, rows, sems):
    pairs = ((heads_in, heads), (tails_in, tails), (rels_in, rels), (negatives_in, negatives), (live_in, live_groups))
    copies = [pltpu.make_async_copy(a, b, sems.at[k]) for k, (a, b) in enumerate(pairs)]
    for copy in copies:
        copy.start()
    for copy in copies:
        copy.wait()
    edges = heads.shape[1]
    half = edges // 2
    rows[...] = jnp.zeros(rows.shape, F32)
    for step in (1, 2):
        for kind, ref in ((HEADS, heads), (TAILS, tails), (RELS, rels)):
            k = (kind * 2 + step - 1) * 2
            row = ref[step:step + 1, :]
            rows[k:k + 1, :] = (row >> 8).astype(F32)
            rows[k + 1:k + 2, :] = (row & 255).astype(F32)
        k = (NEGS * 2 + step - 1) * 2
        for g in range(2):
            row = negatives[step, g:g + 1, :]
            rows[k:k + 1, g * half:(g + 1) * half] = (row >> 8).astype(F32)
            rows[k + 1:k + 2, g * half:(g + 1) * half] = (row & 255).astype(F32)
        k = LIVE + step - 1
        rows[k:k + 1, :] = jnp.broadcast_to(live_groups[:, step:step + 1], (1, edges)).astype(F32)
    packed[...] = rows[...].astype(BF16)


def prepare_kernel(emb, rel, heads, tails, rels, negatives, live_groups, grad, sums, q1, q2, r1, r2, log1, log2, hot, hf, rf, qf, sf, qq, log):
    edges, entities = heads.shape[1], emb.shape[1]
    head_hot = one_hot(heads[0:1, :], entities)
    hf[...] = dot(emb[...], head_hot, NN)
    rf[...] = gather_relations(rel, rels[0:1, :], hot)
    make_query(hf, rf, qf)
    q = qf[...].astype(BF16)
    sf[...] = dot(emb[...], q, TN)
    log_counts([negatives[0, g:g + 1, :] for g in range(2)], entities, log)
    loss, miss = softmax_terms(sf, log, tails[0:1, :], qq)
    live = live_row(live_groups[:, 0:1], edges)
    scale = miss * live * (1.0 / 256.0)
    high, low = split(q.astype(F32) * scale)
    g = dot(high, qq[...], NT) + dot(low, qq[...], NT)
    hf[...] = dot(emb[...], qq[...], NN)
    head_grad(hf, rf, scale, qf)
    high, low = split(qf[...])
    grad[...] = g + dot(high, head_hot, NT) + dot(low, head_hot, NT)
    sums[0:1, :] = loss * live
    sums[1:2, :] = live
    for step, q_out, r_out, log_out in ((1, q1, r1, log1), (2, q2, r2, log2)):
        rf[...] = gather_relations(rel, rels[step:step + 1, :], hot)
        hf[...] = dot(emb[...], one_hot(heads[step:step + 1, :], entities), NN)
        make_query(hf, rf, qf)
        log_counts([negatives[step, g:g + 1, :] for g in range(2)], entities, log_out)
        r_out[...] = rf[...].astype(BF16)
        q_out[...] = qf[...].astype(BF16)


def head_bucket(step, tail, q_in, r_in, log, heads, tails, live_groups, acc, hf, rf, qf, sf, qq):
    edges, (width, entities) = heads.shape[1], acc.shape
    half = edges // 2
    groups = [slice(g * half, (g + 1) * half) for g in range(2)]
    row = slice(step, step + 1)
    for g in groups:
        sf[:, g] = dot(tail[...], q_in[:, g], TN)
    terms = [softmax_terms(sf.at[:, g], log.at[:, k * 128:(k + 1) * 128], tails[row, g], qq.at[:, g])
             for k, g in enumerate(groups)]
    live = live_row(live_groups[:, row], edges)
    loss = jnp.concatenate([t[0] for t in terms], axis=1) * live
    for g in groups:
        hf[:, g] = dot(tail[...], qq[:, g], NN)
    rf[...] = r_in[...].astype(F32)
    for k, g in enumerate(groups):
        head_grad(hf.at[:, g], rf.at[:, g], terms[k][1] * live[:, g] * (1.0 / 256.0), qf.at[:, g])
    for g in groups:
        high, low = split(qf[:, g])
        head_hot = one_hot(heads[row, g], entities)
        acc[...] += dot(high, head_hot, NT) + dot(low, head_hot, NT)
    return loss, live


def far_terms(step, rel, lists, r_out, log_out, hot):
    r_out[...] = gather_relations(rel, unpacked(lists, RELS, step), hot)
    log_counts(halves(unpacked(lists, NEGS, step)), log_out.shape[0], log_out)


def tail_bucket(step, emb, head, lists, rf, log, acc, hf, qf, sf, qq):
    entities, edges = emb.shape[1], lists.shape[1]
    hf[...] = dot(head[...], one_hot(unpacked(lists, HEADS, step), entities), NN)
    make_query(hf, rf, qf)
    q = qf[...].astype(BF16)
    sf[...] = dot(emb[...], q, TN)
    loss, miss = softmax_terms(sf, log, unpacked(lists, TAILS, step), qq)
    scale = miss * live_row(live_counts(lists, step), edges) * (1.0 / 256.0)
    high, low = split(q.astype(F32) * scale)
    acc[...] += dot(high, qq[...], NT) + dot(low, qq[...], NT)


def heads2_kernel(prev2, q2, r2, log2, heads, tails, live_groups, part, sums, grad, sums_out, hf, rf, qf, sf, qq):
    loss, live = head_bucket(2, prev2, q2, r2, log2, heads, tails, live_groups, grad, hf, rf, qf, sf, qq)
    sums_out[0:1, :] = sums[0:1, :] + loss
    sums_out[1:2, :] = sums[1:2, :] + live


def heads1_kernel(sibling, swapped, q1, r1, log1, heads, tails, live_groups, part, sums, grad, row,
                  hf, rf, qf, sf, qq, prev1):
    prev1[...] = jnp.where(lax.axis_index("blk") & 1 == 0, swapped[...], sibling[...])
    loss, live = head_bucket(1, prev1, q1, r1, log1, heads, tails, live_groups, grad, hf, rf, qf, sf, qq)
    loss_all = jnp.sum(sums[0:1, :] + loss, axis=1, keepdims=True)
    live_all = jnp.sum(sums[1:2, :] + live, axis=1, keepdims=True)
    lane = lax.broadcasted_iota(jnp.int32, row.shape, 1)
    row[...] = jnp.where(lane == 0, loss_all, jnp.where(lane == 1, live_all, 0.0))


def after_kernel(block, lists, row, block_out, lists_out):
    pass


def tails2_kernel(rel, emb, next2, lists, part, grad, hot, hf, rf, qf, sf, qq, log):
    far_terms(2, rel, lists, rf, log, hot)
    tail_bucket(2, emb, next2, lists, rf, log, grad, hf, qf, sf, qq)


def tails1_kernel(rel, emb, sibling, swapped, sibling_lists, swapped_lists, part, row, grad,
                  hot, hf, rf, qf, sf, qq, acc, next1, lists, log):
    even = lax.axis_index("blk") & 1 == 0
    next1[...] = jnp.where(even, sibling[...], swapped[...])
    lists[...] = jnp.where(even, sibling_lists[...], swapped_lists[...])
    acc[...] = part[...]
    far_terms(1, rel, lists, rf, log, hot)
    tail_bucket(1, emb, next1, lists, rf, log, acc, hf, qf, sf, qq)
    grad[...] = acc[...].astype(BF16)


def add_kernel(row, other, out):
    out[...] = row[...] + other[...]


def rows_kernel(own, row, other, own_out, rows):
    rows[...] = jnp.broadcast_to(row[0:1, :] + other[0:1, :], rows.shape)


def finish_kernel(own, other, rows, grad, mean):
    grad[...] = own[...].astype(F32) + other[...].astype(F32)
    total = jnp.sum(rows[...], axis=0, keepdims=True)
    mean[...] = total[:, 0:1] / total[:, 1:2]


def kernel(body, outs, scratch, flops, spaces, mib=48, aliases={}):
    return pl.pallas_call(
        body,
        out_shape=[jax.ShapeDtypeStruct(s, t) for s, t in outs],
        in_specs=[pl.BlockSpec(memory_space=m) for m in spaces],
        input_output_aliases=aliases,
        scratch_shapes=[pltpu.VMEM(*s) if isinstance(s, tuple) else s for s in scratch],
        compiler_params=pltpu.CompilerParams(vmem_limit_bytes=mib * 2**20),
        cost_estimate=pl.CostEstimate(flops=flops, bytes_accessed=4 * 2**20, transcendentals=0),
    )


def shifted(x, by):
    peers = lax.axis_size("blk")
    return lax.ppermute(x, "blk", [(i, (i + by) % peers) for i in range(peers)])


def exchanged(x):
    return lax.ppermute(x, "blk", [(i, i ^ 1) for i in range(lax.axis_size("blk"))])


def per_device(embeddings, relations, heads, tails, rels, negatives, live):
    edges = heads.shape[1]
    entities, width = embeddings.shape
    n_rel = relations.shape[0]
    blocks = lax.axis_size("blk")
    emb = embeddings.T
    rel = relations.T
    here = pltpu.VMEM
    big, grads, logs, rows_of = (width, edges), (width, entities), (entities, 256), (8, 128)
    work = [(big, F32), (big, F32), (big, F32), ((entities, edges), F32), ((entities, edges), BF16)]
    hot = ((n_rel, edges), BF16)
    raw = (heads, tails, rels, negatives, live.T)
    prev2 = shifted(emb, 2)
    next2 = shifted(emb, -2)
    sibling = exchanged(emb)
    sent = ((EXTRA, edges), BF16)
    (lists,) = kernel(
        pack_kernel, [sent],
        [(x.shape, x.dtype) for x in raw] + [((EXTRA, edges), F32), pltpu.SemaphoreType.DMA((len(raw),))],
        2 * 10**9, [pltpu.HBM] * len(raw), 56,
    )(*raw)
    next2_lists = shifted(lists, -2)
    sibling_lists = exchanged(lists)
    part, sums, q1, q2, r1, r2, log1, log2 = kernel(
        prepare_kernel,
        [(grads, F32), ((8, edges), F32)] + [(big, BF16)] * 4 + [(logs, F32)] * 2,
        [hot] + work + [(logs, F32)], 20 * 10**9, [here] * 7)(emb, rel, *raw)
    own_lists = (heads, tails, live.T)
    swapped_prev = exchanged(prev2)
    part, sums = kernel(heads2_kernel, [(grads, F32), ((8, edges), F32)], work, 8 * 10**9, [here] * 9, aliases={7: 0})(
        prev2, q2, r2, log2, *own_lists, part, sums)
    part, row = kernel(heads1_kernel, [(grads, F32), (rows_of, F32)], work + [(big, BF16)], 3 * 10**9, [here] * 10, aliases={8: 0})(
        sibling, swapped_prev, q1, r1, log1, *own_lists, part, sums)
    core_row = exchanged(row)
    next2, next2_lists = kernel(after_kernel, [(big, BF16), sent], [], 10**6, [here] * 3, aliases={0: 0, 1: 1})(
        next2, next2_lists, row)
    swapped_next = exchanged(next2)
    swapped_lists = exchanged(next2_lists)
    (part,) = kernel(tails2_kernel, [(grads, F32)], [hot] + work + [(logs, F32)], 10 * 10**9, [here] * 5, aliases={4: 0})(
        rel, emb, next2, next2_lists, part)
    (row,) = kernel(add_kernel, [(rows_of, F32)], [], 10**6, [here] * 2)(row, core_row)
    rep_row = lax.ppermute(row, "rep", [(0, 1), (1, 0)])
    (own,) = kernel(
        tails1_kernel, [(grads, BF16)],
        [hot] + work + [(grads, F32), (big, BF16), sent, (logs, F32)], 10 * 10**9, [here] * 8,
    )(rel, emb, sibling, swapped_next, sibling_lists, swapped_lists, part, row)
    own, rows = kernel(rows_kernel, [(grads, BF16), ((blocks // 2, 128), F32)], [], 10**6, [here] * 3, aliases={0: 0})(
        own, row, rep_row)
    other = lax.ppermute(own, "rep", [(0, 1), (1, 0)])
    rows = lax.all_to_all(rows, "blk", 0, 0, tiled=True,
                          axis_index_groups=[[k + 2 * i for i in range(blocks // 2)] for k in (0, 1)])
    grad, mean = kernel(finish_kernel, [(grads, F32), ((1, 1), F32)], [], 10**6, [here] * 3)(own, other, rows)
    return grad.T, mean[0, 0]


def solution(mesh):
    placed = (
        P("blk", None),
        P(),
        P(None, ("blk", "rep")),
        P(None, ("blk", "rep")),
        P(None, ("blk", "rep")),
        P(None, ("blk", "rep"), None),
        P(None, ("blk", "rep")),
    )
    return jax.shard_map(
        per_device, mesh=mesh, in_specs=placed, out_specs=(P("blk", None), P()), check_vma=False
    )
```

```python
import jax
import jax.numpy as jnp
from jax import lax
from jax.experimental import pallas as pl
from jax.experimental.pallas import tpu as pltpu
from jax.sharding import PartitionSpec as P

STEPS = 3
F32 = jnp.float32
BF16 = jnp.bfloat16
NEVER = -1e30
TN = (((0,), (0,)), ((), ()))
NN = (((1,), (0,)), ((), ()))
NT = (((1,), (1,)), ((), ()))


def dot(a, b, dims):
    return lax.dot_general(a, b, dims, preferred_element_type=F32)


def one_hot(row, size):
    hit = lax.broadcasted_iota(jnp.int32, (size, row.shape[1]), 0) == row
    return jnp.where(hit, 1.0, 0.0).astype(BF16)


def gather_relations(rel_t, row, hot_ref):
    block = 256
    low = one_hot(row & (block - 1), block)
    high = row >> 8
    for j in range(rel_t.shape[1] // block):
        here = jnp.where(high == j, 1.0, 0.0).astype(BF16)
        hot_ref[j * block:(j + 1) * block, :] = low * here
    return dot(rel_t[...], hot_ref[...], NN)


def make_query(h_ref, r_ref, q_ref):
    half = h_ref.shape[0] // 2
    step = 40
    for c in range(0, half, step):
        re, im = slice(c, c + step), slice(half + c, half + c + step)
        h_re, h_im, r_re, r_im = h_ref[re, :], h_ref[im, :], r_ref[re, :], r_ref[im, :]
        q_ref[re, :] = h_re * r_re - h_im * r_im
        q_ref[im, :] = h_re * r_im + h_im * r_re


def head_grad(d_ref, r_ref, scale, out_ref):
    half = d_ref.shape[0] // 2
    step = 40
    for c in range(0, half, step):
        re, im = slice(c, c + step), slice(half + c, half + c + step)
        d_re, d_im, r_re, r_im = d_ref[re, :] * scale, d_ref[im, :] * scale, r_ref[re, :], r_ref[im, :]
        out_ref[re, :] = d_re * r_re + d_im * r_im
        out_ref[im, :] = d_im * r_re - d_re * r_im


def halves(row):
    half = row.shape[1] // 2
    return row[:, :half], row[:, half:]


def log_counts(neg_rows, entities, out_ref):
    for g, neg_row in enumerate(neg_rows):
        hot = one_hot(neg_row, entities)
        count = dot(hot, jnp.ones((neg_row.shape[1], 128), BF16), NN)
        out_ref[:, g * 128:(g + 1) * 128] = jnp.where(count > 0.5, jnp.log(jnp.maximum(count, 1.0)), NEVER)


def softmax_terms(s_ref, log_ref, tail_row, q_ref):
    entities, edges = s_ref.shape
    step = 16384 // edges
    iota = lax.broadcasted_iota(jnp.int32, (step, edges), 0)
    top = jnp.full((8, edges), NEVER, F32)
    pos = jnp.zeros((8, edges), F32)
    for c in range(0, entities, step):
        s = s_ref[c:c + step, :]
        hit = jnp.where(iota == tail_row - c, s, 0.0)
        log = log_ref[c:c + step, :]
        tiles = edges // log.shape[1]
        log = jnp.concatenate([log[:, k // tiles * 128:k // tiles * 128 + 128] for k in range(edges // 128)], axis=1)
        s = s + log
        s_ref[c:c + step, :] = s
        for k in range(0, step, 8):
            pos = pos + hit[k:k + 8, :]
            top = jnp.maximum(top, s[k:k + 8, :])
    positive = jnp.sum(pos, axis=0, keepdims=True)
    top = jnp.max(top, axis=0, keepdims=True)
    total = jnp.zeros((8, edges), F32)
    for c in range(0, entities, step):
        e = jnp.exp(s_ref[c:c + step, :] - top)
        s_ref[c:c + step, :] = e
        for k in range(0, step, 8):
            total = total + e[k:k + 8, :]
    total = jnp.sum(total, axis=0, keepdims=True)
    share = 1.0 / total
    for c in range(0, entities, step):
        p = s_ref[c:c + step, :] * share
        q_ref[c:c + step, :] = jnp.where(iota == tail_row - c, p - 1.0, p).astype(BF16)
    gap = jnp.log(total) + top - positive
    low = jnp.exp(-jnp.abs(gap))
    loss = jnp.maximum(gap, 0.0) + jnp.log(1.0 + low)
    miss = jnp.where(gap >= 0.0, 1.0, low) / (1.0 + low)
    return loss, miss


def live_row(count, edges):
    group = jnp.where(lax.broadcasted_iota(jnp.int32, (1, edges), 1) < edges // 2, 0, 1)
    return jnp.where(group < count, 1.0, 0.0)


HEADS, TAILS, RELS, NEGS, LIVE, EXTRA = 0, 1, 2, 3, 16, 32


def unpacked(lists, kind, step):
    rows = lists[...].astype(F32)
    k = (kind * 2 + step - 1) * 2
    return (rows[k:k + 1, :] * 256.0 + rows[k + 1:k + 2, :]).astype(jnp.int32)


def live_counts(lists, step):
    k = LIVE + step - 1
    return lists[...].astype(F32)[k:k + 1, :].astype(jnp.int32)


def split(x):
    high = x.astype(BF16)
    return high, (x - high.astype(F32)).astype(BF16)


def pack_kernel(heads_in, tails_in, rels_in, negatives_in, live_in, packed,
                heads, tails, rels, negatives, live_groups, rows, sems):
    pairs = ((heads_in, heads), (tails_in, tails), (rels_in, rels), (negatives_in, negatives), (live_in, live_groups))
    copies = [pltpu.make_async_copy(a, b, sems.at[k]) for k, (a, b) in enumerate(pairs)]
    for copy in copies:
        copy.start()
    for copy in copies:
        copy.wait()
    edges = heads.shape[1]
    half = edges // 2
    rows[...] = jnp.zeros(rows.shape, F32)
    for step in (1, 2):
        for kind, ref in ((HEADS, heads), (TAILS, tails), (RELS, rels)):
            k = (kind * 2 + step - 1) * 2
            row = ref[step:step + 1, :]
            rows[k:k + 1, :] = (row >> 8).astype(F32)
            rows[k + 1:k + 2, :] = (row & 255).astype(F32)
        k = (NEGS * 2 + step - 1) * 2
        for g in range(2):
            row = negatives[step, g:g + 1, :]
            rows[k:k + 1, g * half:(g + 1) * half] = (row >> 8).astype(F32)
            rows[k + 1:k + 2, g * half:(g + 1) * half] = (row & 255).astype(F32)
        k = LIVE + step - 1
        rows[k:k + 1, :] = jnp.broadcast_to(live_groups[:, step:step + 1], (1, edges)).astype(F32)
    packed[...] = rows[...].astype(BF16)


def prepare_kernel(emb, rel, heads, tails, rels, negatives, live_groups, grad, sums, q1, q2, r1, r2, log1, log2, hot, hf, rf, qf, sf, qq, log):
    edges, entities = heads.shape[1], emb.shape[1]
    head_hot = one_hot(heads[0:1, :], entities)
    hf[...] = dot(emb[...], head_hot, NN)
    rf[...] = gather_relations(rel, rels[0:1, :], hot)
    make_query(hf, rf, qf)
    q = qf[...].astype(BF16)
    sf[...] = dot(emb[...], q, TN)
    log_counts([negatives[0, g:g + 1, :] for g in range(2)], entities, log)
    loss, miss = softmax_terms(sf, log, tails[0:1, :], qq)
    live = live_row(live_groups[:, 0:1], edges)
    scale = miss * live * (1.0 / 256.0)
    high, low = split(q.astype(F32) * scale)
    g = dot(high, qq[...], NT) + dot(low, qq[...], NT)
    hf[...] = dot(emb[...], qq[...], NN)
    head_grad(hf, rf, scale, qf)
    high, low = split(qf[...])
    grad[...] = g + dot(high, head_hot, NT) + dot(low, head_hot, NT)
    sums[0:1, :] = loss * live
    sums[1:2, :] = live
    for step, q_out, r_out, log_out in ((1, q1, r1, log1), (2, q2, r2, log2)):
        rf[...] = gather_relations(rel, rels[step:step + 1, :], hot)
        hf[...] = dot(emb[...], one_hot(heads[step:step + 1, :], entities), NN)
        make_query(hf, rf, qf)
        log_counts([negatives[step, g:g + 1, :] for g in range(2)], entities, log_out)
        r_out[...] = rf[...].astype(BF16)
        q_out[...] = qf[...].astype(BF16)


def head_bucket(step, tail, q_in, r_in, log, heads, tails, live_groups, acc, hf, rf, qf, sf, qq):
    edges, (width, entities) = heads.shape[1], acc.shape
    half = edges // 2
    groups = [slice(g * half, (g + 1) * half) for g in range(2)]
    row = slice(step, step + 1)
    for g in groups:
        sf[:, g] = dot(tail[...], q_in[:, g], TN)
    terms = [softmax_terms(sf.at[:, g], log.at[:, k * 128:(k + 1) * 128], tails[row, g], qq.at[:, g])
             for k, g in enumerate(groups)]
    live = live_row(live_groups[:, row], edges)
    loss = jnp.concatenate([t[0] for t in terms], axis=1) * live
    for g in groups:
        hf[:, g] = dot(tail[...], qq[:, g], NN)
    rf[...] = r_in[...].astype(F32)
    for k, g in enumerate(groups):
        head_grad(hf.at[:, g], rf.at[:, g], terms[k][1] * live[:, g] * (1.0 / 256.0), qf.at[:, g])
    for g in groups:
        high, low = split(qf[:, g])
        head_hot = one_hot(heads[row, g], entities)
        acc[...] += dot(high, head_hot, NT) + dot(low, head_hot, NT)
    return loss, live


def far_terms(step, rel, lists, r_out, log_out, hot):
    r_out[...] = gather_relations(rel, unpacked(lists, RELS, step), hot)
    log_counts(halves(unpacked(lists, NEGS, step)), log_out.shape[0], log_out)


def tail_bucket(step, emb, head, lists, rf, log, acc, hf, qf, sf, qq):
    entities, edges = emb.shape[1], lists.shape[1]
    hf[...] = dot(head[...], one_hot(unpacked(lists, HEADS, step), entities), NN)
    make_query(hf, rf, qf)
    q = qf[...].astype(BF16)
    sf[...] = dot(emb[...], q, TN)
    loss, miss = softmax_terms(sf, log, unpacked(lists, TAILS, step), qq)
    scale = miss * live_row(live_counts(lists, step), edges) * (1.0 / 256.0)
    high, low = split(q.astype(F32) * scale)
    acc[...] += dot(high, qq[...], NT) + dot(low, qq[...], NT)


def heads2_kernel(prev2, q2, r2, log2, heads, tails, live_groups, part, sums, grad, sums_out, hf, rf, qf, sf, qq):
    loss, live = head_bucket(2, prev2, q2, r2, log2, heads, tails, live_groups, grad, hf, rf, qf, sf, qq)
    sums_out[0:1, :] = sums[0:1, :] + loss
    sums_out[1:2, :] = sums[1:2, :] + live


def heads1_kernel(prev1, q1, r1, log1, heads, tails, live_groups, part, sums, grad, row, hf, rf, qf, sf, qq):
    loss, live = head_bucket(1, prev1, q1, r1, log1, heads, tails, live_groups, grad, hf, rf, qf, sf, qq)
    loss_all = jnp.sum(sums[0:1, :] + loss, axis=1, keepdims=True)
    live_all = jnp.sum(sums[1:2, :] + live, axis=1, keepdims=True)
    lane = lax.broadcasted_iota(jnp.int32, row.shape, 1)
    row[...] = jnp.where(lane == 0, loss_all, jnp.where(lane == 1, live_all, 0.0))


def choose_kernel(emb, prev2, passed):
    passed[...] = jnp.where(lax.axis_index("blk") & 1 == 0, emb[...], prev2[...])


def after_kernel(block, lists, emb, own_lists, row, block_out, lists_out, passed, passed_lists):
    even = lax.axis_index("blk") & 1 == 0
    passed[...] = jnp.where(even, block[...], emb[...])
    passed_lists[...] = jnp.where(even, lists[...], own_lists[...])


def tails2_kernel(rel, emb, next2, lists, part, grad, hot, hf, rf, qf, sf, qq, log):
    far_terms(2, rel, lists, rf, log, hot)
    tail_bucket(2, emb, next2, lists, rf, log, grad, hf, qf, sf, qq)


def tails1_kernel(rel, emb, next1, lists, part, row, grad, hot, hf, rf, qf, sf, qq, acc, log):
    acc[...] = part[...]
    far_terms(1, rel, lists, rf, log, hot)
    tail_bucket(1, emb, next1, lists, rf, log, acc, hf, qf, sf, qq)
    grad[...] = acc[...].astype(BF16)


def add_kernel(row, other, out):
    out[...] = row[...] + other[...]


def rows_kernel(own, row, other, own_out, rows):
    rows[...] = jnp.broadcast_to(row[0:1, :] + other[0:1, :], rows.shape)


def finish_kernel(own, other, rows, grad, mean):
    grad[...] = own[...].astype(F32) + other[...].astype(F32)
    total = jnp.sum(rows[...], axis=0, keepdims=True)
    mean[...] = total[:, 0:1] / total[:, 1:2]


def kernel(body, outs, scratch, flops, spaces, mib=48, aliases={}):
    return pl.pallas_call(
        body,
        out_shape=[jax.ShapeDtypeStruct(s, t) for s, t in outs],
        in_specs=[pl.BlockSpec(memory_space=m) for m in spaces],
        input_output_aliases=aliases,
        scratch_shapes=[pltpu.VMEM(*s) if isinstance(s, tuple) else s for s in scratch],
        compiler_params=pltpu.CompilerParams(vmem_limit_bytes=mib * 2**20),
        cost_estimate=pl.CostEstimate(flops=flops, bytes_accessed=4 * 2**20, transcendentals=0),
    )


def shifted(x, by):
    peers = lax.axis_size("blk")
    return lax.ppermute(x, "blk", [(i, (i + by) % peers) for i in range(peers)])


def exchanged(x):
    return lax.ppermute(x, "blk", [(i, i ^ 1) for i in range(lax.axis_size("blk"))])


def per_device(embeddings, relations, heads, tails, rels, negatives, live):
    edges = heads.shape[1]
    entities, width = embeddings.shape
    n_rel = relations.shape[0]
    blocks = lax.axis_size("blk")
    emb = embeddings.T
    rel = relations.T
    here = pltpu.VMEM
    big, grads, logs, rows_of = (width, edges), (width, entities), (entities, 256), (8, 128)
    work = [(big, F32), (big, F32), (big, F32), ((entities, edges), F32), ((entities, edges), BF16)]
    hot = ((n_rel, edges), BF16)
    raw = (heads, tails, rels, negatives, live.T)
    prev2 = shifted(emb, 2)
    next2 = shifted(emb, -2)
    sent = ((EXTRA, edges), BF16)
    (lists,) = kernel(
        pack_kernel, [sent],
        [(x.shape, x.dtype) for x in raw] + [((EXTRA, edges), F32), pltpu.SemaphoreType.DMA((len(raw),))],
        2 * 10**9, [pltpu.HBM] * len(raw), 56,
    )(*raw)
    next2_lists = shifted(lists, -2)
    part, sums, q1, q2, r1, r2, log1, log2 = kernel(
        prepare_kernel,
        [(grads, F32), ((8, edges), F32)] + [(big, BF16)] * 4 + [(logs, F32)] * 2,
        [hot] + work + [(logs, F32)], 20 * 10**9, [here] * 7)(emb, rel, *raw)
    own_lists = (heads, tails, live.T)
    (passed,) = kernel(choose_kernel, [(big, BF16)], [], 10**6, [here] * 2)(emb, prev2)
    prev1 = exchanged(passed)
    part, sums = kernel(heads2_kernel, [(grads, F32), ((8, edges), F32)], work, 8 * 10**9, [here] * 9, aliases={7: 0})(
        prev2, q2, r2, log2, *own_lists, part, sums)
    part, row = kernel(heads1_kernel, [(grads, F32), (rows_of, F32)], work, 3 * 10**9, [here] * 9, aliases={7: 0})(
        prev1, q1, r1, log1, *own_lists, part, sums)
    core_row = exchanged(row)
    next2, next2_lists, passed, passed_lists = kernel(
        after_kernel, [(big, BF16), sent] * 2, [], 10**6, [here] * 5, aliases={0: 0, 1: 1})(
        next2, next2_lists, emb, lists, row)
    next1 = exchanged(passed)
    lists1 = exchanged(passed_lists)
    (part,) = kernel(tails2_kernel, [(grads, F32)], [hot] + work + [(logs, F32)], 10 * 10**9, [here] * 5, aliases={4: 0})(
        rel, emb, next2, next2_lists, part)
    (row,) = kernel(add_kernel, [(rows_of, F32)], [], 10**6, [here] * 2)(row, core_row)
    rep_row = lax.ppermute(row, "rep", [(0, 1), (1, 0)])
    (own,) = kernel(
        tails1_kernel, [(grads, BF16)],
        [hot] + work + [(grads, F32), (logs, F32)], 10 * 10**9, [here] * 6,
    )(rel, emb, next1, lists1, part, row)
    own, rows = kernel(rows_kernel, [(grads, BF16), ((blocks // 2, 128), F32)], [], 10**6, [here] * 3, aliases={0: 0})(
        own, row, rep_row)
    other = lax.ppermute(own, "rep", [(0, 1), (1, 0)])
    rows = lax.all_to_all(rows, "blk", 0, 0, tiled=True,
                          axis_index_groups=[[k + 2 * i for i in range(blocks // 2)] for k in (0, 1)])
    grad, mean = kernel(finish_kernel, [(grads, F32), ((1, 1), F32)], [], 10**6, [here] * 3)(own, other, rows)
    return grad.T, mean[0, 0]


def solution(mesh):
    placed = (
        P("blk", None),
        P(),
        P(None, ("blk", "rep")),
        P(None, ("blk", "rep")),
        P(None, ("blk", "rep")),
        P(None, ("blk", "rep"), None),
        P(None, ("blk", "rep")),
    )
    return jax.shard_map(
        per_device, mesh=mesh, in_specs=placed, out_specs=(P("blk", None), P()), check_vma=False
    )
```

```python
import jax
import jax.numpy as jnp
from jax import lax
from jax.experimental import pallas as pl
from jax.experimental.pallas import tpu as pltpu
from jax.sharding import PartitionSpec as P

STEPS = 3
F32 = jnp.float32
BF16 = jnp.bfloat16
NEVER = -1e30
TN = (((0,), (0,)), ((), ()))
NN = (((1,), (0,)), ((), ()))
NT = (((1,), (1,)), ((), ()))


def dot(a, b, dims):
    return lax.dot_general(a, b, dims, preferred_element_type=F32)


def one_hot(row, size):
    hit = lax.broadcasted_iota(jnp.int32, (size, row.shape[1]), 0) == row
    return jnp.where(hit, 1.0, 0.0).astype(BF16)


def gather_relations(rel_t, row, hot_ref):
    block = 256
    low = one_hot(row & (block - 1), block)
    high = row >> 8
    for j in range(rel_t.shape[1] // block):
        here = jnp.where(high == j, 1.0, 0.0).astype(BF16)
        hot_ref[j * block:(j + 1) * block, :] = low * here
    return dot(rel_t[...], hot_ref[...], NN)


def make_query(h_ref, r_ref, q_ref):
    half = h_ref.shape[0] // 2
    step = 40
    for c in range(0, half, step):
        re, im = slice(c, c + step), slice(half + c, half + c + step)
        h_re, h_im, r_re, r_im = h_ref[re, :], h_ref[im, :], r_ref[re, :], r_ref[im, :]
        q_ref[re, :] = h_re * r_re - h_im * r_im
        q_ref[im, :] = h_re * r_im + h_im * r_re


def head_grad(d_ref, r_ref, scale, out_ref):
    half = d_ref.shape[0] // 2
    step = 40
    for c in range(0, half, step):
        re, im = slice(c, c + step), slice(half + c, half + c + step)
        d_re, d_im, r_re, r_im = d_ref[re, :] * scale, d_ref[im, :] * scale, r_ref[re, :], r_ref[im, :]
        out_ref[re, :] = d_re * r_re + d_im * r_im
        out_ref[im, :] = d_im * r_re - d_re * r_im


def halves(row):
    half = row.shape[1] // 2
    return row[:, :half], row[:, half:]


def log_counts(neg_rows, entities, out_ref):
    for g, neg_row in enumerate(neg_rows):
        hot = one_hot(neg_row, entities)
        count = dot(hot, jnp.ones((neg_row.shape[1], 128), BF16), NN)
        out_ref[:, g * 128:(g + 1) * 128] = jnp.where(count > 0.5, jnp.log(jnp.maximum(count, 1.0)), NEVER)


def softmax_terms(s_ref, log_ref, tail_row, q_ref):
    entities, edges = s_ref.shape
    step = 16384 // edges
    iota = lax.broadcasted_iota(jnp.int32, (step, edges), 0)
    top = jnp.full((8, edges), NEVER, F32)
    pos = jnp.zeros((8, edges), F32)
    for c in range(0, entities, step):
        s = s_ref[c:c + step, :]
        hit = jnp.where(iota == tail_row - c, s, 0.0)
        log = log_ref[c:c + step, :]
        tiles = edges // log.shape[1]
        log = jnp.concatenate([log[:, k // tiles * 128:k // tiles * 128 + 128] for k in range(edges // 128)], axis=1)
        s = s + log
        s_ref[c:c + step, :] = s
        for k in range(0, step, 8):
            pos = pos + hit[k:k + 8, :]
            top = jnp.maximum(top, s[k:k + 8, :])
    positive = jnp.sum(pos, axis=0, keepdims=True)
    top = jnp.max(top, axis=0, keepdims=True)
    total = jnp.zeros((8, edges), F32)
    for c in range(0, entities, step):
        e = jnp.exp(s_ref[c:c + step, :] - top)
        s_ref[c:c + step, :] = e
        for k in range(0, step, 8):
            total = total + e[k:k + 8, :]
    total = jnp.sum(total, axis=0, keepdims=True)
    share = 1.0 / total
    for c in range(0, entities, step):
        p = s_ref[c:c + step, :] * share
        q_ref[c:c + step, :] = jnp.where(iota == tail_row - c, p - 1.0, p).astype(BF16)
    gap = jnp.log(total) + top - positive
    low = jnp.exp(-jnp.abs(gap))
    loss = jnp.maximum(gap, 0.0) + jnp.log(1.0 + low)
    miss = jnp.where(gap >= 0.0, 1.0, low) / (1.0 + low)
    return loss, miss


def live_row(count, edges):
    group = jnp.where(lax.broadcasted_iota(jnp.int32, (1, edges), 1) < edges // 2, 0, 1)
    return jnp.where(group < count, 1.0, 0.0)


HEADS, TAILS, RELS, NEGS, LIVE, EXTRA = 0, 1, 2, 3, 16, 32


def unpacked(lists, kind, step):
    rows = lists[...].astype(F32)
    k = (kind * 2 + step - 1) * 2
    return (rows[k:k + 1, :] * 256.0 + rows[k + 1:k + 2, :]).astype(jnp.int32)


def live_counts(lists, step):
    k = LIVE + step - 1
    return lists[...].astype(F32)[k:k + 1, :].astype(jnp.int32)


def split(x):
    high = x.astype(BF16)
    return high, (x - high.astype(F32)).astype(BF16)


def pack_kernel(heads_in, tails_in, rels_in, negatives_in, live_in, packed,
                heads, tails, rels, negatives, live_groups, rows, sems):
    pairs = ((heads_in, heads), (tails_in, tails), (rels_in, rels), (negatives_in, negatives), (live_in, live_groups))
    copies = [pltpu.make_async_copy(a, b, sems.at[k]) for k, (a, b) in enumerate(pairs)]
    for copy in copies:
        copy.start()
    for copy in copies:
        copy.wait()
    edges = heads.shape[1]
    half = edges // 2
    rows[...] = jnp.zeros(rows.shape, F32)
    for step in (1, 2):
        for kind, ref in ((HEADS, heads), (TAILS, tails), (RELS, rels)):
            k = (kind * 2 + step - 1) * 2
            row = ref[step:step + 1, :]
            rows[k:k + 1, :] = (row >> 8).astype(F32)
            rows[k + 1:k + 2, :] = (row & 255).astype(F32)
        k = (NEGS * 2 + step - 1) * 2
        for g in range(2):
            row = negatives[step, g:g + 1, :]
            rows[k:k + 1, g * half:(g + 1) * half] = (row >> 8).astype(F32)
            rows[k + 1:k + 2, g * half:(g + 1) * half] = (row & 255).astype(F32)
        k = LIVE + step - 1
        rows[k:k + 1, :] = jnp.broadcast_to(live_groups[:, step:step + 1], (1, edges)).astype(F32)
    packed[...] = rows[...].astype(BF16)


def prepare_kernel(emb, rel, heads, tails, rels, negatives, live_groups, grad, sums, q1, q2, r1, r2, log1, log2, hot, hf, rf, qf, sf, qq, log):
    edges, entities = heads.shape[1], emb.shape[1]
    head_hot = one_hot(heads[0:1, :], entities)
    hf[...] = dot(emb[...], head_hot, NN)
    rf[...] = gather_relations(rel, rels[0:1, :], hot)
    make_query(hf, rf, qf)
    q = qf[...].astype(BF16)
    sf[...] = dot(emb[...], q, TN)
    log_counts([negatives[0, g:g + 1, :] for g in range(2)], entities, log)
    loss, miss = softmax_terms(sf, log, tails[0:1, :], qq)
    live = live_row(live_groups[:, 0:1], edges)
    scale = miss * live * (1.0 / 256.0)
    high, low = split(q.astype(F32) * scale)
    g = dot(high, qq[...], NT) + dot(low, qq[...], NT)
    hf[...] = dot(emb[...], qq[...], NN)
    head_grad(hf, rf, scale, qf)
    high, low = split(qf[...])
    grad[...] = g + dot(high, head_hot, NT) + dot(low, head_hot, NT)
    sums[0:1, :] = loss * live
    sums[1:2, :] = live
    for step, q_out, r_out, log_out in ((1, q1, r1, log1), (2, q2, r2, log2)):
        rf[...] = gather_relations(rel, rels[step:step + 1, :], hot)
        hf[...] = dot(emb[...], one_hot(heads[step:step + 1, :], entities), NN)
        make_query(hf, rf, qf)
        log_counts([negatives[step, g:g + 1, :] for g in range(2)], entities, log_out)
        r_out[...] = rf[...].astype(BF16)
        q_out[...] = qf[...].astype(BF16)


def head_bucket(step, tail, q_in, r_in, log, heads, tails, live_groups, acc, hf, rf, qf, sf, qq):
    edges, (width, entities) = heads.shape[1], acc.shape
    half = edges // 2
    groups = [slice(g * half, (g + 1) * half) for g in range(2)]
    row = slice(step, step + 1)
    for g in groups:
        sf[:, g] = dot(tail[...], q_in[:, g], TN)
    terms = [softmax_terms(sf.at[:, g], log.at[:, k * 128:(k + 1) * 128], tails[row, g], qq.at[:, g])
             for k, g in enumerate(groups)]
    live = live_row(live_groups[:, row], edges)
    loss = jnp.concatenate([t[0] for t in terms], axis=1) * live
    for g in groups:
        hf[:, g] = dot(tail[...], qq[:, g], NN)
    rf[...] = r_in[...].astype(F32)
    for k, g in enumerate(groups):
        head_grad(hf.at[:, g], rf.at[:, g], terms[k][1] * live[:, g] * (1.0 / 256.0), qf.at[:, g])
    for g in groups:
        high, low = split(qf[:, g])
        head_hot = one_hot(heads[row, g], entities)
        acc[...] += dot(high, head_hot, NT) + dot(low, head_hot, NT)
    return loss, live


def far_terms(step, rel, lists, r_out, log_out, hot):
    r_out[...] = gather_relations(rel, unpacked(lists, RELS, step), hot)
    log_counts(halves(unpacked(lists, NEGS, step)), log_out.shape[0], log_out)


def tail_bucket(step, emb, head, lists, rf, log, acc, hf, qf, sf, qq):
    entities, edges = emb.shape[1], lists.shape[1]
    hf[...] = dot(head[...], one_hot(unpacked(lists, HEADS, step), entities), NN)
    make_query(hf, rf, qf)
    q = qf[...].astype(BF16)
    sf[...] = dot(emb[...], q, TN)
    loss, miss = softmax_terms(sf, log, unpacked(lists, TAILS, step), qq)
    scale = miss * live_row(live_counts(lists, step), edges) * (1.0 / 256.0)
    high, low = split(q.astype(F32) * scale)
    acc[...] += dot(high, qq[...], NT) + dot(low, qq[...], NT)


def heads2_kernel(prev2, q2, r2, log2, heads, tails, live_groups, part, sums, grad, sums_out, hf, rf, qf, sf, qq):
    loss, live = head_bucket(2, prev2, q2, r2, log2, heads, tails, live_groups, grad, hf, rf, qf, sf, qq)
    sums_out[0:1, :] = sums[0:1, :] + loss
    sums_out[1:2, :] = sums[1:2, :] + live


def heads1_kernel(prev1, q1, r1, log1, heads, tails, live_groups, part, sums, grad, row, hf, rf, qf, sf, qq):
    loss, live = head_bucket(1, prev1, q1, r1, log1, heads, tails, live_groups, grad, hf, rf, qf, sf, qq)
    loss_all = jnp.sum(sums[0:1, :] + loss, axis=1, keepdims=True)
    live_all = jnp.sum(sums[1:2, :] + live, axis=1, keepdims=True)
    lane = lax.broadcasted_iota(jnp.int32, row.shape, 1)
    row[...] = jnp.where(lane == 0, loss_all, jnp.where(lane == 1, live_all, 0.0))


def choose_kernel(emb, prev2, passed):
    passed[...] = jnp.where(lax.axis_index("blk") & 1 == 0, emb[...], prev2[...])


def after_kernel(block, lists, emb, own_lists, row, block_out, lists_out, passed, passed_lists):
    even = lax.axis_index("blk") & 1 == 0
    passed[...] = jnp.where(even, block[...], emb[...])
    passed_lists[...] = jnp.where(even, lists[...], own_lists[...])


def tails2_kernel(rel, emb, next2, lists, part, grad, hot, hf, rf, qf, sf, qq, log):
    far_terms(2, rel, lists, rf, log, hot)
    tail_bucket(2, emb, next2, lists, rf, log, grad, hf, qf, sf, qq)


def tails1_kernel(rel, emb, next1, lists, part, row, grad, hot, hf, rf, qf, sf, qq, acc, log):
    acc[...] = part[...]
    far_terms(1, rel, lists, rf, log, hot)
    tail_bucket(1, emb, next1, lists, rf, log, acc, hf, qf, sf, qq)
    grad[...] = acc[...].astype(BF16)


def add_kernel(row, other, out):
    out[...] = row[...] + other[...]


def rows_kernel(own, row, other, own_out, rows):
    rows[...] = jnp.broadcast_to(row[0:1, :] + other[0:1, :], rows.shape)


def finish_kernel(own, other, rows, grad, mean):
    grad[...] = own[...].astype(F32) + other[...].astype(F32)
    total = jnp.sum(rows[...], axis=0, keepdims=True)
    mean[...] = total[:, 0:1] / total[:, 1:2]


def kernel(body, outs, scratch, flops, spaces, mib=48, aliases={}):
    return pl.pallas_call(
        body,
        out_shape=[jax.ShapeDtypeStruct(s, t) for s, t in outs],
        in_specs=[pl.BlockSpec(memory_space=m) for m in spaces],
        input_output_aliases=aliases,
        scratch_shapes=[pltpu.VMEM(*s) if isinstance(s, tuple) else s for s in scratch],
        compiler_params=pltpu.CompilerParams(vmem_limit_bytes=mib * 2**20),
        cost_estimate=pl.CostEstimate(flops=flops, bytes_accessed=4 * 2**20, transcendentals=0),
    )


def shifted(x, by):
    peers = lax.axis_size("blk")
    return lax.ppermute(x, "blk", [(i, (i + by) % peers) for i in range(peers)])


def exchanged(x):
    return lax.ppermute(x, "blk", [(i, i ^ 1) for i in range(lax.axis_size("blk"))])


def per_device(embeddings, relations, heads, tails, rels, negatives, live):
    edges = heads.shape[1]
    entities, width = embeddings.shape
    n_rel = relations.shape[0]
    blocks = lax.axis_size("blk")
    emb = embeddings.T
    rel = relations.T
    here = pltpu.VMEM
    big, grads, logs, rows_of = (width, edges), (width, entities), (entities, 256), (8, 128)
    work = [(big, F32), (big, F32), (big, F32), ((entities, edges), F32), ((entities, edges), BF16)]
    hot = ((n_rel, edges), BF16)
    raw = (heads, tails, rels, negatives, live.T)
    prev2 = shifted(emb, 2)
    next2 = shifted(emb, -2)
    sent = ((EXTRA, edges), BF16)
    (lists,) = kernel(
        pack_kernel, [sent],
        [(x.shape, x.dtype) for x in raw] + [((EXTRA, edges), F32), pltpu.SemaphoreType.DMA((len(raw),))],
        2 * 10**9, [pltpu.HBM] * len(raw), 56,
    )(*raw)
    next2_lists = shifted(lists, -2)
    part, sums, q1, q2, r1, r2, log1, log2 = kernel(
        prepare_kernel,
        [(grads, F32), ((8, edges), F32)] + [(big, BF16)] * 4 + [(logs, F32)] * 2,
        [hot] + work + [(logs, F32)], 20 * 10**9, [here] * 7)(emb, rel, *raw)
    own_lists = (heads, tails, live.T)
    (passed,) = kernel(choose_kernel, [(big, BF16)], [], 10**6, [here] * 2)(emb, prev2)
    prev1 = exchanged(passed)
    part, sums = kernel(heads2_kernel, [(grads, F32), ((8, edges), F32)], work, 8 * 10**9, [here] * 9, aliases={7: 0})(
        prev2, q2, r2, log2, *own_lists, part, sums)
    part, row = kernel(heads1_kernel, [(grads, F32), (rows_of, F32)], work, 3 * 10**9, [here] * 9, aliases={7: 0})(
        prev1, q1, r1, log1, *own_lists, part, sums)
    core_row = exchanged(row)
    next2, next2_lists, passed, passed_lists = kernel(
        after_kernel, [(big, BF16), sent] * 2, [], 10**6, [here] * 5, aliases={0: 0, 1: 1})(
        next2, next2_lists, emb, lists, row)
    next1 = exchanged(passed)
    lists1 = exchanged(passed_lists)
    (part,) = kernel(tails2_kernel, [(grads, F32)], [hot] + work + [(logs, F32)], 10 * 10**9, [here] * 5, aliases={4: 0})(
        rel, emb, next2, next2_lists, part)
    (row,) = kernel(add_kernel, [(rows_of, F32)], [], 10**6, [here] * 2)(row, core_row)
    half_row = shifted(row, blocks // 2)
    (own,) = kernel(
        tails1_kernel, [(grads, BF16)],
        [hot] + work + [(grads, F32), (logs, F32)], 10 * 10**9, [here] * 6,
    )(rel, emb, next1, lists1, part, row)
    own, rows = kernel(rows_kernel, [(grads, BF16), ((blocks // 2, 128), F32)], [], 10**6, [here] * 3, aliases={0: 0})(
        own, row, half_row)
    other = lax.ppermute(own, "rep", [(0, 1), (1, 0)])
    rows = lax.all_to_all(rows, ("blk", "rep"), 0, 0, tiled=True, axis_index_groups=[
        [h * blocks + 4 * i + 2 * k + r for i in range(blocks // 4) for r in (0, 1)] for h in (0, 1) for k in (0, 1)])
    grad, mean = kernel(finish_kernel, [(grads, F32), ((1, 1), F32)], [], 10**6, [here] * 3)(own, other, rows)
    return grad.T, mean[0, 0]


def solution(mesh):
    placed = (
        P("blk", None),
        P(),
        P(None, ("blk", "rep")),
        P(None, ("blk", "rep")),
        P(None, ("blk", "rep")),
        P(None, ("blk", "rep"), None),
        P(None, ("blk", "rep")),
    )
    return jax.shard_map(
        per_device, mesh=mesh, in_specs=placed, out_specs=(P("blk", None), P()), check_vma=False
    )
```

```python
import jax
import jax.numpy as jnp
from jax import lax
from jax.experimental import pallas as pl
from jax.experimental.pallas import tpu as pltpu
from jax.sharding import PartitionSpec as P

STEPS = 3
F32 = jnp.float32
BF16 = jnp.bfloat16
NEVER = -1e30
TN = (((0,), (0,)), ((), ()))
NN = (((1,), (0,)), ((), ()))
NT = (((1,), (1,)), ((), ()))


def dot(a, b, dims):
    return lax.dot_general(a, b, dims, preferred_element_type=F32)


def one_hot(row, size):
    hit = lax.broadcasted_iota(jnp.int32, (size, row.shape[1]), 0) == row
    return jnp.where(hit, 1.0, 0.0).astype(BF16)


def gather_relations(rel_t, row, hot_ref):
    block = 256
    low = one_hot(row & (block - 1), block)
    high = row >> 8
    for j in range(rel_t.shape[1] // block):
        here = jnp.where(high == j, 1.0, 0.0).astype(BF16)
        hot_ref[j * block:(j + 1) * block, :] = low * here
    return dot(rel_t[...], hot_ref[...], NN)


def make_query(h_ref, r_ref, q_ref):
    half = h_ref.shape[0] // 2
    step = 40
    for c in range(0, half, step):
        re, im = slice(c, c + step), slice(half + c, half + c + step)
        h_re, h_im, r_re, r_im = h_ref[re, :], h_ref[im, :], r_ref[re, :], r_ref[im, :]
        q_ref[re, :] = h_re * r_re - h_im * r_im
        q_ref[im, :] = h_re * r_im + h_im * r_re


def head_grad(d_ref, r_ref, scale, out_ref):
    half = d_ref.shape[0] // 2
    step = 40
    for c in range(0, half, step):
        re, im = slice(c, c + step), slice(half + c, half + c + step)
        d_re, d_im, r_re, r_im = d_ref[re, :] * scale, d_ref[im, :] * scale, r_ref[re, :], r_ref[im, :]
        out_ref[re, :] = d_re * r_re + d_im * r_im
        out_ref[im, :] = d_im * r_re - d_re * r_im


def halves(row):
    half = row.shape[1] // 2
    return row[:, :half], row[:, half:]


def log_counts(neg_rows, entities, out_ref):
    for g, neg_row in enumerate(neg_rows):
        hot = one_hot(neg_row, entities)
        count = dot(hot, jnp.ones((neg_row.shape[1], 128), BF16), NN)
        out_ref[:, g * 128:(g + 1) * 128] = jnp.where(count > 0.5, jnp.log(jnp.maximum(count, 1.0)), NEVER)


def softmax_terms(s_ref, log_ref, tail_row, q_ref):
    entities, edges = s_ref.shape
    step = 16384 // edges
    iota = lax.broadcasted_iota(jnp.int32, (step, edges), 0)
    top = jnp.full((8, edges), NEVER, F32)
    pos = jnp.zeros((8, edges), F32)
    for c in range(0, entities, step):
        s = s_ref[c:c + step, :]
        hit = jnp.where(iota == tail_row - c, s, 0.0)
        log = log_ref[c:c + step, :]
        tiles = edges // log.shape[1]
        log = jnp.concatenate([log[:, k // tiles * 128:k // tiles * 128 + 128] for k in range(edges // 128)], axis=1)
        s = s + log
        s_ref[c:c + step, :] = s
        for k in range(0, step, 8):
            pos = pos + hit[k:k + 8, :]
            top = jnp.maximum(top, s[k:k + 8, :])
    positive = jnp.sum(pos, axis=0, keepdims=True)
    top = jnp.max(top, axis=0, keepdims=True)
    total = jnp.zeros((8, edges), F32)
    for c in range(0, entities, step):
        e = jnp.exp(s_ref[c:c + step, :] - top)
        s_ref[c:c + step, :] = e
        for k in range(0, step, 8):
            total = total + e[k:k + 8, :]
    total = jnp.sum(total, axis=0, keepdims=True)
    share = 1.0 / total
    for c in range(0, entities, step):
        p = s_ref[c:c + step, :] * share
        q_ref[c:c + step, :] = jnp.where(iota == tail_row - c, p - 1.0, p).astype(BF16)
    gap = jnp.log(total) + top - positive
    low = jnp.exp(-jnp.abs(gap))
    loss = jnp.maximum(gap, 0.0) + jnp.log(1.0 + low)
    miss = jnp.where(gap >= 0.0, 1.0, low) / (1.0 + low)
    return loss, miss


def live_row(count, edges):
    group = jnp.where(lax.broadcasted_iota(jnp.int32, (1, edges), 1) < edges // 2, 0, 1)
    return jnp.where(group < count, 1.0, 0.0)


HEADS, TAILS, RELS, NEGS, LIVE, EXTRA = 0, 1, 2, 3, 16, 32


def unpacked(lists, kind, step):
    rows = lists[...].astype(F32)
    k = (kind * 2 + step - 1) * 2
    return (rows[k:k + 1, :] * 256.0 + rows[k + 1:k + 2, :]).astype(jnp.int32)


def live_counts(lists, step):
    k = LIVE + step - 1
    return lists[...].astype(F32)[k:k + 1, :].astype(jnp.int32)


def split(x):
    high = x.astype(BF16)
    return high, (x - high.astype(F32)).astype(BF16)


def pack_kernel(heads_in, tails_in, rels_in, negatives_in, live_in, packed,
                heads, tails, rels, negatives, live_groups, rows, sems):
    pairs = ((heads_in, heads), (tails_in, tails), (rels_in, rels), (negatives_in, negatives), (live_in, live_groups))
    copies = [pltpu.make_async_copy(a, b, sems.at[k]) for k, (a, b) in enumerate(pairs)]
    for copy in copies:
        copy.start()
    for copy in copies:
        copy.wait()
    edges = heads.shape[1]
    half = edges // 2
    rows[...] = jnp.zeros(rows.shape, F32)
    for step in (1, 2):
        for kind, ref in ((HEADS, heads), (TAILS, tails), (RELS, rels)):
            k = (kind * 2 + step - 1) * 2
            row = ref[step:step + 1, :]
            rows[k:k + 1, :] = (row >> 8).astype(F32)
            rows[k + 1:k + 2, :] = (row & 255).astype(F32)
        k = (NEGS * 2 + step - 1) * 2
        for g in range(2):
            row = negatives[step, g:g + 1, :]
            rows[k:k + 1, g * half:(g + 1) * half] = (row >> 8).astype(F32)
            rows[k + 1:k + 2, g * half:(g + 1) * half] = (row & 255).astype(F32)
        k = LIVE + step - 1
        rows[k:k + 1, :] = jnp.broadcast_to(live_groups[:, step:step + 1], (1, edges)).astype(F32)
    packed[...] = rows[...].astype(BF16)


def prepare_kernel(emb, rel, heads, tails, rels, negatives, live_groups, grad, sums, q1, q2, r1, r2, log1, log2, hot, hf, rf, qf, sf, qq, log):
    edges, entities = heads.shape[1], emb.shape[1]
    head_hot = one_hot(heads[0:1, :], entities)
    hf[...] = dot(emb[...], head_hot, NN)
    rf[...] = gather_relations(rel, rels[0:1, :], hot)
    make_query(hf, rf, qf)
    q = qf[...].astype(BF16)
    sf[...] = dot(emb[...], q, TN)
    log_counts([negatives[0, g:g + 1, :] for g in range(2)], entities, log)
    loss, miss = softmax_terms(sf, log, tails[0:1, :], qq)
    live = live_row(live_groups[:, 0:1], edges)
    scale = miss * live * (1.0 / 256.0)
    high, low = split(q.astype(F32) * scale)
    g = dot(high, qq[...], NT) + dot(low, qq[...], NT)
    hf[...] = dot(emb[...], qq[...], NN)
    head_grad(hf, rf, scale, qf)
    high, low = split(qf[...])
    grad[...] = g + dot(high, head_hot, NT) + dot(low, head_hot, NT)
    sums[0:1, :] = loss * live
    sums[1:2, :] = live
    for step, q_out, r_out, log_out in ((1, q1, r1, log1), (2, q2, r2, log2)):
        rf[...] = gather_relations(rel, rels[step:step + 1, :], hot)
        hf[...] = dot(emb[...], one_hot(heads[step:step + 1, :], entities), NN)
        make_query(hf, rf, qf)
        log_counts([negatives[step, g:g + 1, :] for g in range(2)], entities, log_out)
        r_out[...] = rf[...].astype(BF16)
        q_out[...] = qf[...].astype(BF16)


def head_bucket(step, tail, q_in, r_in, log, heads, tails, live_groups, acc, hf, rf, qf, sf, qq):
    edges, (width, entities) = heads.shape[1], acc.shape
    half = edges // 2
    groups = [slice(g * half, (g + 1) * half) for g in range(2)]
    row = slice(step, step + 1)
    for g in groups:
        sf[:, g] = dot(tail[...], q_in[:, g], TN)
    terms = [softmax_terms(sf.at[:, g], log.at[:, k * 128:(k + 1) * 128], tails[row, g], qq.at[:, g])
             for k, g in enumerate(groups)]
    live = live_row(live_groups[:, row], edges)
    loss = jnp.concatenate([t[0] for t in terms], axis=1) * live
    for g in groups:
        hf[:, g] = dot(tail[...], qq[:, g], NN)
    rf[...] = r_in[...].astype(F32)
    for k, g in enumerate(groups):
        head_grad(hf.at[:, g], rf.at[:, g], terms[k][1] * live[:, g] * (1.0 / 256.0), qf.at[:, g])
    for g in groups:
        high, low = split(qf[:, g])
        head_hot = one_hot(heads[row, g], entities)
        acc[...] += dot(high, head_hot, NT) + dot(low, head_hot, NT)
    return loss, live


def far_terms(step, rel, lists, r_out, log_out, hot):
    r_out[...] = gather_relations(rel, unpacked(lists, RELS, step), hot)
    log_counts(halves(unpacked(lists, NEGS, step)), log_out.shape[0], log_out)


def tail_bucket(step, emb, head, lists, rf, log, hf, qf, sf, qq):
    entities, edges = emb.shape[1], lists.shape[1]
    hf[...] = dot(head[...], one_hot(unpacked(lists, HEADS, step), entities), NN)
    make_query(hf, rf, qf)
    q = qf[...].astype(BF16)
    sf[...] = dot(emb[...], q, TN)
    loss, miss = softmax_terms(sf, log, unpacked(lists, TAILS, step), qq)
    scale = miss * live_row(live_counts(lists, step), edges) * (1.0 / 256.0)
    high, low = split(q.astype(F32) * scale)
    return dot(high, qq[...], NT) + dot(low, qq[...], NT)


def heads2_kernel(prev2, q2, r2, log2, heads, tails, live_groups, part, sums, grad, sums_out, hf, rf, qf, sf, qq):
    loss, live = head_bucket(2, prev2, q2, r2, log2, heads, tails, live_groups, grad, hf, rf, qf, sf, qq)
    sums_out[0:1, :] = sums[0:1, :] + loss
    sums_out[1:2, :] = sums[1:2, :] + live


def heads1_kernel(prev1, q1, r1, log1, heads, tails, live_groups, part, sums, grad, row, hf, rf, qf, sf, qq):
    loss, live = head_bucket(1, prev1, q1, r1, log1, heads, tails, live_groups, grad, hf, rf, qf, sf, qq)
    loss_all = jnp.sum(sums[0:1, :] + loss, axis=1, keepdims=True)
    live_all = jnp.sum(sums[1:2, :] + live, axis=1, keepdims=True)
    lane = lax.broadcasted_iota(jnp.int32, row.shape, 1)
    row[...] = jnp.where(lane == 0, loss_all, jnp.where(lane == 1, live_all, 0.0))


def choose_kernel(emb, prev2, passed):
    passed[...] = jnp.where(lax.axis_index("blk") & 1 == 0, emb[...], prev2[...])


def after_kernel(block, lists, emb, own_lists, row, block_out, lists_out, passed, passed_lists):
    even = lax.axis_index("blk") & 1 == 0
    passed[...] = jnp.where(even, block[...], emb[...])
    passed_lists[...] = jnp.where(even, lists[...], own_lists[...])


def tails2_kernel(rel, emb, next2, lists, part, grad, hot, hf, rf, qf, sf, qq, log):
    far_terms(2, rel, lists, rf, log, hot)
    grad[...] += tail_bucket(2, emb, next2, lists, rf, log, hf, qf, sf, qq)


def tails1_kernel(rel, emb, next1, lists, part, row, grad, hot, hf, rf, qf, sf, qq, log):
    far_terms(1, rel, lists, rf, log, hot)
    own = tail_bucket(1, emb, next1, lists, rf, log, hf, qf, sf, qq)
    grad[...] = (part[...] + own).astype(BF16)


def add_kernel(row, other, out):
    out[...] = row[...] + other[...]


def rows_kernel(own, row, other, own_out, rows):
    rows[...] = jnp.broadcast_to(row[0:1, :] + other[0:1, :], rows.shape)


def finish_kernel(own, other, rows, grad, mean):
    grad[...] = own[...].astype(F32) + other[...].astype(F32)
    total = jnp.sum(rows[...], axis=0, keepdims=True)
    mean[...] = total[:, 0:1] / total[:, 1:2]


def kernel(body, outs, scratch, flops, spaces, mib=48, aliases={}):
    return pl.pallas_call(
        body,
        out_shape=[jax.ShapeDtypeStruct(s, t) for s, t in outs],
        in_specs=[pl.BlockSpec(memory_space=m) for m in spaces],
        input_output_aliases=aliases,
        scratch_shapes=[pltpu.VMEM(*s) if isinstance(s, tuple) else s for s in scratch],
        compiler_params=pltpu.CompilerParams(vmem_limit_bytes=mib * 2**20),
        cost_estimate=pl.CostEstimate(flops=flops, bytes_accessed=4 * 2**20, transcendentals=0),
    )


def shifted(x, by):
    peers = lax.axis_size("blk")
    return lax.ppermute(x, "blk", [(i, (i + by) % peers) for i in range(peers)])


def exchanged(x):
    return lax.ppermute(x, "blk", [(i, i ^ 1) for i in range(lax.axis_size("blk"))])


def per_device(embeddings, relations, heads, tails, rels, negatives, live):
    edges = heads.shape[1]
    entities, width = embeddings.shape
    n_rel = relations.shape[0]
    blocks = lax.axis_size("blk")
    emb = embeddings.T
    rel = relations.T
    here = pltpu.VMEM
    big, grads, logs, rows_of = (width, edges), (width, entities), (entities, 256), (8, 128)
    work = [(big, F32), (big, F32), (big, F32), ((entities, edges), F32), ((entities, edges), BF16)]
    hot = ((n_rel, edges), BF16)
    raw = (heads, tails, rels, negatives, live.T)
    prev2 = shifted(emb, 2)
    next2 = shifted(emb, -2)
    sent = ((EXTRA, edges), BF16)
    (lists,) = kernel(
        pack_kernel, [sent],
        [(x.shape, x.dtype) for x in raw] + [((EXTRA, edges), F32), pltpu.SemaphoreType.DMA((len(raw),))],
        2 * 10**9, [pltpu.HBM] * len(raw), 56,
    )(*raw)
    next2_lists = shifted(lists, -2)
    part, sums, q1, q2, r1, r2, log1, log2 = kernel(
        prepare_kernel,
        [(grads, F32), ((8, edges), F32)] + [(big, BF16)] * 4 + [(logs, F32)] * 2,
        [hot] + work + [(logs, F32)], 20 * 10**9, [here] * 7)(emb, rel, *raw)
    own_lists = (heads, tails, live.T)
    (passed,) = kernel(choose_kernel, [(big, BF16)], [], 10**6, [here] * 2)(emb, prev2)
    prev1 = exchanged(passed)
    part, sums = kernel(heads2_kernel, [(grads, F32), ((8, edges), F32)], work, 8 * 10**9, [here] * 9, aliases={7: 0})(
        prev2, q2, r2, log2, *own_lists, part, sums)
    part, row = kernel(heads1_kernel, [(grads, F32), (rows_of, F32)], work, 3 * 10**9, [here] * 9, aliases={7: 0})(
        prev1, q1, r1, log1, *own_lists, part, sums)
    core_row = exchanged(row)
    next2, next2_lists, passed, passed_lists = kernel(
        after_kernel, [(big, BF16), sent] * 2, [], 10**6, [here] * 5, aliases={0: 0, 1: 1})(
        next2, next2_lists, emb, lists, row)
    next1 = exchanged(passed)
    lists1 = exchanged(passed_lists)
    (part,) = kernel(tails2_kernel, [(grads, F32)], [hot] + work + [(logs, F32)], 10 * 10**9, [here] * 5, aliases={4: 0})(
        rel, emb, next2, next2_lists, part)
    (row,) = kernel(add_kernel, [(rows_of, F32)], [], 10**6, [here] * 2)(row, core_row)
    rep_row = lax.ppermute(row, "rep", [(0, 1), (1, 0)])
    (own,) = kernel(
        tails1_kernel, [(grads, BF16)],
        [hot] + work + [(logs, F32)], 10 * 10**9, [here] * 6,
    )(rel, emb, next1, lists1, part, row)
    own, rows = kernel(rows_kernel, [(grads, BF16), ((blocks // 2, 128), F32)], [], 10**6, [here] * 3, aliases={0: 0})(
        own, row, rep_row)
    other = lax.ppermute(own, "rep", [(0, 1), (1, 0)])
    rows = lax.all_to_all(rows, "blk", 0, 0, tiled=True,
                          axis_index_groups=[[k + 2 * i for i in range(blocks // 2)] for k in (0, 1)])
    grad, mean = kernel(finish_kernel, [(grads, F32), ((1, 1), F32)], [], 10**6, [here] * 3)(own, other, rows)
    return grad.T, mean[0, 0]


def solution(mesh):
    placed = (
        P("blk", None),
        P(),
        P(None, ("blk", "rep")),
        P(None, ("blk", "rep")),
        P(None, ("blk", "rep")),
        P(None, ("blk", "rep"), None),
        P(None, ("blk", "rep")),
    )
    return jax.shard_map(
        per_device, mesh=mesh, in_specs=placed, out_specs=(P("blk", None), P()), check_vma=False
    )
```
